32 devices in a mesh: basin: 2 (over x), pair: 8 (over z, y), row: 2 (over core).
Axes of the slice: x: 2, y: 2, z: 4, core: 2. Of those that a mesh axis runs over, the one named last changes fastest.
Arguments:
- snapshots: float32 [8192, 4096], P(('basin', 'row'), 'pair'), parts along dimension 0, may hold values from -60 to 60, as said below
- plan: int32 [4, 16], replicated, may hold values from 0 to 15, as said below
Outputs:
- rotated: float32 [8192, 4096], P(('basin', 'row'), 'pair'), parts along dimension 0
The draws below stay inside these ranges and needn't reach their ends.
There are 2 independent parts, one for each index of `basin`. The reference program is written for one: setup_inputs(seed, part) draws one part's arguments, and reference() takes and returns one part's arrays. A program takes and returns all parts, laid end to end along the dimension named above; an argument that names none is the same for every part. Nothing has to cross between parts.
Inputs may be any that keep to these rules, and one draw needn't show every extreme that they name: `plan`: each row of the table is a permutation of the 16 slots. Slots 2d and 2d + 1 lie on the d-th index of pair; in every round each index sends one of its two blocks to index d + 1 and the other to index d - 1 (both modulo 8). `snapshots`: real values.
All inputs are finite; a program needn't handle non-finite values.
Results may differ from the reference program's by a relative error of at most 0.0003.
Values sent between devices are 32-bit elements; how exact they have to be, the bound alone decides.
No kernel may reach another device: no remote copies, remote signals or barrier semaphores. Data moves between devices by JAX's collectives and lax.ppermute only.
A program may use at most 64 MiB of HBM per device.

```python
import jax
import jax.numpy as jnp
from jax import lax

B = 256
ROUNDS = 4
NS_ITERS = 6
NP = 8
M = 4096
NCOL = 4096


def draw_snapshots(key, part):
    key_rows = jax.random.fold_in(key, 11)
    key_cols = jax.random.fold_in(key, 12)
    key_vals = jax.random.fold_in(key, 13)
    col_scale = jnp.exp(jax.random.uniform(key_cols, (1, NCOL), jnp.float32, jnp.log(0.3), jnp.log(3.0)))
    row_scale = jnp.exp(jax.random.uniform(key_rows, (M, 1), jnp.float32, jnp.log(0.3), jnp.log(3.0)))
    noise = jax.random.truncated_normal(key_vals, -6.0, 6.0, (M, NCOL), jnp.float32)
    values = noise * row_scale * col_scale
    return values.astype(jnp.float32)


def draw_plan(key, part):
    key_bits = jax.random.fold_in(key, 21)
    key_order = jax.random.fold_in(key, 22)
    bits = jax.random.randint(key_bits, (ROUNDS, NP), 0, 2)
    order = jax.random.randint(key_order, (ROUNDS, NP), 0, 2)
    device = jnp.arange(NP)[None, :]
    before = jnp.roll(bits, 1, axis=1)
    after = jnp.roll(bits, -1, axis=1)
    from_below = 2 * ((device + NP - 1) % NP) + before
    from_above = 2 * ((device + 1) % NP) + 1 - after
    slot_zero = jnp.where(order == 0, from_below, from_above)
    slot_one = jnp.where(order == 0, from_above, from_below)
    return jnp.stack((slot_zero, slot_one), axis=2).reshape(ROUNDS, 2 * NP).astype(jnp.int32)


def setup_inputs(seed: int = 0, part: int = 0) -> dict:
    splits = jax.random.split(jax.random.key(seed), 3)
    own_keys = jax.random.split(jax.random.fold_in(splits[2], part), 3)
    return {
        "snapshots": draw_snapshots(jax.random.fold_in(jax.random.fold_in(splits[2], part), 71), part),
        "plan": draw_plan(jax.random.fold_in(splits[2], 71), part),
    }


epsilon = 1e-6


def reference(snapshots, plan):
    highest = lax.Precision.HIGHEST
    identity = jnp.eye(B, dtype=jnp.float32)
    field = snapshots
    for round_index in range(ROUNDS):
        blocks = field.reshape(M, NP, 2, B)
        first = blocks[:, :, 0, :]
        second = blocks[:, :, 1, :]
        cross = jnp.einsum("mpa,mpb->pab", first, second, precision=highest)
        norm_first = jnp.sum(first * first, axis=0)
        norm_second = jnp.sum(second * second, axis=0)
        coupling = cross / (norm_first[:, :, None] + norm_second[:, None, :] + epsilon)
        system = identity[None] + jnp.einsum("pab,pcb->pac", coupling, coupling, precision=highest)
        scale = 1.0 + jnp.sum(coupling * coupling, axis=(1, 2))
        inverse = identity[None] / scale[:, None, None]
        for sweep in range(NS_ITERS):
            product = jnp.einsum("pab,pbc->pac", system, inverse, precision=highest)
            inverse = jnp.einsum("pab,pbc->pac", inverse, 2.0 * identity[None] - product, precision=highest)
        lifted = first - jnp.einsum("mpb,pab->mpa", second, coupling, precision=highest)
        mixed = jnp.einsum("mpa,pac->mpc", lifted, inverse, precision=highest)
        new_first = 2.0 * mixed - first
        new_second = second + 2.0 * jnp.einsum("mpa,pab->mpb", mixed, coupling, precision=highest)
        stacked = jnp.stack((new_first, new_second), axis=2).reshape(M, 2 * NP, B)
        field = stacked[:, plan[round_index], :].reshape(M, NCOL)
    return field
```

```python
import jax
import jax.numpy as jnp
from jax import lax
from jax.sharding import PartitionSpec as P

NS_ITERS = 6
EPSILON = 1e-06
PIECES = (256, 512, 512, 512, 256)


def shift(value, axis, by):
    size = lax.axis_size(axis)
    return lax.ppermute(value, axis, [(i, (i + by) % size) for i in range(size)])


def dot(left, right, left_dim=1, right_dim=0, precision=lax.Precision.HIGH):
    return lax.dot_general(
        left,
        right,
        (((left_dim,), (right_dim,)), ((), ())),
        precision=precision,
        preferred_element_type=jnp.float32,
    )


def piece_bounds(rows):
    unit = rows / sum(PIECES)
    bounds, start = [], 0
    for size in PIECES:
        bounds.append((start, start + int(size * unit)))
        start += int(size * unit)
    return bounds


def rotation(gram, norm_stay, norm_move, stay_first, send_is_stay):
    width = gram.shape[0]
    identity = jnp.eye(width, dtype=jnp.float32)
    cross = jnp.where(stay_first, gram, gram.T)
    norm_first = jnp.where(stay_first, norm_stay, norm_move)
    norm_second = jnp.where(stay_first, norm_move, norm_stay)
    coupling = cross / (norm_first[:, None] + norm_second[None, :] + EPSILON)
    highest = lax.Precision.HIGHEST
    system = identity + dot(coupling, coupling, 1, 1, highest)
    inverse = identity / (1.0 + jnp.sum(coupling * coupling))
    for sweep in range(NS_ITERS):
        inverse = dot(inverse, 2.0 * identity - dot(system, inverse, precision=highest), precision=highest)
    product = dot(inverse, coupling, precision=highest)
    first_first = 2.0 * inverse - identity
    first_second = 2.0 * product
    second_first = -2.0 * product.T
    second_second = identity - 2.0 * dot(coupling, product, 0, 0, highest)
    stay_stay = jnp.where(stay_first, first_first, second_second)
    move_move = jnp.where(stay_first, second_second, first_first)
    stay_move = jnp.where(stay_first, first_second, second_first)
    move_stay = jnp.where(stay_first, second_first, first_second)
    to_stay = jnp.concatenate((stay_stay, move_stay), axis=0)
    to_move = jnp.concatenate((stay_move, move_move), axis=0)
    sent = jnp.where(send_is_stay, to_stay, to_move)
    kept = jnp.where(send_is_stay, to_move, to_stay)
    return sent, kept


def per_device(snapshots, plan):
    rows = snapshots.shape[0]
    width = snapshots.shape[1] // 2
    rounds = plan.shape[0]
    bounds = piece_bounds(rows)
    device = lax.axis_index("pair")
    count = lax.axis_size("pair")
    stay = [snapshots[lo:hi, :width] for lo, hi in bounds]
    move = [snapshots[lo:hi, width:] for lo, hi in bounds]
    stay_first = jnp.bool_(True)
    for round_index in range(rounds):
        odd = round_index % 2
        position = (device + odd) % count
        upper = (position + 1) % count
        layout = plan[round_index]
        upper_zero = lax.dynamic_index_in_dim(layout, 2 * upper, 0, False)
        upper_one = lax.dynamic_index_in_dim(layout, 2 * upper + 1, 0, False)
        second_goes_up = (upper_zero == 2 * position + 1) | (upper_one == 2 * position + 1)
        send_is_second = second_goes_up if odd else ~second_goes_up
        send_is_stay = send_is_second != stay_first

        gram = jnp.zeros((width, width), jnp.float32)
        norm_stay = jnp.zeros((width,), jnp.float32)
        norm_move = jnp.zeros((width,), jnp.float32)
        for kept, came in zip(stay, move):
            gram = gram + dot(kept, came, 0, 0)
            norm_stay = norm_stay + jnp.sum(kept * kept, axis=0)
            norm_move = norm_move + jnp.sum(came * came, axis=0)
        packed = jnp.concatenate((gram, norm_stay[None], norm_move[None], jnp.zeros((6, width), jnp.float32)), axis=0)
        packed = packed + shift(packed, "row", 1)
        sent, kept = rotation(packed[:width], packed[width], packed[width + 1], stay_first, send_is_stay)

        direction = 2 if odd else -2
        arriving = []
        for one, two in zip(stay, move):
            outgoing = dot(one, sent[:width]) + dot(two, sent[width:])
            arriving.append(shift(outgoing, "pair", direction))
        stay = [dot(one, kept[:width]) + dot(two, kept[width:]) for one, two in zip(stay, move)]
        move = arriving
        target = device if odd else (device + 1) % count
        below = (target + count - 1) % count
        source_zero = lax.dynamic_index_in_dim(layout, 2 * target, 0, False)
        zero_from_below = source_zero // 2 == below
        stay_first = ~zero_from_below if odd else zero_from_below
    stay = jnp.concatenate(stay, axis=0)
    move = jnp.concatenate(move, axis=0)
    if rounds % 2:
        stay = shift(stay, "pair", 1)
        move = shift(move, "pair", 1)
        stay_first = shift(stay_first.astype(jnp.int32), "pair", 1) == 1
    return jnp.concatenate(
        (jnp.where(stay_first, stay, move), jnp.where(stay_first, move, stay)), axis=1
    )


def solution(mesh):
    in_specs = (P(("basin", "row"), "pair"), P())
    out_specs = P(("basin", "row"), "pair")
    return jax.shard_map(
        per_device, mesh=mesh, in_specs=in_specs, out_specs=out_specs, check_vma=False
    )
```

```python
import functools

import jax
import jax.numpy as jnp
from jax import lax
from jax.experimental import pallas as pl
from jax.experimental.pallas import tpu as pltpu
from jax.sharding import PartitionSpec as P

NS_ITERS = 6
EPSILON = 1e-06
BLOCK = 256
PIECES = (1, 3, 3, 1)
PARAMS = pltpu.CompilerParams(vmem_limit_bytes=32 * 1024 * 1024)


def shift(value, axis, by):
    size = lax.axis_size(axis)
    return lax.ppermute(value, axis, [(i, (i + by) % size) for i in range(size)])


def split(value):
    high = value.astype(jnp.bfloat16)
    return high, (value - high.astype(jnp.float32)).astype(jnp.bfloat16)


def dot(left, right):
    return jnp.dot(left, right, preferred_element_type=jnp.float32)


def dot3(left, right):
    (left_high, left_low), (right_high, right_low) = left, right
    return dot(left_high, right_high) + dot(left_low, right_high) + dot(left_high, right_low)


def whole(shape):
    return pl.BlockSpec(shape, lambda *_: (0,) * len(shape))


SMEM = pl.BlockSpec(memory_space=pltpu.SMEM)


def cost(flops, size):
    return pl.CostEstimate(flops=flops, bytes_accessed=size, transcendentals=0)


def eye(size):
    row = lax.broadcasted_iota(jnp.int32, (size, size), 0)
    column = lax.broadcasted_iota(jnp.int32, (size, size), 1)
    return jnp.where(row == column, 1.0, 0.0).astype(jnp.float32)


def first_gram_kernel(one, two, total, norm):
    @pl.when(pl.program_id(0) == 0)
    def _():
        total[...] = jnp.zeros_like(total)
        norm[...] = jnp.zeros_like(norm)

    width = one.shape[1]
    turned = one[...].T
    came = two[...]
    total[:width, :] += dot3(split(turned), split(came))
    total[width:, :] += jnp.sum((came * came).reshape(-1, 8, width), axis=0)
    norm[...] += jnp.broadcast_to(jnp.sum(turned * turned, axis=1, keepdims=True), norm.shape)


def first_gram(snapshots, width):
    rows = snapshots.shape[0]
    return pl.pallas_call(
        first_gram_kernel,
        grid=(rows // BLOCK,),
        in_specs=[pl.BlockSpec((BLOCK, width), lambda i: (i, 0)), pl.BlockSpec((BLOCK, width), lambda i: (i, 1))],
        out_specs=[whole((width + 8, width)), whole((width, 128))],
        out_shape=[
            jax.ShapeDtypeStruct((width + 8, width), jnp.float32),
            jax.ShapeDtypeStruct((width, 128), jnp.float32),
        ],
        compiler_params=PARAMS,
        name="first_gram",
    )(snapshots, snapshots)


def gram_kernel(turned, came, before, total):
    width = came.shape[1]
    value = came[...]
    gram = dot3(split(turned[...]), split(value))
    norm = jnp.sum((value * value).reshape(-1, 8, width), axis=0)
    if before is None:
        total[:width, :] = gram
        total[width:, :] = norm
    else:
        total[:width, :] = before[:width, :] + gram
        total[width:, :] = before[width:, :] + norm


def gram(turned, came, before):
    rows, width = came.shape
    body = gram_kernel if before is not None else lambda a, b, c: gram_kernel(a, b, None, c)
    args = (turned, came) if before is None else (turned, came, before)
    return pl.pallas_call(
        body,
        out_shape=jax.ShapeDtypeStruct((width + 8, width), jnp.float32),
        compiler_params=PARAMS,
        cost_estimate=cost(6 * rows * width * width, 4 * (2 * rows * width + 2 * width * width)),
        name="gram",
    )(*args)


def rotation_kernel(flags, mine, other, norm, stay, move, high, low, sent):
    width = stay.shape[1]
    total = mine[...] + other[...]
    norm_move = jnp.sum(total[width:, :], axis=0, keepdims=True)
    coupled = total[:width, :] / (norm[:, :1] + norm_move + EPSILON)
    turned = coupled.T
    stay_first = flags[0] == 1
    send_is_stay = flags[1] == 1
    coupling = jnp.where(stay_first, coupled, turned)
    coupling_turned = jnp.where(stay_first, turned, coupled)
    identity = eye(width)
    scale = 1.0 / (1.0 + jnp.sum(coupled * coupled))
    left, right = split(coupling_turned), split(coupling)
    base = scale * (identity + dot3(right, left))
    inverse = scale * (2.0 * identity - base)
    base_split = split(base)
    base = 2.0 * base - dot3(base_split, base_split)
    for sweep in range(1, NS_ITERS):
        base_split = split(base)
        inverse = 2.0 * inverse - dot3(split(inverse), base_split)
        if sweep < NS_ITERS - 1:
            base = 2.0 * base - dot3(base_split, base_split)
    product_turned = dot3(left, split(inverse))
    second_second = identity - 2.0 * dot3(split(product_turned), right)
    first_first = 2.0 * inverse - identity
    first_second = 2.0 * product_turned.T
    second_first = -2.0 * product_turned
    stay_stay = jnp.where(stay_first, first_first, second_second)
    move_move = jnp.where(stay_first, second_second, first_first)
    stay_move = jnp.where(stay_first, first_second, second_first)
    move_stay = jnp.where(stay_first, second_first, first_second)
    top_sent, top_sent_low = split(jnp.where(send_is_stay, stay_stay, stay_move))
    end_sent, end_sent_low = split(jnp.where(send_is_stay, move_stay, move_move))
    sent[...] = dot3(split(stay[...]), (top_sent, top_sent_low)) + dot3(split(move[...]), (end_sent, end_sent_low))
    top_kept, top_kept_low = split(jnp.where(send_is_stay, stay_move, stay_stay))
    end_kept, end_kept_low = split(jnp.where(send_is_stay, move_move, move_stay))
    high[:width, :width] = top_sent
    high[width:, :width] = end_sent
    high[:width, width:] = top_kept
    high[width:, width:] = end_kept
    low[:width, :width] = top_sent_low
    low[width:, :width] = end_sent_low
    low[:width, width:] = top_kept_low
    low[width:, width:] = end_kept_low


def view(source, block, grid_of_one):
    array, row, column = source
    if grid_of_one:
        return pl.BlockSpec(block, lambda *_: (row, column))
    return pl.BlockSpec(block, lambda i, *_: (row + i, column))


def rotation(flags, mine, other, norm, stay, move, blocks):
    width = mine.shape[1]
    size = (blocks * BLOCK, width)
    return pl.pallas_call(
        rotation_kernel,
        grid=(1,),
        in_specs=[SMEM, whole(mine.shape), whole(other.shape), whole(norm.shape), view(stay, size, True), view(move, size, True)],
        out_specs=[whole((2 * width, 2 * width)), whole((2 * width, 2 * width)), whole(size)],
        out_shape=[
            jax.ShapeDtypeStruct((2 * width, 2 * width), jnp.bfloat16),
            jax.ShapeDtypeStruct((2 * width, 2 * width), jnp.bfloat16),
            jax.ShapeDtypeStruct(size, jnp.float32),
        ],
        compiler_params=PARAMS,
        name="rotation",
    )(flags, mine, other, norm, stay[0], move[0])


def apply_kernel(first, with_sent, stay, move, high, low, *refs):
    if not first:
        before, *refs = refs
    if with_sent:
        sent, *refs = refs
    kept, turned, norm = refs
    width = stay.shape[1]
    lead = 0 if with_sent else width
    joined = jnp.concatenate((stay[...], move[...]), axis=1)
    result = dot3(split(joined), (high[:, lead:], low[:, lead:]))
    if with_sent:
        sent[...] = result[:, :width]
        result = result[:, width:]
    kept[...] = result
    result = result.T
    turned[...] = result
    squares = jnp.broadcast_to(jnp.sum(result * result, axis=1, keepdims=True), norm.shape)
    step = pl.program_id(0)

    @pl.when(step == 0)
    def _():
        norm[...] = squares if first else before[...] + squares

    @pl.when(step > 0)
    def _():
        norm[...] += squares


def apply(stay, move, high, low, before, blocks, with_sent):
    width = high.shape[0] // 2
    rows = blocks * BLOCK
    block = (BLOCK, width)
    by_row = pl.BlockSpec(block, lambda i: (i, 0))
    by_column = pl.BlockSpec((width, BLOCK), lambda i: (0, i))
    norm = whole((width, 128))
    piece = jax.ShapeDtypeStruct((rows, width), jnp.float32)
    first = before is None
    return pl.pallas_call(
        functools.partial(apply_kernel, first, with_sent),
        grid=(blocks,),
        in_specs=[view(stay, block, False), view(move, block, False), whole(high.shape), whole(low.shape)]
        + [norm] * (not first),
        out_specs=[by_row] * with_sent + [by_row, by_column, norm],
        out_shape=[piece] * with_sent
        + [piece, jax.ShapeDtypeStruct((width, rows), jnp.float32), jax.ShapeDtypeStruct((width, 128), jnp.float32)],
        compiler_params=PARAMS,
        cost_estimate=cost(24 * rows * width * width, 20 * rows * width),
        name="apply",
    )(stay[0], move[0], high, low, *([] if first else [before]))


def last_apply_kernel(first, with_sent, place, stay, move, high, low, *refs):
    if not first:
        before, *refs = refs
    width = stay.shape[1]
    lead = 0 if with_sent else width
    joined = jnp.concatenate((stay[...], move[...]), axis=1)
    result = dot3(split(joined), (high[:, lead:], low[:, lead:]))
    if with_sent:
        refs[0][...] = result[:, :width]
        result = result[:, width:]
    refs[-1][...] = result


def last_apply(place, stay, move, high, low, before, start, blocks, shape, with_sent):
    width = high.shape[0] // 2
    block = (BLOCK, width)
    first = before is None
    out = pl.BlockSpec(block, lambda i, place: (start + i, place[0]))
    by_row = pl.BlockSpec(block, lambda i, place: (i, 0))
    rows = blocks * BLOCK
    return pl.pallas_call(
        functools.partial(last_apply_kernel, first, with_sent),
        grid_spec=pltpu.PrefetchScalarGridSpec(
            num_scalar_prefetch=1,
            grid=(blocks,),
            in_specs=[view(stay, block, False), view(move, block, False), whole(high.shape), whole(low.shape)]
            + [pl.BlockSpec(memory_space=pl.ANY)] * (not first),
            out_specs=[by_row] * with_sent + [out],
        ),
        out_shape=[jax.ShapeDtypeStruct((rows, width), jnp.float32)] * with_sent
        + [jax.ShapeDtypeStruct(shape, jnp.float32)],
        input_output_aliases={} if first else {5: 1 if with_sent else 0},
        compiler_params=PARAMS,
        cost_estimate=cost(24 * rows * width * width, 20 * rows * width),
        name="last_apply",
    )(place, stay[0], move[0], high, low, *([] if first else [before]))


def place_kernel(place, came, before, out):
    out[...] = came[...]


def put(place, came, before, start):
    rows, width = came.shape
    block = (BLOCK, width)
    return pl.pallas_call(
        place_kernel,
        grid_spec=pltpu.PrefetchScalarGridSpec(
            num_scalar_prefetch=1,
            grid=(rows // BLOCK,),
            in_specs=[pl.BlockSpec(block, lambda i, place: (i, 0)), pl.BlockSpec(memory_space=pl.ANY)],
            out_specs=pl.BlockSpec(block, lambda i, place: (start + i, place[0])),
        ),
        out_shape=jax.ShapeDtypeStruct(before.shape, jnp.float32),
        input_output_aliases={2: 0},
        compiler_params=PARAMS,
        cost_estimate=cost(0, 8 * rows * width),
        name="put",
    )(place, came, before)


def per_device(snapshots, plan):
    rows = snapshots.shape[0]
    width = snapshots.shape[1] // 2
    rounds = plan.shape[0]
    blocks = rows // BLOCK
    sizes = [share * blocks // sum(PIECES) for share in PIECES]
    starts = [sum(sizes[:i]) for i in range(len(sizes))]
    device = lax.axis_index("pair")
    count = lax.axis_size("pair")
    stay = [(snapshots, start, 0) for start in starts]
    move = [(snapshots, start, 1) for start in starts]
    stay_first = jnp.bool_(True)
    for round_index in range(rounds):
        last = round_index == rounds - 1
        odd = round_index % 2
        position = (device + odd) % count
        upper = (position + 1) % count
        layout = plan[round_index]
        upper_zero = lax.dynamic_index_in_dim(layout, 2 * upper, 0, False)
        upper_one = lax.dynamic_index_in_dim(layout, 2 * upper + 1, 0, False)
        second_goes_up = (upper_zero == 2 * position + 1) | (upper_one == 2 * position + 1)
        send_is_second = second_goes_up if odd else ~second_goes_up
        send_is_stay = send_is_second != stay_first
        flags = jnp.stack((stay_first, send_is_stay)).astype(jnp.int32)
        target = device if odd else (device + 1) % count
        below = (target + count - 1) % count
        source_zero = lax.dynamic_index_in_dim(layout, 2 * target, 0, False)
        zero_from_below = source_zero // 2 == below
        stay_first = ~zero_from_below if odd else zero_from_below

        if round_index == 0:
            total, norm = first_gram(snapshots, width)
            norm = norm + shift(norm, "row", 1)
        else:
            total = None
            for one, two in zip(turned, move):
                total = gram(one, two[0], total)
        other = shift(total, "row", 1)
        high, low, outgoing = rotation(flags, total, other, norm, stay[0], move[0], sizes[0])

        direction = 2 if odd else -2
        arriving = [shift(outgoing, "pair", direction)]
        if last and rounds % 2 == 0:
            stay_column = jnp.where(stay_first, 0, 1).astype(jnp.int32)[None]
            field = None
            for piece in range(1, len(sizes)):
                outgoing, field = last_apply(
                    stay_column, stay[piece], move[piece], high, low, field, starts[piece], sizes[piece], snapshots.shape, True
                )
                arriving.append(shift(outgoing, "pair", direction))
            (field,) = last_apply(
                stay_column, stay[0], move[0], high, low, field, starts[0], sizes[0], snapshots.shape, False
            )
            for piece, start in zip(arriving, starts):
                field = put(1 - stay_column, piece, field, start)
            return field
        norm = None
        held = [None] * len(sizes)
        for piece in range(1, len(sizes)):
            outgoing, *held[piece], norm = apply(stay[piece], move[piece], high, low, norm, sizes[piece], True)
            arriving.append(shift(outgoing, "pair", direction))
        *held[0], norm = apply(stay[0], move[0], high, low, norm, sizes[0], False)
        stay = [(kept, 0, 0) for kept, _ in held]
        turned = [value for _, value in held]
        move = [(value, 0, 0) for value in arriving]
        norm = norm + shift(norm, "row", 1)
    stay = shift(jnp.concatenate([value for value, _, _ in stay], axis=0), "pair", 1)
    move = shift(jnp.concatenate([value for value, _, _ in move], axis=0), "pair", 1)
    stay_first = shift(stay_first.astype(jnp.int32), "pair", 1) == 1
    return jnp.concatenate(
        (jnp.where(stay_first, stay, move), jnp.where(stay_first, move, stay)), axis=1
    )


def solution(mesh):
    in_specs = (P(("basin", "row"), "pair"), P())
    out_specs = P(("basin", "row"), "pair")
    return jax.shard_map(
        per_device, mesh=mesh, in_specs=in_specs, out_specs=out_specs, check_vma=False
    )
```

```python
import functools

import jax
import jax.numpy as jnp
from jax import lax
from jax.experimental import pallas as pl
from jax.experimental.pallas import tpu as pltpu
from jax.sharding import PartitionSpec as P

NS_ITERS = 6
EPSILON = 1e-06
BLOCK = 256
PIECES = (2, 2, 2, 2)
PARAMS = pltpu.CompilerParams(vmem_limit_bytes=12 * 1024 * 1024)


def shift(value, axis, by):
    size = lax.axis_size(axis)
    return lax.ppermute(value, axis, [(i, (i + by) % size) for i in range(size)])


def split(value):
    high = value.astype(jnp.bfloat16)
    return high, (value - high.astype(jnp.float32)).astype(jnp.bfloat16)


def dot(left, right):
    return jnp.dot(left, right, preferred_element_type=jnp.float32)


def dot3(left, right):
    (left_high, left_low), (right_high, right_low) = left, right
    return dot(left_high, right_high) + dot(left_low, right_high) + dot(left_high, right_low)


def whole(shape):
    return pl.BlockSpec(shape, lambda *_: (0,) * len(shape))


SMEM = pl.BlockSpec(memory_space=pltpu.SMEM)


COST = pl.CostEstimate(flops=1024, bytes_accessed=1024, transcendentals=0)


def eye(size):
    row = lax.broadcasted_iota(jnp.int32, (size, size), 0)
    column = lax.broadcasted_iota(jnp.int32, (size, size), 1)
    return jnp.where(row == column, 1.0, 0.0).astype(jnp.float32)


def flags_kernel(count, plan, device, flags):
    rounds = plan.shape[0]
    stay_first = jnp.int32(1)
    for step in range(rounds):
        odd = step % 2
        position = lax.rem(device[0] + odd, count)
        upper = lax.rem(position + 1, count)
        second = 2 * position + 1
        second_up = jnp.where((plan[step, 2 * upper] == second) | (plan[step, 2 * upper + 1] == second), 1, 0)
        send_second = second_up if odd else 1 - second_up
        flags[step, 0] = stay_first
        flags[step, 1] = jnp.where(send_second == stay_first, 0, 1)
        target = device[0] if odd else upper
        below = lax.rem(target + count - 1, count)
        from_below = jnp.where(plan[step, 2 * target] // 2 == below, 1, 0)
        stay_first = 1 - from_below if odd else from_below
    flags[rounds, 0] = 1 - stay_first
    flags[rounds, 1] = stay_first


def make_flags(plan, device, count):
    return pl.pallas_call(
        functools.partial(flags_kernel, count),
        in_specs=[SMEM, SMEM],
        out_specs=SMEM,
        out_shape=jax.ShapeDtypeStruct((plan.shape[0] + 1, 2), jnp.int32),
        compiler_params=PARAMS,
        cost_estimate=COST,
        name="flags",
    )(plan, device)


def first_gram_kernel(snapshots, total, norm, stay, move):
    rows, width = stay.shape
    total[...] = jnp.zeros_like(total)
    norm[...] = jnp.zeros_like(norm)

    def body(one, two, stay_part, move_part):
        kept, came = one[...], two[...]
        stay_part[...] = kept
        move_part[...] = came
        turned = kept.T
        total[:width, :] += dot3(split(turned), split(came))
        total[width:, :] += jnp.sum((came * came).reshape(-1, 8, width), axis=0)
        norm[...] += jnp.broadcast_to(jnp.sum(turned * turned, axis=1, keepdims=True), norm.shape)

    block = (BLOCK, width)
    by_row = pl.BlockSpec(block, lambda i: (i, 0))
    pltpu.emit_pipeline(
        body,
        grid=(rows // BLOCK,),
        in_specs=[by_row, pl.BlockSpec(block, lambda i: (i, 1))],
        out_specs=[by_row, by_row],
    )(snapshots, snapshots, stay, move)


def first_gram(snapshots, width):
    rows = snapshots.shape[0]
    vmem = pl.BlockSpec(memory_space=pltpu.VMEM)
    anywhere = pl.BlockSpec(memory_space=pl.ANY)
    return pl.pallas_call(
        first_gram_kernel,
        in_specs=[pl.BlockSpec(memory_space=pltpu.HBM)],
        out_specs=[vmem, vmem, anywhere, anywhere],
        out_shape=[
            jax.ShapeDtypeStruct((width + 8, width), jnp.float32),
            jax.ShapeDtypeStruct((width, 128), jnp.float32),
            jax.ShapeDtypeStruct((rows, width), jnp.float32),
            jax.ShapeDtypeStruct((rows, width), jnp.float32),
        ],
        compiler_params=PARAMS,
        cost_estimate=COST,
        name="first_gram",
    )(snapshots)


def gram_kernel(turned, came, before, total):
    width = came.shape[1]
    value = came[...]
    gram = dot3(split(turned[...]), split(value))
    norm = jnp.sum((value * value).reshape(-1, 8, width), axis=0)
    if before is None:
        total[:width, :] = gram
        total[width:, :] = norm
    else:
        total[:width, :] = before[:width, :] + gram
        total[width:, :] = before[width:, :] + norm


def gram(turned, came, before):
    rows, width = came.shape
    body = gram_kernel if before is not None else lambda a, b, c: gram_kernel(a, b, None, c)
    args = (turned, came) if before is None else (turned, came, before)
    return pl.pallas_call(
        body,
        out_shape=jax.ShapeDtypeStruct((width + 8, width), jnp.float32),
        compiler_params=PARAMS,
        cost_estimate=COST,
        name="gram",
    )(*args)


def rotation_kernel(step, flags, mine, other, norm, stay, move, high, low, sent):
    width = stay.shape[1]
    total = mine[...] + other[...]
    norm_move = jnp.sum(total[width:, :], axis=0, keepdims=True)
    coupled = total[:width, :] / (norm[:, :1] + norm_move + EPSILON)
    turned = coupled.T
    stay_first = flags[step, 0] == 1
    send_is_stay = flags[step, 1] == 1
    coupling = jnp.where(stay_first, coupled, turned)
    coupling_turned = jnp.where(stay_first, turned, coupled)
    identity = eye(width)
    scale = 1.0 / (1.0 + jnp.sum(coupled * coupled))
    left, right = split(coupling_turned), split(coupling)
    base = scale * (identity + dot3(right, left))
    inverse = scale * (2.0 * identity - base)
    base_split = split(base)
    base = 2.0 * base - dot3(base_split, base_split)
    for sweep in range(1, NS_ITERS):
        base_split = split(base)
        inverse = 2.0 * inverse - dot3(split(inverse), base_split)
        if sweep < NS_ITERS - 1:
            base = 2.0 * base - dot3(base_split, base_split)
    product_turned = dot3(left, split(inverse))
    second_second = identity - 2.0 * dot3(split(product_turned), right)
    first_first = 2.0 * inverse - identity
    first_second = 2.0 * product_turned.T
    second_first = -2.0 * product_turned
    stay_stay = jnp.where(stay_first, first_first, second_second)
    move_move = jnp.where(stay_first, second_second, first_first)
    stay_move = jnp.where(stay_first, first_second, second_first)
    move_stay = jnp.where(stay_first, second_first, first_second)
    top_sent, top_sent_low = split(jnp.where(send_is_stay, stay_stay, stay_move))
    end_sent, end_sent_low = split(jnp.where(send_is_stay, move_stay, move_move))
    sent[...] = dot3(split(stay[...]), (top_sent, top_sent_low)) + dot3(split(move[...]), (end_sent, end_sent_low))
    top_kept, top_kept_low = split(jnp.where(send_is_stay, stay_move, stay_stay))
    end_kept, end_kept_low = split(jnp.where(send_is_stay, move_move, move_stay))
    high[:width, :width] = top_sent
    high[width:, :width] = end_sent
    high[:width, width:] = top_kept
    high[width:, width:] = end_kept
    low[:width, :width] = top_sent_low
    low[width:, :width] = end_sent_low
    low[:width, width:] = top_kept_low
    low[width:, width:] = end_kept_low


def view(source, block, grid_of_one):
    array, row, column = source
    if grid_of_one:
        return pl.BlockSpec(block, lambda *_: (row * BLOCK // block[0], column))
    return pl.BlockSpec(block, lambda i, *_: (row + i, column))


def rotation(step, flags, mine, other, norm, stay, move, blocks):
    width = mine.shape[1]
    size = (blocks * BLOCK, width)
    return pl.pallas_call(
        functools.partial(rotation_kernel, step),
        grid=(1,),
        in_specs=[SMEM, whole(mine.shape), whole(other.shape), whole(norm.shape), view(stay, size, True), view(move, size, True)],
        out_specs=[whole((2 * width, 2 * width)), whole((2 * width, 2 * width)), whole(size)],
        out_shape=[
            jax.ShapeDtypeStruct((2 * width, 2 * width), jnp.bfloat16),
            jax.ShapeDtypeStruct((2 * width, 2 * width), jnp.bfloat16),
            jax.ShapeDtypeStruct(size, jnp.float32),
        ],
        compiler_params=PARAMS,
        cost_estimate=COST,
        name="rotation",
    )(flags, mine, other, norm, stay[0], move[0])


def apply_kernel(first, with_sent, stay, move, high, low, *refs):
    if not first:
        before, *refs = refs
    if with_sent:
        sent, *refs = refs
    kept, turned, norm = refs
    width = stay.shape[1]
    lead = 0 if with_sent else width
    joined = jnp.concatenate((stay[...], move[...]), axis=1)
    result = dot3(split(joined), (high[:, lead:], low[:, lead:]))
    if with_sent:
        sent[...] = result[:, :width]
        result = result[:, width:]
    kept[...] = result
    result = result.T
    turned[...] = result
    squares = jnp.broadcast_to(jnp.sum(result * result, axis=1, keepdims=True), norm.shape)
    step = pl.program_id(0)

    @pl.when(step == 0)
    def _():
        norm[...] = squares if first else before[...] + squares

    @pl.when(step > 0)
    def _():
        norm[...] += squares


def apply(stay, move, high, low, before, blocks, with_sent):
    width = high.shape[0] // 2
    rows = blocks * BLOCK
    block = (BLOCK, width)
    by_row = pl.BlockSpec(block, lambda i: (i, 0))
    by_column = pl.BlockSpec((width, BLOCK), lambda i: (0, i))
    norm = whole((width, 128))
    piece = jax.ShapeDtypeStruct((rows, width), jnp.float32)
    first = before is None
    return pl.pallas_call(
        functools.partial(apply_kernel, first, with_sent),
        grid=(blocks,),
        in_specs=[view(stay, block, False), view(move, block, False), whole(high.shape), whole(low.shape)]
        + [norm] * (not first),
        out_specs=[by_row] * with_sent + [by_row, by_column, norm],
        out_shape=[piece] * with_sent
        + [piece, jax.ShapeDtypeStruct((width, rows), jnp.float32), jax.ShapeDtypeStruct((width, 128), jnp.float32)],
        compiler_params=PARAMS,
        cost_estimate=COST,
        name="apply",
    )(stay[0], move[0], high, low, *([] if first else [before]))


def last_apply_kernel(first, with_sent, place, stay, move, high, low, *refs):
    if not first:
        before, *refs = refs
    width = stay.shape[1]
    lead = 0 if with_sent else width
    joined = jnp.concatenate((stay[...], move[...]), axis=1)
    result = dot3(split(joined), (high[:, lead:], low[:, lead:]))
    if with_sent:
        refs[0][...] = result[:, :width]
        result = result[:, width:]
    refs[-1][...] = result


def last_apply(place, stay, move, high, low, before, start, blocks, shape, with_sent):
    width = high.shape[0] // 2
    block = (BLOCK, width)
    first = before is None
    out = pl.BlockSpec(block, lambda i, place: (start + i, place[place.shape[0] - 1, 0]))
    by_row = pl.BlockSpec(block, lambda i, place: (i, 0))
    rows = blocks * BLOCK
    return pl.pallas_call(
        functools.partial(last_apply_kernel, first, with_sent),
        grid_spec=pltpu.PrefetchScalarGridSpec(
            num_scalar_prefetch=1,
            grid=(blocks,),
            in_specs=[view(stay, block, False), view(move, block, False), whole(high.shape), whole(low.shape)]
            + [pl.BlockSpec(memory_space=pl.ANY)] * (not first),
            out_specs=[by_row] * with_sent + [out],
        ),
        out_shape=[jax.ShapeDtypeStruct((rows, width), jnp.float32)] * with_sent
        + [jax.ShapeDtypeStruct(shape, jnp.float32)],
        input_output_aliases={} if first else {5: 1 if with_sent else 0},
        compiler_params=PARAMS,
        cost_estimate=COST,
        name="last_apply",
    )(place, stay[0], move[0], high, low, *([] if first else [before]))


def place_kernel(place, came, before, out):
    out[...] = came[...]


def put(place, came, before, start):
    rows, width = came.shape
    block = (BLOCK, width)
    return pl.pallas_call(
        place_kernel,
        grid_spec=pltpu.PrefetchScalarGridSpec(
            num_scalar_prefetch=1,
            grid=(rows // BLOCK,),
            in_specs=[pl.BlockSpec(block, lambda i, place: (i, 0)), pl.BlockSpec(memory_space=pl.ANY)],
            out_specs=pl.BlockSpec(block, lambda i, place: (start + i, place[place.shape[0] - 1, 1])),
        ),
        out_shape=jax.ShapeDtypeStruct(before.shape, jnp.float32),
        input_output_aliases={2: 0},
        compiler_params=PARAMS,
        cost_estimate=COST,
        name="put",
    )(place, came, before)


def per_device(snapshots, plan):
    rows = snapshots.shape[0]
    width = snapshots.shape[1] // 2
    rounds = plan.shape[0]
    blocks = rows // BLOCK
    sizes = [share * blocks // sum(PIECES) for share in PIECES]
    starts = [sum(sizes[:i]) for i in range(len(sizes))]
    device = lax.axis_index("pair")
    count = lax.axis_size("pair")
    total, norm, stay, move = first_gram(snapshots, width)
    stay = [(stay, start, 0) for start in starts]
    move = [(move, start, 0) for start in starts]
    flags = make_flags(plan, device[None], count)
    for round_index in range(rounds):
        last = round_index == rounds - 1
        odd = round_index % 2
        if round_index == 0:
            norm = norm + shift(norm, "row", 1)
        else:
            total = None
            for one, two in zip(turned, move):
                total = gram(one, two[0], total)
        other = shift(total, "row", 1)
        high, low, outgoing = rotation(round_index, flags, total, other, norm, stay[0], move[0], sizes[0])

        direction = 2 if odd else -2
        arriving = [shift(outgoing, "pair", direction)]
        if last and rounds % 2 == 0:
            field = None
            for piece in range(1, len(sizes)):
                outgoing, field = last_apply(
                    flags, stay[piece], move[piece], high, low, field, starts[piece], sizes[piece], snapshots.shape, True
                )
                arriving.append(shift(outgoing, "pair", direction))
            (field,) = last_apply(
                flags, stay[0], move[0], high, low, field, starts[0], sizes[0], snapshots.shape, False
            )
            for piece, start in zip(arriving, starts):
                field = put(flags, piece, field, start)
            return field
        norm = None
        held = [None] * len(sizes)
        for piece in range(1, len(sizes)):
            outgoing, *held[piece], norm = apply(stay[piece], move[piece], high, low, norm, sizes[piece], True)
            arriving.append(shift(outgoing, "pair", direction))
        *held[0], norm = apply(stay[0], move[0], high, low, norm, sizes[0], False)
        stay = [(kept, 0, 0) for kept, _ in held]
        turned = [value for _, value in held]
        move = [(value, 0, 0) for value in arriving]
        norm = norm + shift(norm, "row", 1)
    stay = shift(jnp.concatenate([value for value, _, _ in stay], axis=0), "pair", 1)
    move = shift(jnp.concatenate([value for value, _, _ in move], axis=0), "pair", 1)
    stay_first = shift(flags[rounds, 1], "pair", 1) == 1
    return jnp.concatenate(
        (jnp.where(stay_first, stay, move), jnp.where(stay_first, move, stay)), axis=1
    )


def solution(mesh):
    in_specs = (P(("basin", "row"), "pair"), P())
    out_specs = P(("basin", "row"), "pair")
    return jax.shard_map(
        per_device, mesh=mesh, in_specs=in_specs, out_specs=out_specs, check_vma=False
    )
```

```python
import functools

import jax
import jax.numpy as jnp
from jax import lax
from jax.experimental import pallas as pl
from jax.experimental.pallas import tpu as pltpu
from jax.sharding import PartitionSpec as P

NS_ITERS = 6
EPSILON = 1e-06
BLOCK = 256
PIECES = 4
SIDE = 128
PARAMS = pltpu.CompilerParams(vmem_limit_bytes=12 * 1024 * 1024)


def shift(value, axis, by):
    size = lax.axis_size(axis)
    return lax.ppermute(value, axis, [(i, (i + by) % size) for i in range(size)])


def split(value):
    high = value.astype(jnp.bfloat16)
    return high, (value - high.astype(jnp.float32)).astype(jnp.bfloat16)


def dot(left, right):
    return jnp.dot(left, right, preferred_element_type=jnp.float32)


def dot3(left, right):
    (left_high, left_low), (right_high, right_low) = left, right
    return dot(left_high, right_high) + dot(left_low, right_high) + dot(left_high, right_low)


def whole(shape):
    return pl.BlockSpec(shape, lambda *_: (0,) * len(shape))


SMEM = pl.BlockSpec(memory_space=pltpu.SMEM)


COST = pl.CostEstimate(flops=1024, bytes_accessed=1024, transcendentals=0)


def eye(size):
    row = lax.broadcasted_iota(jnp.int32, (size, size), 0)
    column = lax.broadcasted_iota(jnp.int32, (size, size), 1)
    return jnp.where(row == column, 1.0, 0.0).astype(jnp.float32)


def route(count, plan, device):
    stay_first = jnp.int32(1)
    flags = []
    for step in range(plan.shape[0]):
        odd = step % 2
        position = lax.rem(device + odd, count)
        upper = lax.rem(position + 1, count)
        second = 2 * position + 1
        second_up = jnp.where((plan[step, 2 * upper] == second) | (plan[step, 2 * upper + 1] == second), 1, 0)
        send_second = second_up if odd else 1 - second_up
        flags.append((stay_first, jnp.where(send_second == stay_first, 0, 1)))
        target = device if odd else upper
        below = lax.rem(target + count - 1, count)
        from_below = jnp.where(plan[step, 2 * target] // 2 == below, 1, 0)
        stay_first = 1 - from_below if odd else from_below
    return flags, stay_first


def flags_kernel(count, plan, device, flags):
    rounds = plan.shape[0]
    own, stay_first = route(count, plan, device[0])
    above, _ = route(count, plan, lax.rem(device[0] + 2, count))
    below, _ = route(count, plan, lax.rem(device[0] + count - 2 % count, count))
    for step in range(rounds):
        flags[step, 0], flags[step, 1] = own[step]
        sender = below[step] if step % 2 else above[step]
        flags[rounds + step, 0] = 1 - sender[0]
        flags[rounds + step, 1] = 1 - sender[1]
    flags[2 * rounds, 0] = 1 - stay_first
    flags[2 * rounds, 1] = stay_first


def make_flags(plan, device, count):
    return pl.pallas_call(
        functools.partial(flags_kernel, count),
        in_specs=[SMEM, SMEM],
        out_specs=SMEM,
        out_shape=jax.ShapeDtypeStruct((2 * plan.shape[0] + 1, 2), jnp.int32),
        compiler_params=PARAMS,
        cost_estimate=COST,
        name="flags",
    )(plan, device)


def first_gram_kernel(snapshots, total, norm, stay, move):
    rows, width = stay.shape
    total[...] = jnp.zeros_like(total)
    norm[...] = jnp.zeros_like(norm)

    def body(one, two, stay_part, move_part):
        kept, came = one[...], two[...]
        stay_part[...] = kept
        move_part[...] = came
        turned = kept.T
        total[:width, :] += dot3(split(turned), split(came))
        total[width:, :] += jnp.sum((came * came).reshape(-1, 8, width), axis=0)
        norm[...] += jnp.broadcast_to(jnp.sum(turned * turned, axis=1, keepdims=True), norm.shape)

    block = (BLOCK, width)
    by_row = pl.BlockSpec(block, lambda i: (i, 0))
    pltpu.emit_pipeline(
        body,
        grid=(rows // BLOCK,),
        in_specs=[by_row, pl.BlockSpec(block, lambda i: (i, 1))],
        out_specs=[by_row, by_row],
    )(snapshots, snapshots, stay, move)


def first_gram(snapshots, width):
    rows = snapshots.shape[0]
    vmem = pl.BlockSpec(memory_space=pltpu.VMEM)
    anywhere = pl.BlockSpec(memory_space=pl.ANY)
    return pl.pallas_call(
        first_gram_kernel,
        in_specs=[pl.BlockSpec(memory_space=pltpu.HBM)],
        out_specs=[vmem, vmem, anywhere, anywhere],
        out_shape=[
            jax.ShapeDtypeStruct((width + 8, width), jnp.float32),
            jax.ShapeDtypeStruct((width, 128), jnp.float32),
            jax.ShapeDtypeStruct((rows, width), jnp.float32),
            jax.ShapeDtypeStruct((rows, width), jnp.float32),
        ],
        compiler_params=PARAMS,
        cost_estimate=COST,
        name="first_gram",
    )(snapshots)


def gram_kernel(first, turned, came, *refs):
    before, total = refs[0], refs[-1]
    width = came.shape[1]
    value = came[...]
    result = dot3(split(turned[...]), split(value))
    norm = jnp.sum((value * value).reshape(-1, 8, width), axis=0)
    total[:width, :] = result if first else before[:width, :] + result
    total[width:, :] = norm if first else before[width:, :] + norm


def gram(turned, came, before, after=()):
    width = came.shape[1]
    chain = [] if before is None else [before]
    vmem = pl.BlockSpec(memory_space=pltpu.VMEM)
    return pl.pallas_call(
        functools.partial(gram_kernel, before is None),
        in_specs=[vmem] * (2 + len(chain)) + [pl.BlockSpec(memory_space=pl.ANY)] * len(after),
        out_shape=jax.ShapeDtypeStruct((width + 8, width), jnp.float32),
        compiler_params=PARAMS,
        cost_estimate=COST,
        name="gram",
    )(turned, came, *chain, *after)


def rotation_kernel(step, side, both, flags, mine, other, norm, *refs):
    width = mine.shape[1]
    total = mine[...] + other[...]
    norm_move = jnp.sum(total[width:, :], axis=0, keepdims=True)
    coupled = total[:width, :] / (norm[:, side : side + 1] + norm_move + EPSILON)
    turned = coupled.T
    stay_first = flags[step, 0] == 1
    send_is_stay = flags[step, 1] == 1
    coupling = jnp.where(stay_first, coupled, turned)
    coupling_turned = jnp.where(stay_first, turned, coupled)
    identity = eye(width)
    scale = 1.0 / (1.0 + jnp.sum(coupled * coupled))
    left, right = split(coupling_turned), split(coupling)
    base = scale * (identity + dot3(right, left))
    inverse = scale * (2.0 * identity - base)
    base_split = split(base)
    base = 2.0 * base - dot3(base_split, base_split)
    for sweep in range(1, NS_ITERS):
        base_split = split(base)
        inverse = 2.0 * inverse - dot3(split(inverse), base_split)
        if sweep < NS_ITERS - 1:
            base = 2.0 * base - dot3(base_split, base_split)
    product_turned = dot3(left, split(inverse))
    second_second = identity - 2.0 * dot3(split(product_turned), right)
    first_first = 2.0 * inverse - identity
    first_second = 2.0 * product_turned.T
    second_first = -2.0 * product_turned
    stay_stay = jnp.where(stay_first, first_first, second_second)
    move_move = jnp.where(stay_first, second_second, first_first)
    stay_move = jnp.where(stay_first, first_second, second_first)
    move_stay = jnp.where(stay_first, second_first, first_second)
    top = split(jnp.where(send_is_stay, stay_stay, stay_move))
    end = split(jnp.where(send_is_stay, move_stay, move_move))
    if len(refs) == 5:
        stay, move, *refs, sent = refs
        sent[...] = dot3(split(stay[...]), top) + dot3(split(move[...]), end)
    high, low = refs
    for ref, upper, lower in zip((high, low), top, end):
        ref[:width, :width] = upper
        ref[width:, :width] = lower
    if both:
        top = split(jnp.where(send_is_stay, stay_move, stay_stay))
        end = split(jnp.where(send_is_stay, move_move, move_stay))
        for ref, upper, lower in zip((high, low), top, end):
            ref[:width, width:] = upper
            ref[width:, width:] = lower


def view(source, block, grid_of_one=False):
    array, row = source
    if grid_of_one:
        return pl.BlockSpec(block, lambda *_: (row * BLOCK // block[0], 0))
    return pl.BlockSpec(block, lambda i, *_: (row + i, 0))


def rotation(step, side, both, flags, total, norm, piece=()):
    other = shift(total, "row", 1)
    width = total.shape[1]
    size = (piece[2] * BLOCK, width) if piece else None
    matrix = (2 * width, 2 * width if both else width)
    return pl.pallas_call(
        functools.partial(rotation_kernel, step, side, both),
        grid=(1,),
        in_specs=[SMEM, whole(total.shape), whole(other.shape), whole(norm.shape)]
        + [view(source, size, True) for source in piece[:2]],
        out_specs=[whole(matrix)] * 2 + ([whole(size)] if piece else []),
        out_shape=[jax.ShapeDtypeStruct(matrix, jnp.bfloat16)] * 2
        + ([jax.ShapeDtypeStruct(size, jnp.float32)] if piece else []),
        compiler_params=PARAMS,
        cost_estimate=COST,
        name="rotation",
    )(flags, total, other, norm, *[source[0] for source in piece[:2]])


def apply_both_kernel(first, stay, move, high, low, *refs):
    if not first:
        before, *refs = refs
    sent, sent_turned, kept, kept_turned, norm = refs
    width = stay.shape[1]
    joined = jnp.concatenate((stay[...], move[...]), axis=1)
    result = dot3(split(joined), (high[...], low[...]))
    sent[...] = result[:, :width]
    kept[...] = result[:, width:]
    squares = []
    for half, ref in ((result[:, width:], kept_turned), (result[:, :width], sent_turned)):
        turned = half.T
        ref[...] = turned
        squares.append(jnp.broadcast_to(jnp.sum(turned * turned, axis=1, keepdims=True), (width, SIDE)))
    squares = jnp.concatenate(squares, axis=1)
    step = pl.program_id(0)

    @pl.when(step == 0)
    def _():
        norm[...] = squares if first else before[...] + squares

    @pl.when(step > 0)
    def _():
        norm[...] += squares


def apply_both(stay, move, high, low, before, blocks):
    width = high.shape[0] // 2
    rows = blocks * BLOCK
    block = (BLOCK, width)
    by_row = pl.BlockSpec(block, lambda i: (i, 0))
    by_column = pl.BlockSpec((width, BLOCK), lambda i: (0, i))
    norm = whole((width, 2 * SIDE))
    piece = jax.ShapeDtypeStruct((rows, width), jnp.float32)
    turned = jax.ShapeDtypeStruct((width, rows), jnp.float32)
    first = before is None
    return pl.pallas_call(
        functools.partial(apply_both_kernel, first),
        grid=(blocks,),
        in_specs=[view(stay, block), view(move, block), whole(high.shape), whole(low.shape)] + [norm] * (not first),
        out_specs=[by_row, by_column, by_row, by_column, norm],
        out_shape=[piece, turned, piece, turned, jax.ShapeDtypeStruct((width, 2 * SIDE), jnp.float32)],
        compiler_params=PARAMS,
        cost_estimate=COST,
        name="apply_both",
    )(stay[0], move[0], high, low, *([] if first else [before]))


def apply_one_kernel(stay, move, high, low, sent):
    joined = jnp.concatenate((stay[...], move[...]), axis=1)
    sent[...] = dot3(split(joined), (high[...], low[...]))


def apply_one(stay, move, high, low, blocks):
    width = high.shape[0] // 2
    block = (BLOCK, width)
    half = whole((2 * width, width))
    return pl.pallas_call(
        apply_one_kernel,
        grid=(blocks,),
        in_specs=[view(stay, block), view(move, block), half, half],
        out_specs=pl.BlockSpec(block, lambda i: (i, 0)),
        out_shape=jax.ShapeDtypeStruct((blocks * BLOCK, width), jnp.float32),
        compiler_params=PARAMS,
        cost_estimate=COST,
        name="apply_one",
    )(stay[0], move[0], high, low)


def finish_kernel(place, stay, move, high, low, *refs):
    joined = jnp.concatenate((stay[...], move[...]), axis=1)
    refs[-1][...] = dot3(split(joined), (high[...], low[...]))


def finish(kept, flags, stay, move, high, low, before, start, blocks, shape):
    width = high.shape[0] // 2
    block = (BLOCK, width)
    first = before is None
    half = pl.BlockSpec((2 * width, width), lambda *_: (0, kept))
    out = pl.BlockSpec(block, lambda i, place: (start + i, place[place.shape[0] - 1, 1 - kept]))
    return pl.pallas_call(
        finish_kernel,
        grid_spec=pltpu.PrefetchScalarGridSpec(
            num_scalar_prefetch=1,
            grid=(blocks,),
            in_specs=[view(stay, block), view(move, block), half, half]
            + [pl.BlockSpec(memory_space=pl.ANY)] * (not first),
            out_specs=out,
        ),
        out_shape=jax.ShapeDtypeStruct(shape, jnp.float32),
        input_output_aliases={} if first else {5: 0},
        compiler_params=PARAMS,
        cost_estimate=COST,
        name="finish",
    )(flags, stay[0], move[0], high, low, *([] if first else [before]))


def per_device(snapshots, plan):
    rows = snapshots.shape[0]
    width = snapshots.shape[1] // 2
    rounds = plan.shape[0]
    blocks = rows // BLOCK
    size = blocks // PIECES
    starts = range(0, blocks, size)
    device = lax.axis_index("pair")
    count = lax.axis_size("pair")
    total, norm, stay, move = first_gram(snapshots, width)
    flags = make_flags(plan, device[None], count)
    norm = norm + shift(norm, "row", 1)
    stay = [(stay, start) for start in starts]
    move = [(move, start) for start in starts]
    high, low, outgoing = rotation(0, 0, True, flags, total, norm, (stay[0], move[0], size))
    arriving = [shift(outgoing, "pair", -2)]
    norm = None
    held = [None] * PIECES
    for piece in [*range(1, PIECES), 0]:
        *held[piece], norm = apply_both(stay[piece], move[piece], high, low, norm, size)
        if piece:
            arriving.append(shift(held[piece][0], "pair", -2))
    move = [(value, 0) for value in arriving]
    for step in range(1, rounds):
        last = step == rounds - 1
        sent = [(value[0], 0) for value in held]
        sent_turned = [value[1] for value in held]
        stay = [(value[2], 0) for value in held]
        stay_turned = [value[3] for value in held]
        norm = norm + shift(norm, "row", 1)
        arriving = [(shift(value, "pair", 2 if step % 2 else -2), 0) for value, _ in stay]

        total = None
        for one, (two, _) in zip(stay_turned, move):
            total = gram(one, two, total)
        high, low = rotation(step, 0, True, flags, total, norm)
        if last:
            field = None
            for piece, start in enumerate(starts):
                field = finish(1, flags, stay[piece], move[piece], high, low, field, start, size, snapshots.shape)
        else:
            own_norm = None
            held = [None] * PIECES
            for piece in range(PIECES):
                *held[piece], own_norm = apply_both(stay[piece], move[piece], high, low, own_norm, size)

        total = None
        for one, (two, _) in zip(sent_turned, arriving):
            total = gram(one, two, total, () if total is not None else (field if last else own_norm,))
        high, low = rotation(rounds + step, SIDE, False, flags, total, norm)
        if last:
            for piece, start in enumerate(starts):
                field = finish(0, flags, sent[piece], arriving[piece], high, low, field, start, size, snapshots.shape)
            return field
        move = [(apply_one(sent[piece], arriving[piece], high, low, size), 0) for piece in range(PIECES)]
        norm = own_norm


def solution(mesh):
    in_specs = (P(("basin", "row"), "pair"), P())
    out_specs = P(("basin", "row"), "pair")
    return jax.shard_map(
        per_device, mesh=mesh, in_specs=in_specs, out_specs=out_specs, check_vma=False
    )
```

```python
import functools

import jax
import jax.numpy as jnp
from jax import lax
from jax.experimental import pallas as pl
from jax.experimental.pallas import tpu as pltpu
from jax.sharding import PartitionSpec as P

NS_ITERS = 6
EPSILON = 1e-06
BLOCK = 256
PIECES = 4
SIDE = 128
PARAMS = pltpu.CompilerParams(vmem_limit_bytes=12 * 1024 * 1024)
LARGE = pltpu.CompilerParams(vmem_limit_bytes=24 * 1024 * 1024)


def shift(value, axis, by):
    size = lax.axis_size(axis)
    return lax.ppermute(value, axis, [(i, (i + by) % size) for i in range(size)])


def split(value):
    high = value.astype(jnp.bfloat16)
    return high, (value - high.astype(jnp.float32)).astype(jnp.bfloat16)


def dot(left, right):
    return jnp.dot(left, right, preferred_element_type=jnp.float32)


def dot3(left, right):
    (left_high, left_low), (right_high, right_low) = left, right
    return dot(left_high, right_high) + dot(left_low, right_high) + dot(left_high, right_low)


def whole(shape):
    return pl.BlockSpec(shape, lambda *_: (0,) * len(shape))


SMEM = pl.BlockSpec(memory_space=pltpu.SMEM)


COST = pl.CostEstimate(flops=1024, bytes_accessed=1024, transcendentals=0)


def eye(size):
    row = lax.broadcasted_iota(jnp.int32, (size, size), 0)
    column = lax.broadcasted_iota(jnp.int32, (size, size), 1)
    return jnp.where(row == column, 1.0, 0.0).astype(jnp.float32)


def route(count, plan, device):
    stay_first = jnp.int32(1)
    flags = []
    for step in range(plan.shape[0]):
        odd = step % 2
        position = lax.rem(device + odd, count)
        upper = lax.rem(position + 1, count)
        second = 2 * position + 1
        second_up = jnp.where((plan[step, 2 * upper] == second) | (plan[step, 2 * upper + 1] == second), 1, 0)
        send_second = second_up if odd else 1 - second_up
        flags.append((stay_first, jnp.where(send_second == stay_first, 0, 1)))
        target = device if odd else upper
        below = lax.rem(target + count - 1, count)
        from_below = jnp.where(plan[step, 2 * target] // 2 == below, 1, 0)
        stay_first = 1 - from_below if odd else from_below
    return flags, stay_first


def flags_kernel(count, plan, device, flags):
    rounds = plan.shape[0]
    own, stay_first = route(count, plan, device[0])
    above, _ = route(count, plan, lax.rem(device[0] + 2, count))
    below, _ = route(count, plan, lax.rem(device[0] + count - 2 % count, count))
    for step in range(rounds):
        flags[step, 0], flags[step, 1] = own[step]
        sender = below[step] if step % 2 else above[step]
        flags[rounds + step, 0] = 1 - sender[0]
        flags[rounds + step, 1] = 1 - sender[1]
    flags[2 * rounds, 0] = 1 - stay_first
    flags[2 * rounds, 1] = stay_first


def make_flags(plan, device, count):
    return pl.pallas_call(
        functools.partial(flags_kernel, count),
        in_specs=[SMEM, SMEM],
        out_specs=SMEM,
        out_shape=jax.ShapeDtypeStruct((2 * plan.shape[0] + 1, 2), jnp.int32),
        compiler_params=PARAMS,
        cost_estimate=COST,
        name="flags",
    )(plan, device)


def column(row):
    return jnp.broadcast_to(row, (SIDE, row.shape[1])).T


def row_sums(value):
    return jnp.sum((value * value).reshape(-1, 8, value.shape[1]), axis=0)


def first_gram_kernel(snapshots, total, norm, stay, move, squares):
    rows, width = stay.shape
    total[...] = jnp.zeros_like(total)
    squares[...] = jnp.zeros_like(squares)

    def body(one, two, stay_part, move_part):
        kept, came = one[...], two[...]
        stay_part[...] = kept
        move_part[...] = came
        total[:width, :] += dot3(split(kept.T), split(came))
        total[width:, :] += row_sums(came)
        squares[...] += row_sums(kept)

    block = (2 * BLOCK, width)
    by_row = pl.BlockSpec(block, lambda i: (i, 0))
    pltpu.emit_pipeline(
        body,
        grid=(rows // (2 * BLOCK),),
        in_specs=[by_row, pl.BlockSpec(block, lambda i: (i, 1))],
        out_specs=[by_row, by_row],
    )(snapshots, snapshots, stay, move)
    norm[...] = column(jnp.sum(squares[...], axis=0, keepdims=True))


def first_gram(snapshots, width):
    rows = snapshots.shape[0]
    vmem = pl.BlockSpec(memory_space=pltpu.VMEM)
    anywhere = pl.BlockSpec(memory_space=pl.ANY)
    return pl.pallas_call(
        first_gram_kernel,
        in_specs=[pl.BlockSpec(memory_space=pltpu.HBM)],
        out_specs=[vmem, vmem, anywhere, anywhere],
        out_shape=[
            jax.ShapeDtypeStruct((width + 8, width), jnp.float32),
            jax.ShapeDtypeStruct((width, 128), jnp.float32),
            jax.ShapeDtypeStruct((rows, width), jnp.float32),
            jax.ShapeDtypeStruct((rows, width), jnp.float32),
        ],
        scratch_shapes=[pltpu.VMEM((8, width), jnp.float32)],
        compiler_params=PARAMS,
        cost_estimate=COST,
        name="first_gram",
    )(snapshots)


def add_gram(total, turned, value, first):
    width = value.shape[1]
    result, norm = dot3(split(turned), split(value)), row_sums(value)
    total[:width, :] = result if first else total[:width, :] + result
    total[width:, :] = norm if first else total[width:, :] + norm


def parts(refs):
    return [ref.at[pl.ds(start, BLOCK)] for ref in refs for start in range(0, ref.shape[0], BLOCK)]


def turned_parts(refs):
    return [ref.at[:, pl.ds(start, BLOCK)] for ref in refs for start in range(0, ref.shape[1], BLOCK)]


def gram_kernel(counts, offset, *refs):
    turned, refs = refs[: counts[0]], refs[counts[0] :]
    came, refs = refs[: counts[1]], refs[counts[1] :]
    total = refs[-1]
    if counts[2]:
        total[...] = refs[0][...]
    for index, (one, two) in enumerate(zip(turned_parts(turned)[offset:], parts(came))):
        add_gram(total, one[...], two[...], index + counts[2] == 0)


def gram(turned, came, before=(), after=(), offset=0):
    width = came[0].shape[1]
    vmem = pl.BlockSpec(memory_space=pltpu.VMEM)
    args = (*turned, *came, *before)
    return pl.pallas_call(
        functools.partial(gram_kernel, (len(turned), len(came), len(before)), offset),
        in_specs=[vmem] * len(args) + [pl.BlockSpec(memory_space=pl.ANY)] * len(after),
        out_specs=vmem,
        out_shape=jax.ShapeDtypeStruct((width + 8, width), jnp.float32),
        compiler_params=PARAMS,
        cost_estimate=COST,
        name="gram",
    )(*args, *after)


def rotation_kernel(step, side, both, flags, mine, other, norm, *refs):
    width = mine.shape[1]
    total = mine[...] + other[...]
    norm_move = jnp.sum(total[width:, :], axis=0, keepdims=True)
    coupled = total[:width, :] / (norm[:, side : side + 1] + norm_move + EPSILON)
    turned = coupled.T
    stay_first = flags[step, 0] == 1
    send_is_stay = flags[step, 1] == 1
    coupling = jnp.where(stay_first, coupled, turned)
    coupling_turned = jnp.where(stay_first, turned, coupled)
    identity = eye(width)
    scale = 1.0 / (1.0 + jnp.sum(coupled * coupled))
    left, right = split(coupling_turned), split(coupling)
    base = scale * (identity + dot3(right, left))
    inverse = scale * (2.0 * identity - base)
    base_split = split(base)
    base = 2.0 * base - dot3(base_split, base_split)
    for sweep in range(1, NS_ITERS):
        base_split = split(base)
        inverse = 2.0 * inverse - dot3(split(inverse), base_split)
        if sweep < NS_ITERS - 1:
            base = 2.0 * base - dot3(base_split, base_split)
    product_turned = dot3(left, split(inverse))
    second_second = identity - 2.0 * dot3(split(product_turned), right)
    first_first = 2.0 * inverse - identity
    first_second = 2.0 * product_turned.T
    second_first = -2.0 * product_turned
    stay_stay = jnp.where(stay_first, first_first, second_second)
    move_move = jnp.where(stay_first, second_second, first_first)
    stay_move = jnp.where(stay_first, first_second, second_first)
    move_stay = jnp.where(stay_first, second_first, first_second)
    top = split(jnp.where(send_is_stay, stay_stay, stay_move))
    end = split(jnp.where(send_is_stay, move_stay, move_move))
    if len(refs) == 5:
        stay, move, *refs, sent = refs
        sent[...] = dot3(split(stay[...]), top) + dot3(split(move[...]), end)
    high, low = refs
    for ref, upper, lower in zip((high, low), top, end):
        ref[:width, :width] = upper
        ref[width:, :width] = lower
    if both:
        top = split(jnp.where(send_is_stay, stay_move, stay_stay))
        end = split(jnp.where(send_is_stay, move_move, move_stay))
        for ref, upper, lower in zip((high, low), top, end):
            ref[:width, width:] = upper
            ref[width:, width:] = lower


def view(source, block, grid_of_one=False):
    array, row = source
    if grid_of_one:
        return pl.BlockSpec(block, lambda *_: (row * BLOCK // block[0], 0))
    return pl.BlockSpec(block, lambda i, *_: (row + i, 0))


def rotation(step, side, both, flags, total, norm, piece=()):
    other = shift(total, "row", 1)
    width = total.shape[1]
    size = (piece[2] * BLOCK, width) if piece else None
    matrix = (2 * width, 2 * width if both else width)
    return pl.pallas_call(
        functools.partial(rotation_kernel, step, side, both),
        grid=(1,),
        in_specs=[SMEM, whole(total.shape), whole(other.shape), whole(norm.shape)]
        + [view(source, size, True) for source in piece[:2]],
        out_specs=[whole(matrix)] * 2 + ([whole(size)] if piece else []),
        out_shape=[jax.ShapeDtypeStruct(matrix, jnp.bfloat16)] * 2
        + ([jax.ShapeDtypeStruct(size, jnp.float32)] if piece else []),
        compiler_params=PARAMS,
        cost_estimate=COST,
        name="rotation",
    )(flags, total, other, norm, *[source[0] for source in piece[:2]])


def apply_both_kernel(first, stay, move, high, low, *refs):
    if not first:
        before, *refs = refs
    sent, sent_turned, kept, kept_turned, norm = refs
    width = stay.shape[1]
    joined = jnp.concatenate((stay[...], move[...]), axis=1)
    result = dot3(split(joined), (high[...], low[...]))
    sent[...] = result[:, :width]
    kept[...] = result[:, width:]
    squares = []
    for half, ref in ((result[:, width:], kept_turned), (result[:, :width], sent_turned)):
        turned = half.T
        ref[...] = turned
        squares.append(jnp.broadcast_to(jnp.sum(turned * turned, axis=1, keepdims=True), (width, SIDE)))
    squares = jnp.concatenate(squares, axis=1)
    step = pl.program_id(0)

    @pl.when(step == 0)
    def _():
        norm[...] = squares if first else before[...] + squares

    @pl.when(step > 0)
    def _():
        norm[...] += squares


def apply_both(stay, move, high, low, before, blocks):
    width = high.shape[0] // 2
    rows = blocks * BLOCK
    block = (BLOCK, width)
    by_row = pl.BlockSpec(block, lambda i: (i, 0))
    by_column = pl.BlockSpec((width, BLOCK), lambda i: (0, i))
    norm = whole((width, 2 * SIDE))
    piece = jax.ShapeDtypeStruct((rows, width), jnp.float32)
    turned = jax.ShapeDtypeStruct((width, rows), jnp.float32)
    first = before is None
    return pl.pallas_call(
        functools.partial(apply_both_kernel, first),
        grid=(blocks,),
        in_specs=[view(stay, block), view(move, block), whole(high.shape), whole(low.shape)] + [norm] * (not first),
        out_specs=[by_row, by_column, by_row, by_column, norm],
        out_shape=[piece, turned, piece, turned, jax.ShapeDtypeStruct((width, 2 * SIDE), jnp.float32)],
        compiler_params=PARAMS,
        cost_estimate=COST,
        name="apply_both",
    )(stay[0], move[0], high, low, *([] if first else [before]))


def rotate(one, two, high, low):
    joined = jnp.concatenate((one[...], two[...]), axis=1)
    return dot3(split(joined), (high[...], low[...]))


def apply_all_kernel(counts, *refs):
    stay, refs = refs[: counts[0]], refs[counts[0] :]
    move, refs = refs[: counts[1]], refs[counts[1] :]
    high, low, sent, sent_turned, kept_turned, norm, *kept = refs
    width = norm.shape[0]
    sums = [0.0, 0.0]
    for index, (one, two, out) in enumerate(zip(parts(stay), parts(move), parts(kept))):
        result = rotate(one, two, high, low)
        rows = pl.ds(index * BLOCK, BLOCK)
        for half, (ref, turned) in enumerate(((out, kept_turned), (sent.at[rows], sent_turned))):
            value = result[:, width:] if half == 0 else result[:, :width]
            ref[...] = value
            turned[:, rows] = value.T
            sums[half] += row_sums(value)
    for half in range(2):
        norm[:, half * SIDE : (half + 1) * SIDE] = column(jnp.sum(sums[half], axis=0, keepdims=True))


def apply_all(stay, move, high, low, sizes):
    width = high.shape[0] // 2
    rows = sum(sizes)
    shapes = [(rows, width), (width, rows), (width, rows), (width, 2 * SIDE)] + [(size, width) for size in sizes]
    vmem = pl.BlockSpec(memory_space=pltpu.VMEM)
    sent, sent_turned, kept_turned, norm, *kept = pl.pallas_call(
        functools.partial(apply_all_kernel, (len(stay), len(move))),
        in_specs=[vmem] * (len(stay) + len(move) + 2),
        out_specs=[vmem] * len(shapes),
        out_shape=[jax.ShapeDtypeStruct(shape, jnp.float32) for shape in shapes],
        compiler_params=LARGE,
        cost_estimate=COST,
        name="apply_all",
    )(*stay, *move, high, low)
    return sent, sent_turned, kept, kept_turned, norm


def rebuild_kernel(counts, *refs):
    sent, refs = refs[: counts[0]], refs[counts[0] :]
    raw, refs = refs[: counts[1]], refs[counts[1] :]
    high, low, turned, came, total = refs
    for index, (one, two) in enumerate(zip(parts(sent), parts(raw))):
        value = rotate(one, two, high, low)
        rows = pl.ds(index * BLOCK, BLOCK)
        came[rows, :] = value
        add_gram(total, turned[:, rows], value, index == 0)


def rebuild(sent, raw, high, low, turned):
    width, rows = turned.shape
    vmem = pl.BlockSpec(memory_space=pltpu.VMEM)
    args = (*sent, *raw, high, low, turned)
    return pl.pallas_call(
        functools.partial(rebuild_kernel, (len(sent), len(raw))),
        in_specs=[vmem] * len(args),
        out_specs=[vmem] * 2,
        out_shape=[
            jax.ShapeDtypeStruct((rows, width), jnp.float32),
            jax.ShapeDtypeStruct((width + 8, width), jnp.float32),
        ],
        compiler_params=LARGE,
        cost_estimate=COST,
        name="rebuild",
    )(*args)


def finish_kernel(counts, kept, aliased, flags, *refs):
    stay, refs = refs[: counts[0]], refs[counts[0] :]
    move, refs = refs[: counts[1]], refs[counts[1] :]
    high, low, *refs = refs
    out, token, held, done = refs[aliased:]
    width = held.shape[2]
    token[...] = jnp.zeros_like(token)
    half = pl.ds(width, width) if kept else pl.ds(0, width)
    column_of = flags[flags.shape[0] - 1, 1 - kept]
    columns = pl.ds(pl.multiple_of(column_of * width, width), width)
    copies = []
    for index, (one, two) in enumerate(zip(parts(stay), parts(move))):
        held[index] = rotate(one, two, high.at[:, half], low.at[:, half])
        copy = pltpu.make_async_copy(held.at[index], out.at[pl.ds(index * BLOCK, BLOCK), columns], done.at[index])
        copy.start()
        copies.append(copy)
    for copy in copies:
        copy.wait()


def finish(kept, flags, stay, move, high, low, before, shape):
    width = high.shape[0] // 2
    vmem = pl.BlockSpec(memory_space=pltpu.VMEM)
    anywhere = pl.BlockSpec(memory_space=pl.ANY)
    args = (flags, *stay, *move, high, low)
    blocks = shape[0] // BLOCK
    return pl.pallas_call(
        functools.partial(finish_kernel, (len(stay), len(move)), kept, len(before)),
        in_specs=[SMEM] + [vmem] * (len(args) - 1) + [anywhere] * len(before),
        out_specs=[anywhere, vmem],
        out_shape=[jax.ShapeDtypeStruct(shape, jnp.float32), jax.ShapeDtypeStruct((8, SIDE), jnp.float32)],
        input_output_aliases={len(args): 0} if before else {},
        scratch_shapes=[pltpu.VMEM((blocks, BLOCK, width), jnp.float32), pltpu.SemaphoreType.DMA((blocks,))],
        compiler_params=LARGE,
        cost_estimate=COST,
        name="finish",
    )(*args, *before)


def per_device(snapshots, plan):
    rows = snapshots.shape[0]
    width = snapshots.shape[1] // 2
    rounds = plan.shape[0]
    blocks = rows // BLOCK
    size = blocks // PIECES
    starts = range(0, blocks, size)
    device = lax.axis_index("pair")
    count = lax.axis_size("pair")
    total, norm, stay, move = first_gram(snapshots, width)
    flags = make_flags(plan, device[None], count)
    norm = norm + shift(norm, "row", 1)
    stay = [(stay, start) for start in starts]
    move = [(move, start) for start in starts]
    high, low, outgoing = rotation(0, 0, True, flags, total, norm, (stay[0], move[0], size))
    move_next = [shift(outgoing, "pair", -2)]
    norm = None
    held = [None] * PIECES
    for piece in [*range(1, PIECES), 0]:
        *held[piece], norm = apply_both(stay[piece], move[piece], high, low, norm, size)
        if piece:
            move_next.append(shift(held[piece][0], "pair", -2))
    move = move_next
    sent, sent_turned, stay, stay_turned = zip(*held)
    total = ()
    for one, two in zip(stay_turned, move):
        total = (gram((one,), (two,), total),)
    (total,) = total
    for step in range(1, rounds):
        last = step == rounds - 1
        raw = [shift(value, "pair", 2 if step % 2 else -2) for value in stay]
        norm = norm + shift(norm, "row", 1)
        high, low = rotation(step, 0, True, flags, total, norm)
        if last:
            field, token = finish(1, flags, stay, move, high, low, (), snapshots.shape)
        else:
            sizes = [rows // 2, rows // 4, rows // 4] if step == rounds - 2 else [rows // 2] * 2
            new_sent, new_sent_turned, stay, stay_turned, token = apply_all(stay, move, high, low, sizes)
        if last:
            total = ()
            offset = 0
            for value in raw:
                total = (gram(sent_turned, (value,), total, () if total else (token,), offset),)
                offset += value.shape[0] // BLOCK
            (total,) = total
        else:
            total = gram(sent_turned, raw, (), (token,))
        high, low = rotation(rounds + step, SIDE, False, flags, total, norm)
        if last:
            return finish(0, flags, sent, raw, high, low, (field,), snapshots.shape)[0]
        came, total = rebuild(sent, raw, high, low, stay_turned)
        move, norm = (came,), token
        sent, sent_turned = (new_sent,), (new_sent_turned,)


def solution(mesh):
    in_specs = (P(("basin", "row"), "pair"), P())
    out_specs = P(("basin", "row"), "pair")
    return jax.shard_map(
        per_device, mesh=mesh, in_specs=in_specs, out_specs=out_specs, check_vma=False
    )
```

```python
import functools

import jax
import jax.numpy as jnp
from jax import lax
from jax.experimental import pallas as pl
from jax.experimental.pallas import tpu as pltpu
from jax.sharding import PartitionSpec as P

NS_ITERS = 6
EPSILON = 1e-06
BLOCK = 256
PIECES = 4
SIDE = 128
PUT = 128
PARAMS = pltpu.CompilerParams(vmem_limit_bytes=12 * 1024 * 1024)
LARGE = pltpu.CompilerParams(vmem_limit_bytes=24 * 1024 * 1024)


def shift(value, axis, by):
    size = lax.axis_size(axis)
    return lax.ppermute(value, axis, [(i, (i + by) % size) for i in range(size)])


def split(value):
    high = value.astype(jnp.bfloat16)
    return high, (value - high.astype(jnp.float32)).astype(jnp.bfloat16)


def dot(left, right):
    return jnp.dot(left, right, preferred_element_type=jnp.float32)


def dot3(left, right):
    (left_high, left_low), (right_high, right_low) = left, right
    return dot(left_high, right_high) + dot(left_low, right_high) + dot(left_high, right_low)


def whole(shape):
    return pl.BlockSpec(shape, lambda *_: (0,) * len(shape))


SMEM = pl.BlockSpec(memory_space=pltpu.SMEM)


COST = pl.CostEstimate(flops=1024, bytes_accessed=1024, transcendentals=0)
LONG = pl.CostEstimate(flops=4_000_000_000, bytes_accessed=1024, transcendentals=0)


def eye(size):
    row = lax.broadcasted_iota(jnp.int32, (size, size), 0)
    column = lax.broadcasted_iota(jnp.int32, (size, size), 1)
    return jnp.where(row == column, 1.0, 0.0).astype(jnp.float32)


def route(count, plan, device):
    stay_first = jnp.int32(1)
    flags = []
    for step in range(plan.shape[0]):
        odd = step % 2
        position = lax.rem(device + odd, count)
        upper = lax.rem(position + 1, count)
        second = 2 * position + 1
        second_up = jnp.where((plan[step, 2 * upper] == second) | (plan[step, 2 * upper + 1] == second), 1, 0)
        send_second = second_up if odd else 1 - second_up
        flags.append((stay_first, jnp.where(send_second == stay_first, 0, 1)))
        target = device if odd else upper
        below = lax.rem(target + count - 1, count)
        from_below = jnp.where(plan[step, 2 * target] // 2 == below, 1, 0)
        stay_first = 1 - from_below if odd else from_below
    return flags, stay_first


def flags_kernel(count, plan, device, flags):
    rounds = plan.shape[0]
    own, stay_first = route(count, plan, device[0])
    above, _ = route(count, plan, lax.rem(device[0] + 2, count))
    below, _ = route(count, plan, lax.rem(device[0] + count - 2 % count, count))
    for step in range(rounds):
        flags[step, 0], flags[step, 1] = own[step]
        sender = below[step] if step % 2 else above[step]
        flags[rounds + step, 0] = 1 - sender[0]
        flags[rounds + step, 1] = 1 - sender[1]
    flags[2 * rounds, 0] = 1 - stay_first
    flags[2 * rounds, 1] = stay_first
    flags[2 * rounds + 1, 0] = device[1]
    flags[2 * rounds + 1, 1] = device[1]


def make_flags(plan, device, count):
    return pl.pallas_call(
        functools.partial(flags_kernel, count),
        in_specs=[SMEM, SMEM],
        out_specs=SMEM,
        out_shape=jax.ShapeDtypeStruct((2 * plan.shape[0] + 2, 2), jnp.int32),
        compiler_params=PARAMS,
        cost_estimate=COST,
        name="flags",
    )(plan, device)


def column(row):
    return jnp.broadcast_to(row, (SIDE, row.shape[1])).T


def row_sums(value):
    return jnp.sum((value * value).reshape(-1, 8, value.shape[1]), axis=0)


def first_gram_kernel(snapshots, total, norm, stay, move, squares):
    rows, width = stay.shape
    total[...] = jnp.zeros_like(total)
    squares[...] = jnp.zeros_like(squares)

    def body(one, two, stay_part, move_part):
        kept, came = one[...], two[...]
        stay_part[...] = kept
        move_part[...] = came
        total[:width, :] += dot3(split(kept.T), split(came))
        total[width:, :] += row_sums(came)
        squares[...] += row_sums(kept)

    block = (2 * BLOCK, width)
    by_row = pl.BlockSpec(block, lambda i: (i, 0))
    pltpu.emit_pipeline(
        body,
        grid=(rows // (2 * BLOCK),),
        in_specs=[by_row, pl.BlockSpec(block, lambda i: (i, 1))],
        out_specs=[by_row, by_row],
    )(snapshots, snapshots, stay, move)
    norm[...] = column(jnp.sum(squares[...], axis=0, keepdims=True))


def first_gram(snapshots, width):
    rows = snapshots.shape[0]
    vmem = pl.BlockSpec(memory_space=pltpu.VMEM)
    anywhere = pl.BlockSpec(memory_space=pl.ANY)
    return pl.pallas_call(
        first_gram_kernel,
        in_specs=[pl.BlockSpec(memory_space=pltpu.HBM)],
        out_specs=[vmem, vmem, anywhere, anywhere],
        out_shape=[
            jax.ShapeDtypeStruct((width + 8, width), jnp.float32),
            jax.ShapeDtypeStruct((width, 128), jnp.float32),
            jax.ShapeDtypeStruct((rows, width), jnp.float32),
            jax.ShapeDtypeStruct((rows, width), jnp.float32),
        ],
        scratch_shapes=[pltpu.VMEM((8, width), jnp.float32)],
        compiler_params=pltpu.CompilerParams(vmem_limit_bytes=48 * 1024 * 1024),
        cost_estimate=COST,
        name="first_gram",
    )(snapshots)


def add_gram(total, turned, value, first):
    width = value.shape[1]
    result, norm = dot3(split(turned), split(value)), row_sums(value)
    total[:width, :] = result if first else total[:width, :] + result
    total[width:, :] = norm if first else total[width:, :] + norm


def parts(refs):
    return [ref.at[pl.ds(start, BLOCK)] for ref in refs for start in range(0, ref.shape[0], BLOCK)]


def turned_parts(refs):
    return [ref.at[:, pl.ds(start, BLOCK)] for ref in refs for start in range(0, ref.shape[1], BLOCK)]


def gram_kernel(counts, offset, *refs):
    turned, refs = refs[: counts[0]], refs[counts[0] :]
    came, refs = refs[: counts[1]], refs[counts[1] :]
    total = refs[-1]
    if counts[2]:
        total[...] = refs[0][...]
    for index, (one, two) in enumerate(zip(turned_parts(turned)[offset:], parts(came))):
        add_gram(total, one[...], two[...], index + counts[2] == 0)


def gram(turned, came, before=(), after=(), offset=0):
    width = came[0].shape[1]
    vmem = pl.BlockSpec(memory_space=pltpu.VMEM)
    args = (*turned, *came, *before)
    return pl.pallas_call(
        functools.partial(gram_kernel, (len(turned), len(came), len(before)), offset),
        in_specs=[vmem] * len(args) + [pl.BlockSpec(memory_space=pl.ANY)] * len(after),
        out_specs=vmem,
        out_shape=jax.ShapeDtypeStruct((width + 8, width), jnp.float32),
        compiler_params=PARAMS,
        cost_estimate=COST,
        name="gram",
    )(*args, *after)


def rotation_kernel(step, side, both, note, flags, mine, other, norm, *refs):
    width = mine.shape[1]
    first_core = flags[flags.shape[0] - 1, 0] == 0
    if note == "read":
        one, two = mine[: width // 2, :], other[: width // 2, :]
        total = jnp.concatenate((jnp.where(first_core, one, two), jnp.where(first_core, two, one)), axis=0)
        norm_move = mine[width // 2 : width // 2 + 1, :]
        norm_stay = column(mine[width // 2 + 1 : width // 2 + 2, :])[:, :1]
    else:
        total = mine[...] + other[...]
        norm_move = jnp.sum(total[width:, :], axis=0, keepdims=True)
        norm_stay = norm[:, side : side + 1]
        total = total[:width, :]
    if note == "write":
        *refs, message = refs
        message[: width // 2, :] = jnp.where(first_core, total[: width // 2, :], total[width // 2 :, :])
        stay_row = norm[:, side : side + SIDE].T[:1, :]
        index = lax.broadcasted_iota(jnp.int32, (8, width), 0)
        message[width // 2 :, :] = jnp.where(index == 0, norm_move, stay_row)
    coupled = total / (norm_stay + norm_move + EPSILON)
    turned = coupled.T
    stay_first = flags[step, 0] == (0 if note == "read" else 1)
    send_is_stay = flags[step, 1] == (0 if note == "read" else 1)
    coupling = jnp.where(stay_first, coupled, turned)
    coupling_turned = jnp.where(stay_first, turned, coupled)
    identity = eye(width)
    scale = 1.0 / (1.0 + jnp.sum(coupled * coupled))
    left, right = split(coupling_turned), split(coupling)
    base = scale * (identity + dot3(right, left))
    inverse = scale * (2.0 * identity - base)
    base_split = split(base)
    base = 2.0 * base - dot3(base_split, base_split)
    for sweep in range(1, NS_ITERS):
        base_split = split(base)
        inverse = 2.0 * inverse - dot3(split(inverse), base_split)
        if sweep < NS_ITERS - 1:
            base = 2.0 * base - dot3(base_split, base_split)
    product_turned = dot3(left, split(inverse))
    second_second = identity - 2.0 * dot3(split(product_turned), right)
    first_first = 2.0 * inverse - identity
    first_second = 2.0 * product_turned.T
    second_first = -2.0 * product_turned
    stay_stay = jnp.where(stay_first, first_first, second_second)
    move_move = jnp.where(stay_first, second_second, first_first)
    stay_move = jnp.where(stay_first, first_second, second_first)
    move_stay = jnp.where(stay_first, second_first, first_second)
    top = split(jnp.where(send_is_stay, stay_stay, stay_move))
    end = split(jnp.where(send_is_stay, move_stay, move_move))
    if len(refs) > 2:
        stay, move, *refs, sent = refs
        sent[...] = dot3(split(stay[...]), top) + dot3(split(move[...]), end)
    high, low = refs
    for ref, upper, lower in zip((high, low), top, end):
        ref[:width, :width] = upper
        ref[width:, :width] = lower
    if both:
        top = split(jnp.where(send_is_stay, stay_move, stay_stay))
        end = split(jnp.where(send_is_stay, move_move, move_stay))
        for ref, upper, lower in zip((high, low), top, end):
            ref[:width, width:] = upper
            ref[width:, width:] = lower


def view(source, block, grid_of_one=False):
    array, row = source
    if grid_of_one:
        return pl.BlockSpec(block, lambda *_: (row * BLOCK // block[0], 0))
    return pl.BlockSpec(block, lambda i, *_: (row + i, 0))


def rotation(step, side, both, flags, total, norm, piece=(), note=None):
    other = shift(total, "row", 1)
    width = total.shape[1]
    size = (piece[2] * BLOCK, width) if piece else None
    matrix = (2 * width, 2 * width if both else width)
    shapes = [size] if piece else [(width // 2 + 8, width)] if note == "write" else []
    return pl.pallas_call(
        functools.partial(rotation_kernel, step, side, both, note),
        grid=(1,),
        in_specs=[SMEM, whole(total.shape), whole(other.shape), whole(norm.shape)]
        + [view(source, size, True) for source in piece[:2]],
        out_specs=[whole(matrix)] * 2 + [whole(shape) for shape in shapes],
        out_shape=[jax.ShapeDtypeStruct(matrix, jnp.bfloat16)] * 2
        + [jax.ShapeDtypeStruct(shape, jnp.float32) for shape in shapes],
        compiler_params=PARAMS,
        cost_estimate=LONG if note == "read" else COST,
        name="rotation",
    )(flags, total, other, norm, *[source[0] for source in piece[:2]])


def apply_both_kernel(first, stay, move, high, low, *refs):
    if not first:
        before, *refs = refs
    sent, sent_turned, kept, kept_turned, norm = refs
    width = stay.shape[1]
    joined = jnp.concatenate((stay[...], move[...]), axis=1)
    result = dot3(split(joined), (high[...], low[...]))
    sent[...] = result[:, :width]
    kept[...] = result[:, width:]
    squares = []
    for half, ref in ((result[:, width:], kept_turned), (result[:, :width], sent_turned)):
        turned = half.T
        ref[...] = turned
        squares.append(jnp.broadcast_to(jnp.sum(turned * turned, axis=1, keepdims=True), (width, SIDE)))
    squares = jnp.concatenate(squares, axis=1)
    step = pl.program_id(0)

    @pl.when(step == 0)
    def _():
        norm[...] = squares if first else before[...] + squares

    @pl.when(step > 0)
    def _():
        norm[...] += squares


def apply_both(stay, move, high, low, before, blocks):
    width = high.shape[0] // 2
    rows = blocks * BLOCK
    block = (BLOCK, width)
    by_row = pl.BlockSpec(block, lambda i: (i, 0))
    by_column = pl.BlockSpec((width, BLOCK), lambda i: (0, i))
    norm = whole((width, 2 * SIDE))
    piece = jax.ShapeDtypeStruct((rows, width), jnp.float32)
    turned = jax.ShapeDtypeStruct((width, rows), jnp.float32)
    first = before is None
    return pl.pallas_call(
        functools.partial(apply_both_kernel, first),
        grid=(blocks,),
        in_specs=[view(stay, block), view(move, block), whole(high.shape), whole(low.shape)] + [norm] * (not first),
        out_specs=[by_row, by_column, by_row, by_column, norm],
        out_shape=[piece, turned, piece, turned, jax.ShapeDtypeStruct((width, 2 * SIDE), jnp.float32)],
        compiler_params=PARAMS,
        cost_estimate=COST,
        name="apply_both",
    )(stay[0], move[0], high, low, *([] if first else [before]))


def rotate(one, two, high, low):
    joined = jnp.concatenate((one[...], two[...]), axis=1)
    return dot3(split(joined), (high[...], low[...]))


def apply_all_kernel(counts, *refs):
    stay, refs = refs[: counts[0]], refs[counts[0] :]
    move, refs = refs[: counts[1]], refs[counts[1] :]
    high, low, sent, sent_turned, kept_turned, norm, *kept = refs
    width = norm.shape[0]
    sums = [0.0, 0.0]
    for index, (one, two, out) in enumerate(zip(parts(stay), parts(move), parts(kept))):
        result = rotate(one, two, high, low)
        rows = pl.ds(index * BLOCK, BLOCK)
        for half, (ref, turned) in enumerate(((out, kept_turned), (sent.at[rows], sent_turned))):
            value = result[:, width:] if half == 0 else result[:, :width]
            ref[...] = value
            turned[:, rows] = value.T
            sums[half] += row_sums(value)
    for half in range(2):
        norm[:, half * SIDE : (half + 1) * SIDE] = column(jnp.sum(sums[half], axis=0, keepdims=True))


def apply_all(stay, move, high, low, sizes):
    width = high.shape[0] // 2
    rows = sum(sizes)
    shapes = [(rows, width), (width, rows), (width, rows), (width, 2 * SIDE)] + [(size, width) for size in sizes]
    vmem = pl.BlockSpec(memory_space=pltpu.VMEM)
    sent, sent_turned, kept_turned, norm, *kept = pl.pallas_call(
        functools.partial(apply_all_kernel, (len(stay), len(move))),
        in_specs=[vmem] * (len(stay) + len(move) + 2),
        out_specs=[vmem] * len(shapes),
        out_shape=[jax.ShapeDtypeStruct(shape, jnp.float32) for shape in shapes],
        compiler_params=LARGE,
        cost_estimate=COST,
        name="apply_all",
    )(*stay, *move, high, low)
    return sent, sent_turned, kept, kept_turned, norm


def rebuild_kernel(counts, *refs):
    sent, refs = refs[: counts[0]], refs[counts[0] :]
    raw, refs = refs[: counts[1]], refs[counts[1] :]
    high, low, turned, came, total = refs
    for index, (one, two) in enumerate(zip(parts(sent), parts(raw))):
        value = rotate(one, two, high, low)
        rows = pl.ds(index * BLOCK, BLOCK)
        came[rows, :] = value
        add_gram(total, turned[:, rows], value, index == 0)


def rebuild(sent, raw, high, low, turned):
    width, rows = turned.shape
    vmem = pl.BlockSpec(memory_space=pltpu.VMEM)
    args = (*sent, *raw, high, low, turned)
    return pl.pallas_call(
        functools.partial(rebuild_kernel, (len(sent), len(raw))),
        in_specs=[vmem] * len(args),
        out_specs=[vmem] * 2,
        out_shape=[
            jax.ShapeDtypeStruct((rows, width), jnp.float32),
            jax.ShapeDtypeStruct((width + 8, width), jnp.float32),
        ],
        compiler_params=LARGE,
        cost_estimate=COST,
        name="rebuild",
    )(*args)


def finish_kernel(counts, kept, aliased, flags, *refs):
    stay, refs = refs[: counts[0]], refs[counts[0] :]
    move, refs = refs[: counts[1]], refs[counts[1] :]
    high, low, *refs = refs
    out, token, held, done = refs[aliased:]
    width = held.shape[2]
    token[...] = jnp.zeros_like(token)
    half = pl.ds(width, width) if kept else pl.ds(0, width)
    column_of = flags[flags.shape[0] - 2, 1 - kept]
    columns = pl.ds(pl.multiple_of(column_of * width, width), width)
    copies = []
    for index, (one, two) in enumerate(zip(parts(stay), parts(move))):
        held[index] = rotate(one, two, high.at[:, half], low.at[:, half])
        copy = pltpu.make_async_copy(held.at[index], out.at[pl.ds(index * BLOCK, BLOCK), columns], done.at[index])
        copy.start()
        copies.append(copy)
    for copy in copies:
        copy.wait()


def put_kernel(start, flags, came, before, out, done):
    width = came.shape[1]
    columns = pl.ds(pl.multiple_of(flags[flags.shape[0] - 2, 1] * width, width), width)
    copies = []
    for index in range(came.shape[0] // PUT):
        rows = pl.ds(index * PUT, PUT)
        copy = pltpu.make_async_copy(came.at[rows], out.at[pl.ds(start + index * PUT, PUT), columns], done.at[index])
        copy.start()
        copies.append(copy)
    for copy in copies:
        copy.wait()


def put(flags, came, before, start):
    vmem = pl.BlockSpec(memory_space=pltpu.VMEM)
    anywhere = pl.BlockSpec(memory_space=pl.ANY)
    return pl.pallas_call(
        functools.partial(put_kernel, start),
        in_specs=[SMEM, vmem, anywhere],
        out_specs=anywhere,
        out_shape=jax.ShapeDtypeStruct(before.shape, jnp.float32),
        input_output_aliases={2: 0},
        scratch_shapes=[pltpu.SemaphoreType.DMA((came.shape[0] // PUT,))],
        compiler_params=PARAMS,
        cost_estimate=COST,
        name="put",
    )(flags, came, before)


def relay_kernel(message, *refs):
    refs[-1][...] = message[...]


def relay(message, after):
    vmem = pl.BlockSpec(memory_space=pltpu.VMEM)
    return pl.pallas_call(
        relay_kernel,
        in_specs=[vmem] + [pl.BlockSpec(memory_space=pl.ANY)] * len(after),
        out_specs=vmem,
        out_shape=jax.ShapeDtypeStruct(message.shape, jnp.float32),
        compiler_params=PARAMS,
        cost_estimate=COST,
        name="relay",
    )(message, *after)


def apply_one_kernel(skip, stay, move, high, low, sent):
    width = sent.shape[1]
    for index, (one, two) in enumerate(zip(parts([stay]), parts([move])[skip:])):
        sent[pl.ds(index * BLOCK, BLOCK), :] = rotate(one, two, high.at[:, pl.ds(0, width)], low.at[:, pl.ds(0, width)])


def apply_one(stay, move, high, low, skip):
    vmem = pl.BlockSpec(memory_space=pltpu.VMEM)
    return pl.pallas_call(
        functools.partial(apply_one_kernel, skip),
        in_specs=[vmem] * 4,
        out_specs=vmem,
        out_shape=jax.ShapeDtypeStruct(stay.shape, jnp.float32),
        compiler_params=PARAMS,
        cost_estimate=COST,
        name="apply_one",
    )(stay, move, high, low)


def finish(kept, flags, stay, move, high, low, before, shape, after=()):
    width = high.shape[0] // 2
    vmem = pl.BlockSpec(memory_space=pltpu.VMEM)
    anywhere = pl.BlockSpec(memory_space=pl.ANY)
    args = (flags, *stay, *move, high, low)
    blocks = shape[0] // BLOCK
    return pl.pallas_call(
        functools.partial(finish_kernel, (len(stay), len(move)), kept, len(before) + len(after)),
        in_specs=[SMEM] + [vmem] * (len(args) - 1) + [anywhere] * (len(before) + len(after)),
        out_specs=[anywhere, vmem],
        out_shape=[jax.ShapeDtypeStruct(shape, jnp.float32), jax.ShapeDtypeStruct((8, SIDE), jnp.float32)],
        input_output_aliases={len(args): 0} if before else {},
        scratch_shapes=[pltpu.VMEM((blocks, BLOCK, width), jnp.float32), pltpu.SemaphoreType.DMA((blocks,))],
        compiler_params=LARGE,
        cost_estimate=COST,
        name="finish",
    )(*args, *before, *after)


def per_device(snapshots, plan):
    rows = snapshots.shape[0]
    width = snapshots.shape[1] // 2
    rounds = plan.shape[0]
    blocks = rows // BLOCK
    size = blocks // PIECES
    starts = range(0, blocks, size)
    device = lax.axis_index("pair")
    count = lax.axis_size("pair")
    total, norm, stay, move = first_gram(snapshots, width)
    flags = make_flags(plan, jnp.stack((device, lax.axis_index("row"))), count)
    norm = norm + shift(norm, "row", 1)
    stay = [(stay, start) for start in starts]
    move = [(move, start) for start in starts]
    high, low, outgoing = rotation(0, 0, True, flags, total, norm, (stay[0], move[0], size))
    move_next = [shift(outgoing, "pair", -2)]
    norm = None
    held = [None] * PIECES
    for piece in [*range(1, PIECES), 0]:
        *held[piece], norm = apply_both(stay[piece], move[piece], high, low, norm, size)
        if piece:
            move_next.append(shift(held[piece][0], "pair", -2))
    move = move_next
    sent, sent_turned, stay, stay_turned = zip(*held)
    total = ()
    for one, two in zip(stay_turned, move):
        total = (gram((one,), (two,), total),)
    (total,) = total
    for step in range(1, rounds):
        last = step == rounds - 1
        direction = 2 if step % 2 else -2
        raw = [shift(value, "pair", direction) for value in (stay[:-1] if last else stay)]
        norm = norm + shift(norm, "row", 1)
        if last:
            break
        high, low = rotation(step, 0, True, flags, total, norm)
        sizes = [rows // 2, rows // 4, rows // 4] if step == rounds - 2 else [rows // 2] * 2
        new_sent, new_sent_turned, stay, stay_turned, own_norm = apply_all(stay, move, high, low, sizes)
        total = gram(sent_turned, raw, (), (own_norm,))
        high, low = rotation(rounds + step, SIDE, False, flags, total, norm)
        came, total = rebuild(sent, raw, high, low, stay_turned)
        move, norm = (came,), own_norm
        sent, sent_turned = (new_sent,), (new_sent_turned,)
    high, low, message = rotation(step, 0, True, flags, total, norm, note="write")
    message = shift(message, "pair", direction)
    outgoing = apply_one(stay[-1], came, high, low, (rows - stay[-1].shape[0]) // BLOCK)
    last_piece = shift(outgoing, "pair", direction)
    field, token = finish(1, flags, stay, move, high, low, (), snapshots.shape, raw)
    message = relay(message, (outgoing, token))
    high, low = rotation(rounds + step, SIDE, False, flags, message, norm, note="read")
    field, _ = finish(0, flags, raw, sent, high, low, (field,), snapshots.shape)
    return put(flags, last_piece, field, rows - last_piece.shape[0])


def solution(mesh):
    in_specs = (P(("basin", "row"), "pair"), P())
    out_specs = P(("basin", "row"), "pair")
    return jax.shard_map(
        per_device, mesh=mesh, in_specs=in_specs, out_specs=out_specs, check_vma=False
    )
```

```python
import functools

import jax
import jax.numpy as jnp
from jax import lax
from jax.experimental import pallas as pl
from jax.experimental.pallas import tpu as pltpu
from jax.sharding import PartitionSpec as P

NS_ITERS = 6
EPSILON = 1e-06
BLOCK = 256
PIECES = 4
SIDE = 128
PUT = 64
FIRST_MIB = 48
PARAMS = pltpu.CompilerParams(vmem_limit_bytes=12 * 1024 * 1024)
LARGE = pltpu.CompilerParams(vmem_limit_bytes=24 * 1024 * 1024)
FIRST = pltpu.CompilerParams(vmem_limit_bytes=FIRST_MIB * 1024 * 1024)


def shift(value, axis, by):
    size = lax.axis_size(axis)
    return lax.ppermute(value, axis, [(i, (i + by) % size) for i in range(size)])


def split(value):
    high = value.astype(jnp.bfloat16)
    return high, (value - high.astype(jnp.float32)).astype(jnp.bfloat16)


def dot(left, right):
    return jnp.dot(left, right, preferred_element_type=jnp.float32)


def dot3(left, right):
    (left_high, left_low), (right_high, right_low) = left, right
    return dot(left_high, right_high) + dot(left_low, right_high) + dot(left_high, right_low)


def whole(shape):
    return pl.BlockSpec(shape, lambda *_: (0,) * len(shape))


SMEM = pl.BlockSpec(memory_space=pltpu.SMEM)


COST = pl.CostEstimate(flops=1024, bytes_accessed=1024, transcendentals=0)
LONG = pl.CostEstimate(flops=4_000_000_000, bytes_accessed=1024, transcendentals=0)


def eye(size):
    row = lax.broadcasted_iota(jnp.int32, (size, size), 0)
    column = lax.broadcasted_iota(jnp.int32, (size, size), 1)
    return jnp.where(row == column, 1.0, 0.0).astype(jnp.float32)


def route(count, plan, device):
    stay_first = jnp.int32(1)
    flags = []
    for step in range(plan.shape[0]):
        odd = step % 2
        position = lax.rem(device + odd, count)
        upper = lax.rem(position + 1, count)
        second = 2 * position + 1
        second_up = jnp.where((plan[step, 2 * upper] == second) | (plan[step, 2 * upper + 1] == second), 1, 0)
        send_second = second_up if odd else 1 - second_up
        flags.append((stay_first, jnp.where(send_second == stay_first, 0, 1)))
        target = device if odd else upper
        below = lax.rem(target + count - 1, count)
        from_below = jnp.where(plan[step, 2 * target] // 2 == below, 1, 0)
        stay_first = 1 - from_below if odd else from_below
    return flags, stay_first


def flags_kernel(count, plan, device, flags):
    rounds = plan.shape[0]
    own, stay_first = route(count, plan, device[0])
    above, _ = route(count, plan, lax.rem(device[0] + 2, count))
    below, _ = route(count, plan, lax.rem(device[0] + count - 2 % count, count))
    for step in range(rounds):
        flags[step, 0], flags[step, 1] = own[step]
        sender = below[step] if step % 2 else above[step]
        flags[rounds + step, 0] = 1 - sender[0]
        flags[rounds + step, 1] = 1 - sender[1]
    flags[2 * rounds, 0] = 1 - stay_first
    flags[2 * rounds, 1] = stay_first
    flags[2 * rounds + 1, 0] = device[1]
    flags[2 * rounds + 1, 1] = device[1]


def make_flags(plan, device, count):
    return pl.pallas_call(
        functools.partial(flags_kernel, count),
        in_specs=[SMEM, SMEM],
        out_specs=SMEM,
        out_shape=jax.ShapeDtypeStruct((2 * plan.shape[0] + 2, 2), jnp.int32),
        compiler_params=PARAMS,
        cost_estimate=COST,
        name="flags",
    )(plan, device)


def column(row):
    return jnp.broadcast_to(row, (SIDE, row.shape[1])).T


def row_sums(value):
    return jnp.sum((value * value).reshape(-1, 8, value.shape[1]), axis=0)


def first_gram_kernel(snapshots, total, norm, held, done):
    rows, columns = snapshots.shape
    width = columns // 2
    copies = []
    for index in range(rows // BLOCK):
        copy = pltpu.make_async_copy(snapshots.at[pl.ds(index * BLOCK, BLOCK)], held.at[index], done.at[index])
        copy.start()
        copies.append(copy)
    squares = jnp.zeros((8, width), jnp.float32)
    for index, copy in enumerate(copies):
        copy.wait()
        kept = held[index, :, :width]
        add_gram(total, kept.T, held[index, :, width:], index == 0)
        squares += row_sums(kept)
    norm[...] = column(jnp.sum(squares, axis=0, keepdims=True))


def first_gram(snapshots):
    rows, columns = snapshots.shape
    width = columns // 2
    vmem = pl.BlockSpec(memory_space=pltpu.VMEM)
    blocks = rows // BLOCK
    return pl.pallas_call(
        first_gram_kernel,
        in_specs=[pl.BlockSpec(memory_space=pl.ANY)],
        out_specs=[vmem, vmem],
        out_shape=[
            jax.ShapeDtypeStruct((width + 8, width), jnp.float32),
            jax.ShapeDtypeStruct((width, SIDE), jnp.float32),
        ],
        scratch_shapes=[pltpu.VMEM((blocks, BLOCK, columns), jnp.float32), pltpu.SemaphoreType.DMA((blocks,))],
        compiler_params=pltpu.CompilerParams(vmem_limit_bytes=52 * 1024 * 1024),
        cost_estimate=COST,
        name="first_gram",
    )(snapshots)


def add_gram(total, turned, value, first):
    width = value.shape[1]
    result, norm = dot3(split(turned), split(value)), row_sums(value)
    total[:width, :] = result if first else total[:width, :] + result
    total[width:, :] = norm if first else total[width:, :] + norm


def parts(refs):
    return [ref.at[pl.ds(start, BLOCK)] for ref in refs for start in range(0, ref.shape[0], BLOCK)]


def turned_parts(refs):
    return [ref.at[:, pl.ds(start, BLOCK)] for ref in refs for start in range(0, ref.shape[1], BLOCK)]


def gram_kernel(counts, offset, *refs):
    turned, refs = refs[: counts[0]], refs[counts[0] :]
    came, refs = refs[: counts[1]], refs[counts[1] :]
    total = refs[-1]
    if counts[2]:
        total[...] = refs[0][...]
    for index, (one, two) in enumerate(zip(turned_parts(turned)[offset:], parts(came))):
        add_gram(total, one[...], two[...], index + counts[2] == 0)


def gram(turned, came, before=(), after=(), offset=0):
    width = came[0].shape[1]
    vmem = pl.BlockSpec(memory_space=pltpu.VMEM)
    args = (*turned, *came, *before)
    return pl.pallas_call(
        functools.partial(gram_kernel, (len(turned), len(came), len(before)), offset),
        in_specs=[vmem] * len(args) + [pl.BlockSpec(memory_space=pl.ANY)] * len(after),
        out_specs=vmem,
        out_shape=jax.ShapeDtypeStruct((width + 8, width), jnp.float32),
        compiler_params=PARAMS,
        cost_estimate=COST,
        name="gram",
    )(*args, *after)


def rotation_kernel(step, side, both, note, piece, flags, mine, other, norm, *refs):
    width = mine.shape[1]
    if piece:
        snapshots, *refs, held, done = refs
        copy = pltpu.make_async_copy(snapshots.at[pl.ds(0, held.shape[0])], held, done)
        copy.start()
    first_core = flags[flags.shape[0] - 1, 0] == 0
    if note == "read":
        one, two = mine[: width // 2, :], other[: width // 2, :]
        total = jnp.concatenate((jnp.where(first_core, one, two), jnp.where(first_core, two, one)), axis=0)
        norm_move = mine[width // 2 : width // 2 + 1, :]
        norm_stay = column(mine[width // 2 + 1 : width // 2 + 2, :])[:, :1]
    else:
        total = mine[...] + other[...]
        norm_move = jnp.sum(total[width:, :], axis=0, keepdims=True)
        norm_stay = norm[:, side : side + 1]
        total = total[:width, :]
    if note == "write":
        *refs, message = refs
        message[: width // 2, :] = jnp.where(first_core, total[: width // 2, :], total[width // 2 :, :])
        stay_row = norm[:, side : side + SIDE].T[:1, :]
        index = lax.broadcasted_iota(jnp.int32, (8, width), 0)
        message[width // 2 :, :] = jnp.where(index == 0, norm_move, stay_row)
    coupled = total / (norm_stay + norm_move + EPSILON)
    turned = coupled.T
    stay_first = flags[step, 0] == (0 if note == "read" else 1)
    send_is_stay = flags[step, 1] == (0 if note == "read" else 1)
    coupling = jnp.where(stay_first, coupled, turned)
    coupling_turned = jnp.where(stay_first, turned, coupled)
    identity = eye(width)
    scale = 1.0 / (1.0 + jnp.sum(coupled * coupled))
    left, right = split(coupling_turned), split(coupling)
    base = scale * (identity + dot3(right, left))
    inverse = scale * (2.0 * identity - base)
    base_split = split(base)
    base = 2.0 * base - dot3(base_split, base_split)
    for sweep in range(1, NS_ITERS):
        base_split = split(base)
        inverse = 2.0 * inverse - dot3(split(inverse), base_split)
        if sweep < NS_ITERS - 1:
            base = 2.0 * base - dot3(base_split, base_split)
    product_turned = dot3(left, split(inverse))
    second_second = identity - 2.0 * dot3(split(product_turned), right)
    first_first = 2.0 * inverse - identity
    first_second = 2.0 * product_turned.T
    second_first = -2.0 * product_turned
    stay_stay = jnp.where(stay_first, first_first, second_second)
    move_move = jnp.where(stay_first, second_second, first_first)
    stay_move = jnp.where(stay_first, first_second, second_first)
    move_stay = jnp.where(stay_first, second_first, first_second)
    top = split(jnp.where(send_is_stay, stay_stay, stay_move))
    end = split(jnp.where(send_is_stay, move_stay, move_move))
    if len(refs) > 2:
        *refs, sent = refs
        copy.wait()
        sent[...] = dot3(split(held[:, :width]), top) + dot3(split(held[:, width:]), end)
    high, low = refs
    for ref, upper, lower in zip((high, low), top, end):
        ref[:width, :width] = upper
        ref[width:, :width] = lower
    if both:
        top = split(jnp.where(send_is_stay, stay_move, stay_stay))
        end = split(jnp.where(send_is_stay, move_move, move_stay))
        for ref, upper, lower in zip((high, low), top, end):
            ref[:width, width:] = upper
            ref[width:, width:] = lower


def rotation(step, side, both, flags, total, norm, note=None, snapshots=(), size=0):
    other = shift(total, "row", 1)
    width = total.shape[1]
    matrix = (2 * width, 2 * width if both else width)
    shapes = [(size, width)] if snapshots else [(width // 2 + 8, width)] if note == "write" else []
    return pl.pallas_call(
        functools.partial(rotation_kernel, step, side, both, note, bool(snapshots)),
        grid=(1,),
        in_specs=[SMEM, whole(total.shape), whole(other.shape), whole(norm.shape)]
        + [pl.BlockSpec(memory_space=pl.ANY)] * len(snapshots),
        out_specs=[whole(matrix)] * 2 + [whole(shape) for shape in shapes],
        out_shape=[jax.ShapeDtypeStruct(matrix, jnp.bfloat16)] * 2
        + [jax.ShapeDtypeStruct(shape, jnp.float32) for shape in shapes],
        scratch_shapes=[pltpu.VMEM((size, 2 * width), jnp.float32), pltpu.SemaphoreType.DMA] if snapshots else [],
        compiler_params=FIRST if snapshots else PARAMS,
        cost_estimate=LONG if note == "read" else COST,
        name="rotation",
    )(flags, total, other, norm, *snapshots)


def apply_both_kernel(first, joined, high, low, *refs):
    if not first:
        before, *refs = refs
    sent, sent_turned, kept, kept_turned, norm = refs
    width = sent.shape[1]
    result = dot3(split(joined[...]), (high[...], low[...]))
    sent[...] = result[:, :width]
    kept[...] = result[:, width:]
    squares = []
    for half, ref in ((result[:, width:], kept_turned), (result[:, :width], sent_turned)):
        turned = half.T
        ref[...] = turned
        squares.append(jnp.broadcast_to(jnp.sum(turned * turned, axis=1, keepdims=True), (width, SIDE)))
    squares = jnp.concatenate(squares, axis=1)
    step = pl.program_id(0)

    @pl.when(step == 0)
    def _():
        norm[...] = squares if first else before[...] + squares

    @pl.when(step > 0)
    def _():
        norm[...] += squares


def apply_both(snapshots, start, high, low, before, blocks):
    width = high.shape[0] // 2
    rows = blocks * BLOCK
    block = (BLOCK, width)
    by_row = pl.BlockSpec(block, lambda i: (i, 0))
    by_column = pl.BlockSpec((width, BLOCK), lambda i: (0, i))
    norm = whole((width, 2 * SIDE))
    piece = jax.ShapeDtypeStruct((rows, width), jnp.float32)
    turned = jax.ShapeDtypeStruct((width, rows), jnp.float32)
    first = before is None
    return pl.pallas_call(
        functools.partial(apply_both_kernel, first),
        grid=(blocks,),
        in_specs=[pl.BlockSpec((BLOCK, 2 * width), lambda i: (start + i, 0)), whole(high.shape), whole(low.shape)]
        + [norm] * (not first),
        out_specs=[by_row, by_column, by_row, by_column, norm],
        out_shape=[piece, turned, piece, turned, jax.ShapeDtypeStruct((width, 2 * SIDE), jnp.float32)],
        compiler_params=FIRST,
        cost_estimate=COST,
        name="apply_both",
    )(snapshots, high, low, *([] if first else [before]))


def rotate(one, two, high, low):
    joined = jnp.concatenate((one[...], two[...]), axis=1)
    return dot3(split(joined), (high[...], low[...]))


def apply_all_kernel(counts, *refs):
    stay, refs = refs[: counts[0]], refs[counts[0] :]
    move, refs = refs[: counts[1]], refs[counts[1] :]
    high, low, sent, sent_turned, kept_turned, norm, *kept = refs
    width = norm.shape[0]
    sums = [0.0, 0.0]
    for index, (one, two, out) in enumerate(zip(parts(stay), parts(move), parts(kept))):
        result = rotate(one, two, high, low)
        rows = pl.ds(index * BLOCK, BLOCK)
        for half, (ref, turned) in enumerate(((out, kept_turned), (sent.at[rows], sent_turned))):
            value = result[:, width:] if half == 0 else result[:, :width]
            ref[...] = value
            turned[:, rows] = value.T
            sums[half] += row_sums(value)
    for half in range(2):
        norm[:, half * SIDE : (half + 1) * SIDE] = column(jnp.sum(sums[half], axis=0, keepdims=True))


def apply_all(stay, move, high, low, sizes):
    width = high.shape[0] // 2
    rows = sum(sizes)
    shapes = [(rows, width), (width, rows), (width, rows), (width, 2 * SIDE)] + [(size, width) for size in sizes]
    vmem = pl.BlockSpec(memory_space=pltpu.VMEM)
    sent, sent_turned, kept_turned, norm, *kept = pl.pallas_call(
        functools.partial(apply_all_kernel, (len(stay), len(move))),
        in_specs=[vmem] * (len(stay) + len(move) + 2),
        out_specs=[vmem] * len(shapes),
        out_shape=[jax.ShapeDtypeStruct(shape, jnp.float32) for shape in shapes],
        compiler_params=LARGE,
        cost_estimate=COST,
        name="apply_all",
    )(*stay, *move, high, low)
    return sent, sent_turned, kept, kept_turned, norm


def rebuild_kernel(counts, *refs):
    sent, refs = refs[: counts[0]], refs[counts[0] :]
    raw, refs = refs[: counts[1]], refs[counts[1] :]
    high, low, turned, came, total = refs
    for index, (one, two) in enumerate(zip(parts(sent), parts(raw))):
        value = rotate(one, two, high, low)
        rows = pl.ds(index * BLOCK, BLOCK)
        came[rows, :] = value
        add_gram(total, turned[:, rows], value, index == 0)


def rebuild(sent, raw, high, low, turned):
    width, rows = turned.shape
    vmem = pl.BlockSpec(memory_space=pltpu.VMEM)
    args = (*sent, *raw, high, low, turned)
    return pl.pallas_call(
        functools.partial(rebuild_kernel, (len(sent), len(raw))),
        in_specs=[vmem] * len(args),
        out_specs=[vmem] * 2,
        out_shape=[
            jax.ShapeDtypeStruct((rows, width), jnp.float32),
            jax.ShapeDtypeStruct((width + 8, width), jnp.float32),
        ],
        compiler_params=LARGE,
        cost_estimate=COST,
        name="rebuild",
    )(*args)


def finish_kernel(counts, kept, aliased, flags, *refs):
    stay, refs = refs[: counts[0]], refs[counts[0] :]
    move, refs = refs[: counts[1]], refs[counts[1] :]
    high, low, *refs = refs
    out, token, held, done = refs[aliased:]
    width = held.shape[2]
    token[...] = jnp.zeros_like(token)
    half = pl.ds(width, width) if kept else pl.ds(0, width)
    column_of = flags[flags.shape[0] - 2, 1 - kept]
    columns = pl.ds(pl.multiple_of(column_of * width, width), width)
    copies = []
    for index, (one, two) in enumerate(zip(parts(stay), parts(move))):
        held[index] = rotate(one, two, high.at[:, half], low.at[:, half])
        copy = pltpu.make_async_copy(held.at[index], out.at[pl.ds(index * BLOCK, BLOCK), columns], done.at[index])
        copy.start()
        copies.append(copy)
    for copy in copies:
        copy.wait()


def put_kernel(start, flags, came, before, out, done):
    width = came.shape[1]
    columns = pl.ds(pl.multiple_of(flags[flags.shape[0] - 2, 1] * width, width), width)
    copies = []
    for index in range(came.shape[0] // PUT):
        rows = pl.ds(index * PUT, PUT)
        copy = pltpu.make_async_copy(came.at[rows], out.at[pl.ds(start + index * PUT, PUT), columns], done.at[index])
        copy.start()
        copies.append(copy)
    for copy in copies:
        copy.wait()


def put(flags, came, before, start):
    vmem = pl.BlockSpec(memory_space=pltpu.VMEM)
    anywhere = pl.BlockSpec(memory_space=pl.ANY)
    return pl.pallas_call(
        functools.partial(put_kernel, start),
        in_specs=[SMEM, vmem, anywhere],
        out_specs=anywhere,
        out_shape=jax.ShapeDtypeStruct(before.shape, jnp.float32),
        input_output_aliases={2: 0},
        scratch_shapes=[pltpu.SemaphoreType.DMA((came.shape[0] // PUT,))],
        compiler_params=PARAMS,
        cost_estimate=COST,
        name="put",
    )(flags, came, before)


def relay_kernel(message, *refs):
    refs[-1][...] = message[...]


def relay(message, after):
    vmem = pl.BlockSpec(memory_space=pltpu.VMEM)
    return pl.pallas_call(
        relay_kernel,
        in_specs=[vmem] + [pl.BlockSpec(memory_space=pl.ANY)] * len(after),
        out_specs=vmem,
        out_shape=jax.ShapeDtypeStruct(message.shape, jnp.float32),
        compiler_params=PARAMS,
        cost_estimate=COST,
        name="relay",
    )(message, *after)


def apply_one_kernel(skip, stay, move, high, low, sent):
    width = sent.shape[1]
    for index, (one, two) in enumerate(zip(parts([stay]), parts([move])[skip:])):
        sent[pl.ds(index * BLOCK, BLOCK), :] = rotate(one, two, high.at[:, pl.ds(0, width)], low.at[:, pl.ds(0, width)])


def apply_one(stay, move, high, low, skip):
    vmem = pl.BlockSpec(memory_space=pltpu.VMEM)
    return pl.pallas_call(
        functools.partial(apply_one_kernel, skip),
        in_specs=[vmem] * 4,
        out_specs=vmem,
        out_shape=jax.ShapeDtypeStruct(stay.shape, jnp.float32),
        compiler_params=PARAMS,
        cost_estimate=COST,
        name="apply_one",
    )(stay, move, high, low)


def finish(kept, flags, stay, move, high, low, before, shape, after=()):
    width = high.shape[0] // 2
    vmem = pl.BlockSpec(memory_space=pltpu.VMEM)
    anywhere = pl.BlockSpec(memory_space=pl.ANY)
    args = (flags, *stay, *move, high, low)
    blocks = shape[0] // BLOCK
    return pl.pallas_call(
        functools.partial(finish_kernel, (len(stay), len(move)), kept, len(before) + len(after)),
        in_specs=[SMEM] + [vmem] * (len(args) - 1) + [anywhere] * (len(before) + len(after)),
        out_specs=[anywhere, vmem],
        out_shape=[jax.ShapeDtypeStruct(shape, jnp.float32), jax.ShapeDtypeStruct((8, SIDE), jnp.float32)],
        input_output_aliases={len(args): 0} if before else {},
        scratch_shapes=[pltpu.VMEM((blocks, BLOCK, width), jnp.float32), pltpu.SemaphoreType.DMA((blocks,))],
        compiler_params=LARGE,
        cost_estimate=COST,
        name="finish",
    )(*args, *before, *after)


def per_device(snapshots, plan):
    rows = snapshots.shape[0]
    rounds = plan.shape[0]
    size = rows // BLOCK // PIECES
    device = lax.axis_index("pair")
    count = lax.axis_size("pair")
    total, norm = first_gram(snapshots)
    flags = make_flags(plan, jnp.stack((device, lax.axis_index("row"))), count)
    norm = norm + shift(norm, "row", 1)
    high, low, outgoing = rotation(0, 0, True, flags, total, norm, None, (snapshots,), size * BLOCK)
    move = [shift(outgoing, "pair", -2)]
    norm = None
    held = [None] * PIECES
    for piece in [*range(1, PIECES), 0]:
        *held[piece], norm = apply_both(snapshots, piece * size, high, low, norm, size)
        if piece:
            move.append(shift(held[piece][0], "pair", -2))
    sent, sent_turned, stay, stay_turned = zip(*held)
    total = ()
    for one, two in zip(stay_turned, move):
        total = (gram((one,), (two,), total),)
    (total,) = total
    for step in range(1, rounds):
        last = step == rounds - 1
        direction = 2 if step % 2 else -2
        raw = [shift(value, "pair", direction) for value in (stay[:-1] if last else stay)]
        norm = norm + shift(norm, "row", 1)
        if last:
            break
        high, low = rotation(step, 0, True, flags, total, norm)
        sizes = [rows // 2, rows // 4, rows // 4] if step == rounds - 2 else [rows // 2] * 2
        new_sent, new_sent_turned, stay, stay_turned, own_norm = apply_all(stay, move, high, low, sizes)
        total = gram(sent_turned, raw, (), (own_norm,))
        high, low = rotation(rounds + step, SIDE, False, flags, total, norm)
        came, total = rebuild(sent, raw, high, low, stay_turned)
        move, norm = (came,), own_norm
        sent, sent_turned = (new_sent,), (new_sent_turned,)
    high, low, message = rotation(step, 0, True, flags, total, norm, note="write")
    message = shift(message, "pair", direction)
    outgoing = apply_one(stay[-1], came, high, low, (rows - stay[-1].shape[0]) // BLOCK)
    last_piece = shift(outgoing, "pair", direction)
    field, token = finish(1, flags, stay, move, high, low, (), snapshots.shape, raw)
    message = relay(message, (outgoing, token))
    high, low = rotation(rounds + step, SIDE, False, flags, message, norm, note="read")
    field, _ = finish(0, flags, raw, sent, high, low, (field,), snapshots.shape)
    return put(flags, last_piece, field, rows - last_piece.shape[0])


def solution(mesh):
    in_specs = (P(("basin", "row"), "pair"), P())
    out_specs = P(("basin", "row"), "pair")
    return jax.shard_map(
        per_device, mesh=mesh, in_specs=in_specs, out_specs=out_specs, check_vma=False
    )
```

```python
import functools

import jax
import jax.numpy as jnp
from jax import lax
from jax.experimental import pallas as pl
from jax.experimental.pallas import tpu as pltpu
from jax.sharding import PartitionSpec as P

NS_ITERS = 6
EPSILON = 1e-06
BLOCK = 256
PIECES = 4
SIDE = 128
PUT = 64
FIRST_MIB = 48
PARAMS = pltpu.CompilerParams(vmem_limit_bytes=12 * 1024 * 1024)
LARGE = pltpu.CompilerParams(vmem_limit_bytes=24 * 1024 * 1024)
FIRST = pltpu.CompilerParams(vmem_limit_bytes=FIRST_MIB * 1024 * 1024)


def shift(value, axis, by):
    size = lax.axis_size(axis)
    return lax.ppermute(value, axis, [(i, (i + by) % size) for i in range(size)])


def split(value):
    high = value.astype(jnp.bfloat16)
    return high, (value - high.astype(jnp.float32)).astype(jnp.bfloat16)


def dot(left, right):
    return jnp.dot(left, right, preferred_element_type=jnp.float32)


def dot3(left, right):
    (left_high, left_low), (right_high, right_low) = left, right
    return dot(left_high, right_high) + dot(left_low, right_high) + dot(left_high, right_low)


def whole(shape):
    return pl.BlockSpec(shape, lambda *_: (0,) * len(shape))


SMEM = pl.BlockSpec(memory_space=pltpu.SMEM)


COST = pl.CostEstimate(flops=1024, bytes_accessed=1024, transcendentals=0)
LONG = pl.CostEstimate(flops=4_000_000_000, bytes_accessed=1024, transcendentals=0)


def eye(size):
    row = lax.broadcasted_iota(jnp.int32, (size, size), 0)
    column = lax.broadcasted_iota(jnp.int32, (size, size), 1)
    return jnp.where(row == column, 1.0, 0.0).astype(jnp.float32)


def route(count, plan, device):
    stay_first = jnp.int32(1)
    flags = []
    for step in range(plan.shape[0]):
        odd = step % 2
        position = lax.rem(device + odd, count)
        upper = lax.rem(position + 1, count)
        second = 2 * position + 1
        second_up = jnp.where((plan[step, 2 * upper] == second) | (plan[step, 2 * upper + 1] == second), 1, 0)
        send_second = second_up if odd else 1 - second_up
        flags.append((stay_first, jnp.where(send_second == stay_first, 0, 1)))
        target = device if odd else upper
        below = lax.rem(target + count - 1, count)
        from_below = jnp.where(plan[step, 2 * target] // 2 == below, 1, 0)
        stay_first = 1 - from_below if odd else from_below
    return flags, stay_first


def flags_kernel(count, plan, device, flags):
    rounds = plan.shape[0]
    own, stay_first = route(count, plan, device[0])
    above, _ = route(count, plan, lax.rem(device[0] + 2, count))
    below, _ = route(count, plan, lax.rem(device[0] + count - 2 % count, count))
    for step in range(rounds):
        flags[step, 0], flags[step, 1] = own[step]
        sender = below[step] if step % 2 else above[step]
        flags[rounds + step, 0] = 1 - sender[0]
        flags[rounds + step, 1] = 1 - sender[1]
    flags[2 * rounds, 0] = 1 - stay_first
    flags[2 * rounds, 1] = stay_first
    flags[2 * rounds + 1, 0] = device[1]
    flags[2 * rounds + 1, 1] = device[1]


def make_flags(plan, device, count):
    return pl.pallas_call(
        functools.partial(flags_kernel, count),
        in_specs=[SMEM, SMEM],
        out_specs=SMEM,
        out_shape=jax.ShapeDtypeStruct((2 * plan.shape[0] + 2, 2), jnp.int32),
        compiler_params=PARAMS,
        cost_estimate=COST,
        name="flags",
    )(plan, device)


def column(row):
    return jnp.broadcast_to(row, (SIDE, row.shape[1])).T


def row_sums(value):
    return jnp.sum((value * value).reshape(-1, 8, value.shape[1]), axis=0)


def first_gram_kernel(snapshots, total, norm, held, done):
    rows, columns = snapshots.shape
    width = columns // 2

    def read(index):
        rows = pl.ds(pl.multiple_of(index * BLOCK, BLOCK), BLOCK)
        return pltpu.make_async_copy(snapshots.at[rows], held.at[index], done.at[index])

    for index in range(rows // BLOCK):
        read(index).start()
    total[...] = jnp.zeros_like(total)

    def step(index, squares):
        read(index).wait()
        kept = held[index, :, :width]
        add_gram(total, kept.T, held[index, :, width:])
        return squares + row_sums(kept)

    squares = lax.fori_loop(0, rows // BLOCK, step, jnp.zeros((8, width), jnp.float32))
    norm[...] = column(jnp.sum(squares, axis=0, keepdims=True))


def first_gram(snapshots):
    rows, columns = snapshots.shape
    width = columns // 2
    vmem = pl.BlockSpec(memory_space=pltpu.VMEM)
    blocks = rows // BLOCK
    return pl.pallas_call(
        first_gram_kernel,
        in_specs=[pl.BlockSpec(memory_space=pl.ANY)],
        out_specs=[vmem, vmem],
        out_shape=[
            jax.ShapeDtypeStruct((width + 8, width), jnp.float32),
            jax.ShapeDtypeStruct((width, SIDE), jnp.float32),
        ],
        scratch_shapes=[pltpu.VMEM((blocks, BLOCK, columns), jnp.float32), pltpu.SemaphoreType.DMA((blocks,))],
        compiler_params=pltpu.CompilerParams(vmem_limit_bytes=52 * 1024 * 1024),
        cost_estimate=COST,
        name="first_gram",
    )(snapshots)


def add_gram(total, turned, value):
    width = value.shape[1]
    total[:width, :] += dot3(split(turned), split(value))
    total[width:, :] += row_sums(value)


def over_blocks(lists, body, carry=None, skip=None):
    skip = skip or [0] * len(lists)
    cuts, ends = [], []
    for pieces, first in zip(lists, skip):
        start, cut = -first, []
        for ref, turned in pieces:
            size = ref.shape[1] if turned else ref.shape[0]
            cut.append((start, start + size, ref, turned))
            start += size
        cuts.append(cut)
        ends.append(start)
    marks = sorted({max(0, edge) for cut in cuts for piece in cut for edge in piece[:2] if edge <= min(ends)})
    for low, high in zip(marks, marks[1:]):
        found = [next(piece for piece in cut if piece[0] <= low < piece[1]) for cut in cuts]

        def step(index, carry):
            views = []
            for start, _, ref, turned in found:
                rows = pl.ds(pl.multiple_of(low - start + index * BLOCK, BLOCK), BLOCK)
                views.append(ref.at[:, rows] if turned else ref.at[rows])
            return body(views, carry)

        carry = lax.fori_loop(0, (high - low) // BLOCK, step, carry)
    return carry


def straight(refs):
    return [(ref, False) for ref in refs]


def transposed(refs):
    return [(ref, True) for ref in refs]


def gram_kernel(counts, offset, *refs):
    turned, refs = refs[: counts[0]], refs[counts[0] :]
    came, refs = refs[: counts[1]], refs[counts[1] :]
    total = refs[-1]
    total[...] = refs[0][...] if counts[2] else jnp.zeros_like(total)

    def body(views, carry):
        add_gram(total, views[0][...], views[1][...])
        return carry

    over_blocks((transposed(turned), straight(came)), body, 0, (offset * BLOCK, 0))


def gram(turned, came, before=(), after=(), offset=0):
    width = came[0].shape[1]
    vmem = pl.BlockSpec(memory_space=pltpu.VMEM)
    args = (*turned, *came, *before)
    return pl.pallas_call(
        functools.partial(gram_kernel, (len(turned), len(came), len(before)), offset),
        in_specs=[vmem] * len(args) + [pl.BlockSpec(memory_space=pl.ANY)] * len(after),
        out_specs=vmem,
        out_shape=jax.ShapeDtypeStruct((width + 8, width), jnp.float32),
        compiler_params=PARAMS,
        cost_estimate=COST,
        name="gram",
    )(*args, *after)


def rotation_kernel(step, side, both, note, piece, flags, mine, other, norm, *refs):
    width = mine.shape[1]
    *refs, base, inverse = refs
    if piece:
        snapshots, *refs, held, done = refs
        copy = pltpu.make_async_copy(snapshots.at[pl.ds(0, held.shape[0])], held, done)
        copy.start()
    first_core = flags[flags.shape[0] - 1, 0] == 0
    if note == "read":
        one, two = mine[: width // 2, :], other[: width // 2, :]
        total = jnp.concatenate((jnp.where(first_core, one, two), jnp.where(first_core, two, one)), axis=0)
        norm_move = mine[width // 2 : width // 2 + 1, :]
        norm_stay = column(mine[width // 2 + 1 : width // 2 + 2, :])[:, :1]
    else:
        total = mine[...] + other[...]
        norm_move = jnp.sum(total[width:, :], axis=0, keepdims=True)
        norm_stay = norm[:, side : side + 1]
        total = total[:width, :]
    if note == "write":
        *refs, message = refs
        message[: width // 2, :] = jnp.where(first_core, total[: width // 2, :], total[width // 2 :, :])
        stay_row = norm[:, side : side + SIDE].T[:1, :]
        index = lax.broadcasted_iota(jnp.int32, (8, width), 0)
        message[width // 2 :, :] = jnp.where(index == 0, norm_move, stay_row)
    coupled = total / (norm_stay + norm_move + EPSILON)
    turned = coupled.T
    stay_first = flags[step, 0] == (0 if note == "read" else 1)
    send_is_stay = flags[step, 1] == (0 if note == "read" else 1)
    coupling = jnp.where(stay_first, coupled, turned)
    coupling_turned = jnp.where(stay_first, turned, coupled)
    identity = eye(width)
    scale = 1.0 / (1.0 + jnp.sum(coupled * coupled))
    left, right = split(coupling_turned), split(coupling)
    base[...] = scale * (identity + dot3(right, left))
    inverse[...] = scale * identity

    def sweep(_, carry):
        pair = split(base[...])
        inverse[...] = 2.0 * inverse[...] - dot3(split(inverse[...]), pair)
        base[...] = 2.0 * base[...] - dot3(pair, pair)
        return carry

    lax.fori_loop(0, NS_ITERS, sweep, 0)
    inverse = inverse[...]
    product_turned = dot3(left, split(inverse))
    second_second = identity - 2.0 * dot3(split(product_turned), right)
    first_first = 2.0 * inverse - identity
    first_second = 2.0 * product_turned.T
    second_first = -2.0 * product_turned
    stay_stay = jnp.where(stay_first, first_first, second_second)
    move_move = jnp.where(stay_first, second_second, first_first)
    stay_move = jnp.where(stay_first, first_second, second_first)
    move_stay = jnp.where(stay_first, second_first, first_second)
    top = split(jnp.where(send_is_stay, stay_stay, stay_move))
    end = split(jnp.where(send_is_stay, move_stay, move_move))
    if len(refs) > 2:
        *refs, sent = refs
        copy.wait()
        sent[...] = dot3(split(held[:, :width]), top) + dot3(split(held[:, width:]), end)
    high, low = refs
    for ref, upper, lower in zip((high, low), top, end):
        ref[:width, :width] = upper
        ref[width:, :width] = lower
    if both:
        top = split(jnp.where(send_is_stay, stay_move, stay_stay))
        end = split(jnp.where(send_is_stay, move_move, move_stay))
        for ref, upper, lower in zip((high, low), top, end):
            ref[:width, width:] = upper
            ref[width:, width:] = lower


def rotation(step, side, both, flags, total, norm, note=None, snapshots=(), size=0):
    other = shift(total, "row", 1)
    width = total.shape[1]
    matrix = (2 * width, 2 * width if both else width)
    shapes = [(size, width)] if snapshots else [(width // 2 + 8, width)] if note == "write" else []
    return pl.pallas_call(
        functools.partial(rotation_kernel, step, side, both, note, bool(snapshots)),
        grid=(1,),
        in_specs=[SMEM, whole(total.shape), whole(other.shape), whole(norm.shape)]
        + [pl.BlockSpec(memory_space=pl.ANY)] * len(snapshots),
        out_specs=[whole(matrix)] * 2 + [whole(shape) for shape in shapes],
        out_shape=[jax.ShapeDtypeStruct(matrix, jnp.bfloat16)] * 2
        + [jax.ShapeDtypeStruct(shape, jnp.float32) for shape in shapes],
        scratch_shapes=([pltpu.VMEM((size, 2 * width), jnp.float32), pltpu.SemaphoreType.DMA] if snapshots else [])
        + [pltpu.VMEM((width, width), jnp.float32)] * 2,
        compiler_params=FIRST if snapshots else PARAMS,
        cost_estimate=LONG if note == "read" else COST,
        name="rotation",
    )(flags, total, other, norm, *snapshots)


def apply_both_kernel(first, joined, high, low, *refs):
    if not first:
        before, *refs = refs
    sent, sent_turned, kept, kept_turned, norm = refs
    width = sent.shape[1]
    result = dot3(split(joined[...]), (high[...], low[...]))
    sent[...] = result[:, :width]
    kept[...] = result[:, width:]
    squares = []
    for half, ref in ((result[:, width:], kept_turned), (result[:, :width], sent_turned)):
        turned = half.T
        ref[...] = turned
        squares.append(jnp.broadcast_to(jnp.sum(turned * turned, axis=1, keepdims=True), (width, SIDE)))
    squares = jnp.concatenate(squares, axis=1)
    step = pl.program_id(0)

    @pl.when(step == 0)
    def _():
        norm[...] = squares if first else before[...] + squares

    @pl.when(step > 0)
    def _():
        norm[...] += squares


def apply_both(snapshots, start, high, low, before, blocks):
    width = high.shape[0] // 2
    rows = blocks * BLOCK
    block = (BLOCK, width)
    by_row = pl.BlockSpec(block, lambda i: (i, 0))
    by_column = pl.BlockSpec((width, BLOCK), lambda i: (0, i))
    norm = whole((width, 2 * SIDE))
    piece = jax.ShapeDtypeStruct((rows, width), jnp.float32)
    turned = jax.ShapeDtypeStruct((width, rows), jnp.float32)
    first = before is None
    return pl.pallas_call(
        functools.partial(apply_both_kernel, first),
        grid=(blocks,),
        in_specs=[pl.BlockSpec((BLOCK, 2 * width), lambda i: (start + i, 0)), whole(high.shape), whole(low.shape)]
        + [norm] * (not first),
        out_specs=[by_row, by_column, by_row, by_column, norm],
        out_shape=[piece, turned, piece, turned, jax.ShapeDtypeStruct((width, 2 * SIDE), jnp.float32)],
        compiler_params=FIRST,
        cost_estimate=COST,
        name="apply_both",
    )(snapshots, high, low, *([] if first else [before]))


def rotate(one, two, high, low):
    joined = jnp.concatenate((one[...], two[...]), axis=1)
    return dot3(split(joined), (high[...], low[...]))


def apply_all_kernel(counts, *refs):
    stay, refs = refs[: counts[0]], refs[counts[0] :]
    move, refs = refs[: counts[1]], refs[counts[1] :]
    high, low, sent, sent_turned, kept_turned, norm, *kept = refs
    width = norm.shape[0]

    def body(views, sums):
        one, two, sent, sent_turned, kept, kept_turned = views
        result = rotate(one, two, high, low)
        new = []
        for start, ref, turned, total in ((width, kept, kept_turned, sums[0]), (0, sent, sent_turned, sums[1])):
            value = result[:, start : start + width]
            ref[...] = value
            turned[...] = value.T
            new.append(total + row_sums(value))
        return tuple(new)

    lists = (
        straight(stay),
        straight(move),
        straight([sent]),
        transposed([sent_turned]),
        straight(kept),
        transposed([kept_turned]),
    )
    sums = over_blocks(lists, body, (jnp.zeros((8, width), jnp.float32),) * 2)
    for half in range(2):
        norm[:, half * SIDE : (half + 1) * SIDE] = column(jnp.sum(sums[half], axis=0, keepdims=True))


def apply_all(stay, move, high, low, sizes):
    width = high.shape[0] // 2
    rows = sum(sizes)
    shapes = [(rows, width), (width, rows), (width, rows), (width, 2 * SIDE)] + [(size, width) for size in sizes]
    vmem = pl.BlockSpec(memory_space=pltpu.VMEM)
    sent, sent_turned, kept_turned, norm, *kept = pl.pallas_call(
        functools.partial(apply_all_kernel, (len(stay), len(move))),
        in_specs=[vmem] * (len(stay) + len(move) + 2),
        out_specs=[vmem] * len(shapes),
        out_shape=[jax.ShapeDtypeStruct(shape, jnp.float32) for shape in shapes],
        compiler_params=LARGE,
        cost_estimate=COST,
        name="apply_all",
    )(*stay, *move, high, low)
    return sent, sent_turned, kept, kept_turned, norm


def rebuild_kernel(counts, *refs):
    sent, refs = refs[: counts[0]], refs[counts[0] :]
    raw, refs = refs[: counts[1]], refs[counts[1] :]
    high, low, turned, came, total = refs
    total[...] = jnp.zeros_like(total)

    def body(views, carry):
        one, two, kept, out = views
        value = rotate(one, two, high, low)
        out[...] = value
        add_gram(total, kept[...], value)
        return carry

    over_blocks((straight(sent), straight(raw), transposed([turned]), straight([came])), body, 0)


def rebuild(sent, raw, high, low, turned):
    width, rows = turned.shape
    vmem = pl.BlockSpec(memory_space=pltpu.VMEM)
    args = (*sent, *raw, high, low, turned)
    return pl.pallas_call(
        functools.partial(rebuild_kernel, (len(sent), len(raw))),
        in_specs=[vmem] * len(args),
        out_specs=[vmem] * 2,
        out_shape=[
            jax.ShapeDtypeStruct((rows, width), jnp.float32),
            jax.ShapeDtypeStruct((width + 8, width), jnp.float32),
        ],
        compiler_params=LARGE,
        cost_estimate=COST,
        name="rebuild",
    )(*args)


def finish_kernel(counts, kept, aliased, flags, *refs):
    stay, refs = refs[: counts[0]], refs[counts[0] :]
    move, refs = refs[: counts[1]], refs[counts[1] :]
    high, low, *refs = refs
    out, token, held, done = refs[aliased:]
    width = held.shape[1]
    token[...] = jnp.zeros_like(token)
    half = pl.ds(width, width) if kept else pl.ds(0, width)
    column_of = flags[flags.shape[0] - 2, 1 - kept]
    columns = pl.ds(pl.multiple_of(column_of * width, width), width)

    def write(index):
        rows = pl.ds(pl.multiple_of(index * BLOCK, BLOCK), BLOCK)
        return pltpu.make_async_copy(held.at[rows], out.at[rows, columns], done.at[index])

    def body(views, index):
        one, two, block = views
        block[...] = rotate(one, two, high.at[:, half], low.at[:, half])
        write(index).start()
        return index + 1

    over_blocks((straight(stay), straight(move), straight([held])), body, 0)
    for index in range(min(sum(ref.shape[0] for ref in pieces) for pieces in (stay, move)) // BLOCK):
        write(index).wait()


def put_kernel(start, flags, came, before, out, done):
    width = came.shape[1]
    columns = pl.ds(pl.multiple_of(flags[flags.shape[0] - 2, 1] * width, width), width)
    copies = []
    for index in range(came.shape[0] // PUT):
        rows = pl.ds(index * PUT, PUT)
        copy = pltpu.make_async_copy(came.at[rows], out.at[pl.ds(start + index * PUT, PUT), columns], done.at[index])
        copy.start()
        copies.append(copy)
    for copy in copies:
        copy.wait()


def put(flags, came, before, start):
    vmem = pl.BlockSpec(memory_space=pltpu.VMEM)
    anywhere = pl.BlockSpec(memory_space=pl.ANY)
    return pl.pallas_call(
        functools.partial(put_kernel, start),
        in_specs=[SMEM, vmem, anywhere],
        out_specs=anywhere,
        out_shape=jax.ShapeDtypeStruct(before.shape, jnp.float32),
        input_output_aliases={2: 0},
        scratch_shapes=[pltpu.SemaphoreType.DMA((came.shape[0] // PUT,))],
        compiler_params=PARAMS,
        cost_estimate=COST,
        name="put",
    )(flags, came, before)


def relay_kernel(message, *refs):
    refs[-1][...] = message[...]


def relay(message, after):
    vmem = pl.BlockSpec(memory_space=pltpu.VMEM)
    return pl.pallas_call(
        relay_kernel,
        in_specs=[vmem] + [pl.BlockSpec(memory_space=pl.ANY)] * len(after),
        out_specs=vmem,
        out_shape=jax.ShapeDtypeStruct(message.shape, jnp.float32),
        compiler_params=PARAMS,
        cost_estimate=COST,
        name="relay",
    )(message, *after)


def apply_one_kernel(skip, stay, move, high, low, sent):
    half = pl.ds(0, sent.shape[1])

    def body(views, carry):
        one, two, out = views
        out[...] = rotate(one, two, high.at[:, half], low.at[:, half])
        return carry

    over_blocks((straight([stay]), straight([move]), straight([sent])), body, 0, (0, skip * BLOCK, 0))


def apply_one(stay, move, high, low, skip):
    vmem = pl.BlockSpec(memory_space=pltpu.VMEM)
    return pl.pallas_call(
        functools.partial(apply_one_kernel, skip),
        in_specs=[vmem] * 4,
        out_specs=vmem,
        out_shape=jax.ShapeDtypeStruct(stay.shape, jnp.float32),
        compiler_params=PARAMS,
        cost_estimate=COST,
        name="apply_one",
    )(stay, move, high, low)


def finish(kept, flags, stay, move, high, low, before, shape, after=()):
    width = high.shape[0] // 2
    vmem = pl.BlockSpec(memory_space=pltpu.VMEM)
    anywhere = pl.BlockSpec(memory_space=pl.ANY)
    args = (flags, *stay, *move, high, low)
    blocks = shape[0] // BLOCK
    return pl.pallas_call(
        functools.partial(finish_kernel, (len(stay), len(move)), kept, len(before) + len(after)),
        in_specs=[SMEM] + [vmem] * (len(args) - 1) + [anywhere] * (len(before) + len(after)),
        out_specs=[anywhere, vmem],
        out_shape=[jax.ShapeDtypeStruct(shape, jnp.float32), jax.ShapeDtypeStruct((8, SIDE), jnp.float32)],
        input_output_aliases={len(args): 0} if before else {},
        scratch_shapes=[pltpu.VMEM((shape[0], width), jnp.float32), pltpu.SemaphoreType.DMA((blocks,))],
        compiler_params=LARGE,
        cost_estimate=COST,
        name="finish",
    )(*args, *before, *after)


def per_device(snapshots, plan):
    rows = snapshots.shape[0]
    rounds = plan.shape[0]
    size = rows // BLOCK // PIECES
    device = lax.axis_index("pair")
    count = lax.axis_size("pair")
    total, norm = first_gram(snapshots)
    flags = make_flags(plan, jnp.stack((device, lax.axis_index("row"))), count)
    norm = norm + shift(norm, "row", 1)
    high, low, outgoing = rotation(0, 0, True, flags, total, norm, None, (snapshots,), size * BLOCK)
    move = [shift(outgoing, "pair", -2)]
    norm = None
    held = [None] * PIECES
    for piece in [*range(1, PIECES), 0]:
        *held[piece], norm = apply_both(snapshots, piece * size, high, low, norm, size)
        if piece:
            move.append(shift(held[piece][0], "pair", -2))
    sent, sent_turned, stay, stay_turned = zip(*held)
    total = ()
    for one, two in zip(stay_turned, move):
        total = (gram((one,), (two,), total),)
    (total,) = total
    for step in range(1, rounds):
        last = step == rounds - 1
        direction = 2 if step % 2 else -2
        raw = [shift(value, "pair", direction) for value in (stay[:-1] if last else stay)]
        norm = norm + shift(norm, "row", 1)
        if last:
            break
        high, low = rotation(step, 0, True, flags, total, norm)
        sizes = [rows // 2, rows // 4, rows // 4] if step == rounds - 2 else [rows // 2] * 2
        new_sent, new_sent_turned, stay, stay_turned, own_norm = apply_all(stay, move, high, low, sizes)
        total = gram(sent_turned, raw, (), (own_norm,))
        high, low = rotation(rounds + step, SIDE, False, flags, total, norm)
        came, total = rebuild(sent, raw, high, low, stay_turned)
        move, norm = (came,), own_norm
        sent, sent_turned = (new_sent,), (new_sent_turned,)
    high, low, message = rotation(step, 0, True, flags, total, norm, note="write")
    message = shift(message, "pair", direction)
    outgoing = apply_one(stay[-1], came, high, low, (rows - stay[-1].shape[0]) // BLOCK)
    last_piece = shift(outgoing, "pair", direction)
    field, token = finish(1, flags, stay, move, high, low, (), snapshots.shape)
    message = relay(message, (outgoing, token, *raw))
    high, low = rotation(rounds + step, SIDE, False, flags, message, norm, note="read")
    field, _ = finish(0, flags, raw, sent, high, low, (field,), snapshots.shape)
    return put(flags, last_piece, field, rows - last_piece.shape[0])


def solution(mesh):
    in_specs = (P(("basin", "row"), "pair"), P())
    out_specs = P(("basin", "row"), "pair")
    return jax.shard_map(
        per_device, mesh=mesh, in_specs=in_specs, out_specs=out_specs, check_vma=False
    )
```

```python
import functools

import jax
import jax.numpy as jnp
from jax import lax
from jax.experimental import pallas as pl
from jax.experimental.pallas import tpu as pltpu
from jax.sharding import PartitionSpec as P

NS_ITERS = 6
EPSILON = 1e-06
BLOCK = 256
PIECES = 4
SIDE = 128
PUT = 64
FIRST_MIB = 48
PARAMS = pltpu.CompilerParams(vmem_limit_bytes=12 * 1024 * 1024)
LARGE = pltpu.CompilerParams(vmem_limit_bytes=24 * 1024 * 1024)
FIRST = pltpu.CompilerParams(vmem_limit_bytes=FIRST_MIB * 1024 * 1024)


def shift(value, axis, by):
    size = lax.axis_size(axis)
    return lax.ppermute(value, axis, [(i, (i + by) % size) for i in range(size)])


def split(value):
    high = value.astype(jnp.bfloat16)
    return high, (value - high.astype(jnp.float32)).astype(jnp.bfloat16)


def dot(left, right):
    return jnp.dot(left, right, preferred_element_type=jnp.float32)


def dot3(left, right):
    (left_high, left_low), (right_high, right_low) = left, right
    return dot(left_high, right_high) + dot(left_low, right_high) + dot(left_high, right_low)


def whole(shape):
    return pl.BlockSpec(shape, lambda *_: (0,) * len(shape))


SMEM = pl.BlockSpec(memory_space=pltpu.SMEM)


COST = pl.CostEstimate(flops=1024, bytes_accessed=1024, transcendentals=0)
LONG = pl.CostEstimate(flops=4_000_000_000, bytes_accessed=1024, transcendentals=0)


def eye(size):
    row = lax.broadcasted_iota(jnp.int32, (size, size), 0)
    column = lax.broadcasted_iota(jnp.int32, (size, size), 1)
    return jnp.where(row == column, 1.0, 0.0).astype(jnp.float32)


def route(count, plan, device):
    stay_first = jnp.int32(1)
    flags = []
    for step in range(plan.shape[0]):
        odd = step % 2
        position = lax.rem(device + odd, count)
        upper = lax.rem(position + 1, count)
        second = 2 * position + 1
        second_up = jnp.where((plan[step, 2 * upper] == second) | (plan[step, 2 * upper + 1] == second), 1, 0)
        send_second = second_up if odd else 1 - second_up
        flags.append((stay_first, jnp.where(send_second == stay_first, 0, 1)))
        target = device if odd else upper
        below = lax.rem(target + count - 1, count)
        from_below = jnp.where(plan[step, 2 * target] // 2 == below, 1, 0)
        stay_first = 1 - from_below if odd else from_below
    return flags, stay_first


def flags_kernel(count, plan, device, flags):
    rounds = plan.shape[0]
    own, stay_first = route(count, plan, device[0])
    above, _ = route(count, plan, lax.rem(device[0] + 2, count))
    below, _ = route(count, plan, lax.rem(device[0] + count - 2 % count, count))
    senders = [(below if step % 2 else above)[step] for step in range(rounds)]
    pairs = own + [(1 - first, 1 - send) for first, send in senders]
    pairs += [(1 - stay_first, stay_first), (device[1], device[1])]
    for index, pair in enumerate(pairs):
        for half in range(2):
            row = jnp.broadcast_to(pair[half], (1, flags.shape[1])).astype(jnp.float32)
            flags[2 * index + half : 2 * index + half + 1, :] = row


def make_flags(plan, device, count, width):
    return pl.pallas_call(
        functools.partial(flags_kernel, count),
        in_specs=[SMEM, SMEM],
        out_specs=pl.BlockSpec(memory_space=pltpu.VMEM),
        out_shape=jax.ShapeDtypeStruct((4 * plan.shape[0] + 4, width), jnp.float32),
        compiler_params=PARAMS,
        cost_estimate=COST,
        name="flags",
    )(plan, device)


def flag(flags, index):
    index = index % flags.shape[0]
    return flags[index : index + 1, :] == 1.0


def output_half(flags, kept):
    row = flags.shape[0] - (4 if kept else 3)
    return jnp.max(flags[row : row + 1, :]).astype(jnp.int32)


def column(row):
    return jnp.broadcast_to(row, (SIDE, row.shape[1])).T


def row_sums(value):
    return jnp.sum((value * value).reshape(-1, 8, value.shape[1]), axis=0)


def first_gram_kernel(snapshots, total, held, done):
    rows, columns = snapshots.shape
    width = columns // 2

    def read(index):
        rows = pl.ds(pl.multiple_of(index * BLOCK, BLOCK), BLOCK)
        return pltpu.make_async_copy(snapshots.at[rows], held.at[index], done.at[index])

    for index in range(rows // BLOCK):
        read(index).start()
    total[...] = jnp.zeros_like(total)

    def step(index, squares):
        read(index).wait()
        kept = held[index, :, :width]
        add_gram(total, kept.T, held[index, :, width:])
        return squares + row_sums(kept)

    total[width + 8 :, :] = lax.fori_loop(0, rows // BLOCK, step, jnp.zeros((8, width), jnp.float32))


def first_gram(snapshots):
    rows, columns = snapshots.shape
    width = columns // 2
    vmem = pl.BlockSpec(memory_space=pltpu.VMEM)
    blocks = rows // BLOCK
    return pl.pallas_call(
        first_gram_kernel,
        in_specs=[pl.BlockSpec(memory_space=pl.ANY)],
        out_specs=vmem,
        out_shape=jax.ShapeDtypeStruct((width + 16, width), jnp.float32),
        scratch_shapes=[pltpu.VMEM((blocks, BLOCK, columns), jnp.float32), pltpu.SemaphoreType.DMA((blocks,))],
        compiler_params=pltpu.CompilerParams(vmem_limit_bytes=52 * 1024 * 1024),
        cost_estimate=COST,
        name="first_gram",
    )(snapshots)


def add_gram(total, turned, value):
    width = value.shape[1]
    total[:width, :] += dot3(split(turned), split(value))
    total[width : width + 8, :] += row_sums(value)


def over_blocks(lists, body, carry=None, skip=None):
    skip = skip or [0] * len(lists)
    cuts, ends = [], []
    for pieces, first in zip(lists, skip):
        start, cut = -first, []
        for ref, turned in pieces:
            size = ref.shape[1] if turned else ref.shape[0]
            cut.append((start, start + size, ref, turned))
            start += size
        cuts.append(cut)
        ends.append(start)
    marks = sorted({max(0, edge) for cut in cuts for piece in cut for edge in piece[:2] if edge <= min(ends)})
    for low, high in zip(marks, marks[1:]):
        found = [next(piece for piece in cut if piece[0] <= low < piece[1]) for cut in cuts]

        def step(index, carry):
            views = []
            for start, _, ref, turned in found:
                rows = pl.ds(pl.multiple_of(low - start + index * BLOCK, BLOCK), BLOCK)
                views.append(ref.at[:, rows] if turned else ref.at[rows])
            return body(views, carry)

        carry = lax.fori_loop(0, (high - low) // BLOCK, step, carry)
    return carry


def straight(refs):
    return [(ref, False) for ref in refs]


def transposed(refs):
    return [(ref, True) for ref in refs]


def gram_kernel(counts, offset, *refs):
    turned, refs = refs[: counts[0]], refs[counts[0] :]
    came, refs = refs[: counts[1]], refs[counts[1] :]
    total = refs[-1]
    total[...] = refs[0][...] if counts[2] else jnp.zeros_like(total)

    def body(views, carry):
        add_gram(total, views[0][...], views[1][...])
        return carry

    over_blocks((transposed(turned), straight(came)), body, 0, (offset * BLOCK, 0))


def gram(turned, came, before=(), after=(), offset=0):
    width = came[0].shape[1]
    vmem = pl.BlockSpec(memory_space=pltpu.VMEM)
    args = (*turned, *came, *before)
    return pl.pallas_call(
        functools.partial(gram_kernel, (len(turned), len(came), len(before)), offset),
        in_specs=[vmem] * len(args) + [pl.BlockSpec(memory_space=pl.ANY)] * len(after),
        out_specs=vmem,
        out_shape=jax.ShapeDtypeStruct((width + 8, width), jnp.float32),
        compiler_params=PARAMS,
        cost_estimate=COST,
        name="gram",
    )(*args, *after)


def rotation_kernel(step, side, both, note, piece, flags, mine, other, *refs):
    width = mine.shape[1]
    *refs, base, inverse = refs
    if step:
        norm, *refs = refs
    if piece:
        snapshots, *refs, held, done = refs
        copy = pltpu.make_async_copy(snapshots.at[pl.ds(0, held.shape[0])], held, done)
        copy.start()
    second_core = flag(flags, -1)
    if note == "read":
        one, two = mine[: width // 2, :], other[: width // 2, :]
        total = jnp.concatenate((jnp.where(second_core, two, one), jnp.where(second_core, one, two)), axis=0)
        norm_move = mine[width // 2 : width // 2 + 1, :]
        norm_stay = column(mine[width // 2 + 1 : width // 2 + 2, :])[:, :1]
    else:
        total = mine[...] + other[...]
        norm_move = jnp.sum(total[width : width + 8, :], axis=0, keepdims=True)
        if step:
            norm_stay = norm[:, side : side + 1]
        else:
            norm_stay = column(jnp.sum(total[width + 8 :, :], axis=0, keepdims=True))[:, :1]
        total = total[:width, :]
    if note == "write":
        *refs, message = refs
        message[: width // 2, :] = jnp.where(second_core, total[width // 2 :, :], total[: width // 2, :])
        stay_row = norm[:, side : side + SIDE].T[:1, :]
        index = lax.broadcasted_iota(jnp.int32, (8, width), 0)
        message[width // 2 :, :] = jnp.where(index == 0, norm_move, stay_row)
    coupled = total / (norm_stay + norm_move + EPSILON)
    turned = coupled.T
    stay_first = flag(flags, 2 * step)
    send_is_stay = flag(flags, 2 * step + 1)
    if note == "read":
        stay_first, send_is_stay = ~stay_first, ~send_is_stay
    coupling = jnp.where(stay_first, coupled, turned)
    coupling_turned = jnp.where(stay_first, turned, coupled)
    identity = eye(width)
    scale = 1.0 / (1.0 + jnp.sum(coupled * coupled))
    left, right = split(coupling_turned), split(coupling)
    base[...] = scale * (identity + dot3(right, left))
    inverse[...] = scale * identity

    def sweep(_, carry):
        pair = split(base[...])
        inverse[...] = 2.0 * inverse[...] - dot3(split(inverse[...]), pair)
        base[...] = 2.0 * base[...] - dot3(pair, pair)
        return carry

    lax.fori_loop(0, NS_ITERS, sweep, 0)
    inverse = inverse[...]
    product_turned = dot3(left, split(inverse))
    second_second = identity - 2.0 * dot3(split(product_turned), right)
    first_first = 2.0 * inverse - identity
    first_second = 2.0 * product_turned.T
    second_first = -2.0 * product_turned
    stay_stay = jnp.where(stay_first, first_first, second_second)
    move_move = jnp.where(stay_first, second_second, first_first)
    stay_move = jnp.where(stay_first, first_second, second_first)
    move_stay = jnp.where(stay_first, second_first, first_second)
    top = split(jnp.where(send_is_stay, stay_stay, stay_move))
    end = split(jnp.where(send_is_stay, move_stay, move_move))
    if len(refs) > 2:
        *refs, sent = refs
        copy.wait()
        sent[...] = dot3(split(held[:, :width]), top) + dot3(split(held[:, width:]), end)
    high, low = refs
    for ref, upper, lower in zip((high, low), top, end):
        ref[:width, :width] = upper
        ref[width:, :width] = lower
    if both:
        top = split(jnp.where(send_is_stay, stay_move, stay_stay))
        end = split(jnp.where(send_is_stay, move_move, move_stay))
        for ref, upper, lower in zip((high, low), top, end):
            ref[:width, width:] = upper
            ref[width:, width:] = lower


def rotation(step, side, both, flags, total, norm, note=None, snapshots=(), size=0):
    other = shift(total, "row", 1)
    width = total.shape[1]
    matrix = (2 * width, 2 * width if both else width)
    shapes = [(size, width)] if snapshots else [(width // 2 + 8, width)] if note == "write" else []
    return pl.pallas_call(
        functools.partial(rotation_kernel, step, side, both, note, bool(snapshots)),
        grid=(1,),
        in_specs=[whole(value.shape) for value in (flags, total, other, *norm)]
        + [pl.BlockSpec(memory_space=pl.ANY)] * len(snapshots),
        out_specs=[whole(matrix)] * 2 + [whole(shape) for shape in shapes],
        out_shape=[jax.ShapeDtypeStruct(matrix, jnp.bfloat16)] * 2
        + [jax.ShapeDtypeStruct(shape, jnp.float32) for shape in shapes],
        scratch_shapes=([pltpu.VMEM((size, 2 * width), jnp.float32), pltpu.SemaphoreType.DMA] if snapshots else [])
        + [pltpu.VMEM((width, width), jnp.float32)] * 2,
        compiler_params=FIRST if snapshots else PARAMS,
        cost_estimate=LONG if note == "read" else COST,
        name="rotation",
    )(flags, total, other, *norm, *snapshots)


def apply_both_kernel(first, joined, high, low, *refs):
    if not first:
        before, *refs = refs
    sent, sent_turned, kept, kept_turned, norm = refs
    width = sent.shape[1]
    result = dot3(split(joined[...]), (high[...], low[...]))
    sent[...] = result[:, :width]
    kept[...] = result[:, width:]
    squares = []
    for half, ref in ((result[:, width:], kept_turned), (result[:, :width], sent_turned)):
        turned = half.T
        ref[...] = turned
        squares.append(jnp.broadcast_to(jnp.sum(turned * turned, axis=1, keepdims=True), (width, SIDE)))
    squares = jnp.concatenate(squares, axis=1)
    step = pl.program_id(0)

    @pl.when(step == 0)
    def _():
        norm[...] = squares if first else before[...] + squares

    @pl.when(step > 0)
    def _():
        norm[...] += squares


def apply_both(snapshots, start, high, low, before, blocks):
    width = high.shape[0] // 2
    rows = blocks * BLOCK
    block = (BLOCK, width)
    by_row = pl.BlockSpec(block, lambda i: (i, 0))
    by_column = pl.BlockSpec((width, BLOCK), lambda i: (0, i))
    norm = whole((width, 2 * SIDE))
    piece = jax.ShapeDtypeStruct((rows, width), jnp.float32)
    turned = jax.ShapeDtypeStruct((width, rows), jnp.float32)
    first = before is None
    return pl.pallas_call(
        functools.partial(apply_both_kernel, first),
        grid=(blocks,),
        in_specs=[pl.BlockSpec((BLOCK, 2 * width), lambda i: (start + i, 0)), whole(high.shape), whole(low.shape)]
        + [norm] * (not first),
        out_specs=[by_row, by_column, by_row, by_column, norm],
        out_shape=[piece, turned, piece, turned, jax.ShapeDtypeStruct((width, 2 * SIDE), jnp.float32)],
        compiler_params=FIRST,
        cost_estimate=COST,
        name="apply_both",
    )(snapshots, high, low, *([] if first else [before]))


def rotate(one, two, high, low):
    joined = jnp.concatenate((one[...], two[...]), axis=1)
    return dot3(split(joined), (high[...], low[...]))


def apply_all_kernel(counts, *refs):
    stay, refs = refs[: counts[0]], refs[counts[0] :]
    move, refs = refs[: counts[1]], refs[counts[1] :]
    high, low, sent, sent_turned, kept_turned, norm, *kept = refs
    width = norm.shape[0]

    def body(views, sums):
        one, two, sent, sent_turned, kept, kept_turned = views
        result = rotate(one, two, high, low)
        new = []
        for start, ref, turned, total in ((width, kept, kept_turned, sums[0]), (0, sent, sent_turned, sums[1])):
            value = result[:, start : start + width]
            ref[...] = value
            turned[...] = value.T
            new.append(total + row_sums(value))
        return tuple(new)

    lists = (
        straight(stay),
        straight(move),
        straight([sent]),
        transposed([sent_turned]),
        straight(kept),
        transposed([kept_turned]),
    )
    sums = over_blocks(lists, body, (jnp.zeros((8, width), jnp.float32),) * 2)
    for half in range(2):
        norm[:, half * SIDE : (half + 1) * SIDE] = column(jnp.sum(sums[half], axis=0, keepdims=True))


def apply_all(stay, move, high, low, sizes):
    width = high.shape[0] // 2
    rows = sum(sizes)
    shapes = [(rows, width), (width, rows), (width, rows), (width, 2 * SIDE)] + [(size, width) for size in sizes]
    vmem = pl.BlockSpec(memory_space=pltpu.VMEM)
    sent, sent_turned, kept_turned, norm, *kept = pl.pallas_call(
        functools.partial(apply_all_kernel, (len(stay), len(move))),
        in_specs=[vmem] * (len(stay) + len(move) + 2),
        out_specs=[vmem] * len(shapes),
        out_shape=[jax.ShapeDtypeStruct(shape, jnp.float32) for shape in shapes],
        compiler_params=LARGE,
        cost_estimate=COST,
        name="apply_all",
    )(*stay, *move, high, low)
    return sent, sent_turned, kept, kept_turned, norm


def rebuild_kernel(counts, *refs):
    sent, refs = refs[: counts[0]], refs[counts[0] :]
    raw, refs = refs[: counts[1]], refs[counts[1] :]
    high, low, turned, came, total = refs
    total[...] = jnp.zeros_like(total)

    def body(views, carry):
        one, two, kept, out = views
        value = rotate(one, two, high, low)
        out[...] = value
        add_gram(total, kept[...], value)
        return carry

    over_blocks((straight(sent), straight(raw), transposed([turned]), straight([came])), body, 0)


def rebuild(sent, raw, high, low, turned):
    width, rows = turned.shape
    vmem = pl.BlockSpec(memory_space=pltpu.VMEM)
    args = (*sent, *raw, high, low, turned)
    return pl.pallas_call(
        functools.partial(rebuild_kernel, (len(sent), len(raw))),
        in_specs=[vmem] * len(args),
        out_specs=[vmem] * 2,
        out_shape=[
            jax.ShapeDtypeStruct((rows, width), jnp.float32),
            jax.ShapeDtypeStruct((width + 8, width), jnp.float32),
        ],
        compiler_params=LARGE,
        cost_estimate=COST,
        name="rebuild",
    )(*args)


def finish_kernel(counts, kept, aliased, flags, *refs):
    stay, refs = refs[: counts[0]], refs[counts[0] :]
    move, refs = refs[: counts[1]], refs[counts[1] :]
    high, low, *refs = refs
    out, token, held, done = refs[aliased:]
    width = held.shape[1]
    token[...] = jnp.zeros_like(token)
    half = pl.ds(width, width) if kept else pl.ds(0, width)
    columns = pl.ds(pl.multiple_of(output_half(flags, kept) * width, width), width)

    def write(index):
        rows = pl.ds(pl.multiple_of(index * BLOCK, BLOCK), BLOCK)
        return pltpu.make_async_copy(held.at[rows], out.at[rows, columns], done.at[index])

    def body(views, index):
        one, two, block = views
        block[...] = rotate(one, two, high.at[:, half], low.at[:, half])
        write(index).start()
        return index + 1

    over_blocks((straight(stay), straight(move), straight([held])), body, 0)
    for index in range(min(sum(ref.shape[0] for ref in pieces) for pieces in (stay, move)) // BLOCK):
        write(index).wait()


def put_kernel(start, flags, came, before, out, done):
    width = came.shape[1]
    columns = pl.ds(pl.multiple_of(output_half(flags, False) * width, width), width)
    copies = []
    for index in range(came.shape[0] // PUT):
        rows = pl.ds(index * PUT, PUT)
        copy = pltpu.make_async_copy(came.at[rows], out.at[pl.ds(start + index * PUT, PUT), columns], done.at[index])
        copy.start()
        copies.append(copy)
    for copy in copies:
        copy.wait()


def put(flags, came, before, start):
    vmem = pl.BlockSpec(memory_space=pltpu.VMEM)
    anywhere = pl.BlockSpec(memory_space=pl.ANY)
    return pl.pallas_call(
        functools.partial(put_kernel, start),
        in_specs=[vmem, vmem, anywhere],
        out_specs=anywhere,
        out_shape=jax.ShapeDtypeStruct(before.shape, jnp.float32),
        input_output_aliases={2: 0},
        scratch_shapes=[pltpu.SemaphoreType.DMA((came.shape[0] // PUT,))],
        compiler_params=PARAMS,
        cost_estimate=COST,
        name="put",
    )(flags, came, before)


def relay_kernel(message, *refs):
    refs[-1][...] = message[...]


def relay(message, after):
    vmem = pl.BlockSpec(memory_space=pltpu.VMEM)
    return pl.pallas_call(
        relay_kernel,
        in_specs=[vmem] + [pl.BlockSpec(memory_space=pl.ANY)] * len(after),
        out_specs=vmem,
        out_shape=jax.ShapeDtypeStruct(message.shape, jnp.float32),
        compiler_params=PARAMS,
        cost_estimate=COST,
        name="relay",
    )(message, *after)


def apply_one_kernel(skip, stay, move, high, low, sent):
    half = pl.ds(0, sent.shape[1])

    def body(views, carry):
        one, two, out = views
        out[...] = rotate(one, two, high.at[:, half], low.at[:, half])
        return carry

    over_blocks((straight([stay]), straight([move]), straight([sent])), body, 0, (0, skip * BLOCK, 0))


def apply_one(stay, move, high, low, skip):
    vmem = pl.BlockSpec(memory_space=pltpu.VMEM)
    return pl.pallas_call(
        functools.partial(apply_one_kernel, skip),
        in_specs=[vmem] * 4,
        out_specs=vmem,
        out_shape=jax.ShapeDtypeStruct(stay.shape, jnp.float32),
        compiler_params=PARAMS,
        cost_estimate=COST,
        name="apply_one",
    )(stay, move, high, low)


def finish(kept, flags, stay, move, high, low, before, shape, after=()):
    width = high.shape[0] // 2
    vmem = pl.BlockSpec(memory_space=pltpu.VMEM)
    anywhere = pl.BlockSpec(memory_space=pl.ANY)
    args = (flags, *stay, *move, high, low)
    blocks = shape[0] // BLOCK
    return pl.pallas_call(
        functools.partial(finish_kernel, (len(stay), len(move)), kept, len(before) + len(after)),
        in_specs=[vmem] * len(args) + [anywhere] * (len(before) + len(after)),
        out_specs=[anywhere, vmem],
        out_shape=[jax.ShapeDtypeStruct(shape, jnp.float32), jax.ShapeDtypeStruct((8, SIDE), jnp.float32)],
        input_output_aliases={len(args): 0} if before else {},
        scratch_shapes=[pltpu.VMEM((shape[0], width), jnp.float32), pltpu.SemaphoreType.DMA((blocks,))],
        compiler_params=LARGE,
        cost_estimate=COST,
        name="finish",
    )(*args, *before, *after)


def per_device(snapshots, plan):
    rows = snapshots.shape[0]
    rounds = plan.shape[0]
    size = rows // BLOCK // PIECES
    device = lax.axis_index("pair")
    count = lax.axis_size("pair")
    total = first_gram(snapshots)
    flags = make_flags(plan, jnp.stack((device, lax.axis_index("row"))), count, snapshots.shape[1] // 2)
    high, low, outgoing = rotation(0, 0, True, flags, total, (), None, (snapshots,), size * BLOCK)
    move = [shift(outgoing, "pair", -2)]
    norm = None
    held = [None] * PIECES
    for piece in [*range(1, PIECES), 0]:
        *held[piece], norm = apply_both(snapshots, piece * size, high, low, norm, size)
        if piece:
            move.append(shift(held[piece][0], "pair", -2))
    sent, sent_turned, stay, stay_turned = zip(*held)
    total = ()
    for one, two in zip(stay_turned, move):
        total = (gram((one,), (two,), total),)
    (total,) = total
    for step in range(1, rounds):
        last = step == rounds - 1
        direction = 2 if step % 2 else -2
        raw = [shift(value, "pair", direction) for value in (stay[:-1] if last else stay)]
        norm = norm + shift(norm, "row", 1)
        if last:
            break
        high, low = rotation(step, 0, True, flags, total, (norm,))
        sizes = [rows // 2, rows // 4, rows // 4] if step == rounds - 2 else [rows // 2] * 2
        new_sent, new_sent_turned, stay, stay_turned, own_norm = apply_all(stay, move, high, low, sizes)
        total = gram(sent_turned, raw, (), (own_norm,))
        high, low = rotation(rounds + step, SIDE, False, flags, total, (norm,))
        came, total = rebuild(sent, raw, high, low, stay_turned)
        move, norm = (came,), own_norm
        sent, sent_turned = (new_sent,), (new_sent_turned,)
    high, low, message = rotation(step, 0, True, flags, total, (norm,), note="write")
    message = shift(message, "pair", direction)
    outgoing = apply_one(stay[-1], came, high, low, (rows - stay[-1].shape[0]) // BLOCK)
    last_piece = shift(outgoing, "pair", direction)
    field, token = finish(1, flags, stay, move, high, low, (), snapshots.shape)
    message = relay(message, (outgoing, token, *raw))
    high, low = rotation(rounds + step, SIDE, False, flags, message, (norm,), note="read")
    field, _ = finish(0, flags, raw, sent, high, low, (field,), snapshots.shape)
    return put(flags, last_piece, field, rows - last_piece.shape[0])


def solution(mesh):
    in_specs = (P(("basin", "row"), "pair"), P())
    out_specs = P(("basin", "row"), "pair")
    return jax.shard_map(
        per_device, mesh=mesh, in_specs=in_specs, out_specs=out_specs, check_vma=False
    )
```

```python
import functools

import jax
import jax.numpy as jnp
from jax import lax
from jax.experimental import pallas as pl
from jax.experimental.pallas import tpu as pltpu
from jax.sharding import PartitionSpec as P

NS_ITERS = 6
EPSILON = 1e-06
BLOCK = 256
PIECES = 4
SIDE = 128
PUT = 64
GROUP = 4
FIRST_MIB = 48
PARAMS = pltpu.CompilerParams(vmem_limit_bytes=12 * 1024 * 1024)
LARGE = pltpu.CompilerParams(vmem_limit_bytes=24 * 1024 * 1024)
FIRST = pltpu.CompilerParams(vmem_limit_bytes=FIRST_MIB * 1024 * 1024)


def shift(value, axis, by):
    size = lax.axis_size(axis)
    return lax.ppermute(value, axis, [(i, (i + by) % size) for i in range(size)])


def split(value):
    high = value.astype(jnp.bfloat16)
    return high, (value - high.astype(jnp.float32)).astype(jnp.bfloat16)


def dot(left, right):
    return jnp.dot(left, right, preferred_element_type=jnp.float32)


def dot3(left, right):
    (left_high, left_low), (right_high, right_low) = left, right
    return dot(left_high, right_high) + dot(left_low, right_high) + dot(left_high, right_low)


def whole(shape):
    return pl.BlockSpec(shape, lambda *_: (0,) * len(shape))


SMEM = pl.BlockSpec(memory_space=pltpu.SMEM)


COST = pl.CostEstimate(flops=1024, bytes_accessed=1024, transcendentals=0)
LONG = pl.CostEstimate(flops=4_000_000_000, bytes_accessed=1024, transcendentals=0)


def eye(size):
    row = lax.broadcasted_iota(jnp.int32, (size, size), 0)
    column = lax.broadcasted_iota(jnp.int32, (size, size), 1)
    return jnp.where(row == column, 1.0, 0.0).astype(jnp.float32)


def route(count, plan, device):
    stay_first = jnp.int32(1)
    flags = []
    for step in range(plan.shape[0]):
        odd = step % 2
        position = lax.rem(device + odd, count)
        upper = lax.rem(position + 1, count)
        second = 2 * position + 1
        second_up = jnp.where((plan[step, 2 * upper] == second) | (plan[step, 2 * upper + 1] == second), 1, 0)
        send_second = second_up if odd else 1 - second_up
        flags.append((stay_first, jnp.where(send_second == stay_first, 0, 1)))
        target = device if odd else upper
        below = lax.rem(target + count - 1, count)
        from_below = jnp.where(plan[step, 2 * target] // 2 == below, 1, 0)
        stay_first = 1 - from_below if odd else from_below
    return flags, stay_first


def flags_kernel(count, plan, device, flags):
    rounds = plan.shape[0]
    own, stay_first = route(count, plan, device[0])
    above, _ = route(count, plan, lax.rem(device[0] + 2, count))
    below, _ = route(count, plan, lax.rem(device[0] + count - 2 % count, count))
    senders = [(below if step % 2 else above)[step] for step in range(rounds)]
    pairs = own + [(1 - first, 1 - send) for first, send in senders]
    pairs += [(1 - stay_first, stay_first), (device[1], device[1])]
    for index, pair in enumerate(pairs):
        for half in range(2):
            row = jnp.broadcast_to(pair[half], (1, flags.shape[1])).astype(jnp.float32)
            flags[2 * index + half : 2 * index + half + 1, :] = row


def make_flags(plan, device, count, width):
    return pl.pallas_call(
        functools.partial(flags_kernel, count),
        in_specs=[SMEM, SMEM],
        out_specs=pl.BlockSpec(memory_space=pltpu.VMEM),
        out_shape=jax.ShapeDtypeStruct((4 * plan.shape[0] + 4, width), jnp.float32),
        compiler_params=PARAMS,
        cost_estimate=COST,
        name="flags",
    )(plan, device)


def flag(flags, index):
    index = index % flags.shape[0]
    return flags[index : index + 1, :] == 1.0


def output_half(flags, kept):
    row = flags.shape[0] - (4 if kept else 3)
    return jnp.max(flags[row : row + 1, :]).astype(jnp.int32)


def column(row):
    return jnp.broadcast_to(row, (SIDE, row.shape[1])).T


def row_sums(value):
    return jnp.sum((value * value).reshape(-1, 8, value.shape[1]), axis=0)


def first_gram_kernel(snapshots, total, held, done):
    rows, columns = snapshots.shape
    width = columns // 2

    def read(index):
        rows = pl.ds(pl.multiple_of(index * BLOCK, BLOCK), BLOCK)
        return pltpu.make_async_copy(snapshots.at[rows], held.at[rows], done.at[index])

    for index in range(rows // BLOCK):
        read(index).start()
    total[...] = jnp.zeros_like(total)

    def step(index, squares):
        for part in range(GROUP):
            read(index * GROUP + part).wait()
        here = pl.ds(pl.multiple_of(index * GROUP * BLOCK, BLOCK), GROUP * BLOCK)
        kept = held[here, :width]
        add_gram(total, kept.T, held[here, width:])
        return squares + row_sums(kept)

    total[width + 8 :, :] = lax.fori_loop(0, rows // (GROUP * BLOCK), step, jnp.zeros((8, width), jnp.float32))


def first_gram(snapshots):
    rows, columns = snapshots.shape
    width = columns // 2
    vmem = pl.BlockSpec(memory_space=pltpu.VMEM)
    blocks = rows // BLOCK
    return pl.pallas_call(
        first_gram_kernel,
        in_specs=[pl.BlockSpec(memory_space=pl.ANY)],
        out_specs=vmem,
        out_shape=jax.ShapeDtypeStruct((width + 16, width), jnp.float32),
        scratch_shapes=[pltpu.VMEM((rows, columns), jnp.float32), pltpu.SemaphoreType.DMA((blocks,))],
        compiler_params=pltpu.CompilerParams(vmem_limit_bytes=52 * 1024 * 1024),
        cost_estimate=COST,
        name="first_gram",
    )(snapshots)


def add_gram(total, turned, value):
    width = value.shape[1]
    total[:width, :] += dot3(split(turned), split(value))
    total[width : width + 8, :] += row_sums(value)


def over_blocks(lists, body, carry=None, skip=None):
    skip = skip or [0] * len(lists)
    cuts, ends = [], []
    for pieces, first in zip(lists, skip):
        start, cut = -first, []
        for ref, turned in pieces:
            size = ref.shape[1] if turned else ref.shape[0]
            cut.append((start, start + size, ref, turned))
            start += size
        cuts.append(cut)
        ends.append(start)
    marks = sorted({max(0, edge) for cut in cuts for piece in cut for edge in piece[:2] if edge <= min(ends)})
    for low, high in zip(marks, marks[1:]):
        found = [next(piece for piece in cut if piece[0] <= low < piece[1]) for cut in cuts]

        def step(index, carry):
            views = []
            for start, _, ref, turned in found:
                rows = pl.ds(pl.multiple_of(low - start + index * BLOCK, BLOCK), BLOCK)
                views.append(ref.at[:, rows] if turned else ref.at[rows])
            return body(views, carry)

        carry = lax.fori_loop(0, (high - low) // BLOCK, step, carry)
    return carry


def straight(refs):
    return [(ref, False) for ref in refs]


def transposed(refs):
    return [(ref, True) for ref in refs]


def gram_kernel(counts, offset, *refs):
    turned, refs = refs[: counts[0]], refs[counts[0] :]
    came, refs = refs[: counts[1]], refs[counts[1] :]
    total = refs[-1]
    total[...] = refs[0][...] if counts[2] else jnp.zeros_like(total)

    def body(views, carry):
        add_gram(total, views[0][...], views[1][...])
        return carry

    over_blocks((transposed(turned), straight(came)), body, 0, (offset * BLOCK, 0))


def gram(turned, came, before=(), after=(), offset=0):
    width = came[0].shape[1]
    vmem = pl.BlockSpec(memory_space=pltpu.VMEM)
    args = (*turned, *came, *before)
    return pl.pallas_call(
        functools.partial(gram_kernel, (len(turned), len(came), len(before)), offset),
        in_specs=[vmem] * len(args) + [pl.BlockSpec(memory_space=pl.ANY)] * len(after),
        out_specs=vmem,
        out_shape=jax.ShapeDtypeStruct((width + 8, width), jnp.float32),
        compiler_params=PARAMS,
        cost_estimate=COST,
        name="gram",
    )(*args, *after)


def rotation_kernel(step, side, both, note, piece, flags, mine, other, *refs):
    width = mine.shape[1]
    *refs, base, product = refs
    if step:
        norm, *refs = refs
    if piece:
        snapshots, *refs, held, done = refs
        copy = pltpu.make_async_copy(snapshots.at[pl.ds(0, held.shape[0])], held, done)
        copy.start()
    second_core = flag(flags, -1)
    if note == "read":
        one, two = mine[: width // 2, :], other[: width // 2, :]
        total = jnp.concatenate((jnp.where(second_core, two, one), jnp.where(second_core, one, two)), axis=0)
        norm_move = mine[width // 2 : width // 2 + 1, :]
        norm_stay = column(mine[width // 2 + 1 : width // 2 + 2, :])[:, :1]
    else:
        total = mine[...] + other[...]
        norm_move = jnp.sum(total[width : width + 8, :], axis=0, keepdims=True)
        if step:
            norm_stay = norm[:, side : side + 1]
        else:
            norm_stay = column(jnp.sum(total[width + 8 :, :], axis=0, keepdims=True))[:, :1]
        total = total[:width, :]
    if note == "write":
        *refs, message = refs
        message[: width // 2, :] = jnp.where(second_core, total[width // 2 :, :], total[: width // 2, :])
        stay_row = norm[:, side : side + SIDE].T[:1, :]
        index = lax.broadcasted_iota(jnp.int32, (8, width), 0)
        message[width // 2 :, :] = jnp.where(index == 0, norm_move, stay_row)
    coupled = total / (norm_stay + norm_move + EPSILON)
    turned = coupled.T
    stay_first = flag(flags, 2 * step)
    send_is_stay = flag(flags, 2 * step + 1)
    if note == "read":
        stay_first, send_is_stay = ~stay_first, ~send_is_stay
    coupling = jnp.where(stay_first, coupled, turned)
    coupling_turned = jnp.where(stay_first, turned, coupled)
    identity = eye(width)
    scale = 1.0 / (1.0 + jnp.sum(coupled * coupled))
    left, right = split(coupling_turned), split(coupling)
    base[...] = scale * (identity + dot3(right, left))
    product[...] = scale * coupling_turned

    def sweep(_, carry):
        pair = split(base[...])
        product[...] = 2.0 * product[...] - dot3(split(product[...]), pair)
        base[...] = 2.0 * base[...] - dot3(pair, pair)
        return carry

    lax.fori_loop(0, NS_ITERS, sweep, 0)
    product_turned = product[...]
    pair = split(product_turned)
    second_second = identity - 2.0 * dot3(pair, right)
    first_first = 2.0 * (base[...] - dot3(right, pair)) - identity
    first_second = 2.0 * product_turned.T
    second_first = -2.0 * product_turned
    stay_stay = jnp.where(stay_first, first_first, second_second)
    move_move = jnp.where(stay_first, second_second, first_first)
    stay_move = jnp.where(stay_first, first_second, second_first)
    move_stay = jnp.where(stay_first, second_first, first_second)
    top = split(jnp.where(send_is_stay, stay_stay, stay_move))
    end = split(jnp.where(send_is_stay, move_stay, move_move))
    if len(refs) > 2:
        *refs, sent = refs
        copy.wait()
        sent[...] = dot3(split(held[:, :width]), top) + dot3(split(held[:, width:]), end)
    high, low = refs
    for ref, upper, lower in zip((high, low), top, end):
        ref[:width, :width] = upper
        ref[width:, :width] = lower
    if both:
        top = split(jnp.where(send_is_stay, stay_move, stay_stay))
        end = split(jnp.where(send_is_stay, move_move, move_stay))
        for ref, upper, lower in zip((high, low), top, end):
            ref[:width, width:] = upper
            ref[width:, width:] = lower


def rotation(step, side, both, flags, total, norm, note=None, snapshots=(), size=0):
    other = shift(total, "row", 1)
    width = total.shape[1]
    matrix = (2 * width, 2 * width if both else width)
    shapes = [(size, width)] if snapshots else [(width // 2 + 8, width)] if note == "write" else []
    return pl.pallas_call(
        functools.partial(rotation_kernel, step, side, both, note, bool(snapshots)),
        grid=(1,),
        in_specs=[whole(value.shape) for value in (flags, total, other, *norm)]
        + [pl.BlockSpec(memory_space=pl.ANY)] * len(snapshots),
        out_specs=[whole(matrix)] * 2 + [whole(shape) for shape in shapes],
        out_shape=[jax.ShapeDtypeStruct(matrix, jnp.bfloat16)] * 2
        + [jax.ShapeDtypeStruct(shape, jnp.float32) for shape in shapes],
        scratch_shapes=([pltpu.VMEM((size, 2 * width), jnp.float32), pltpu.SemaphoreType.DMA] if snapshots else [])
        + [pltpu.VMEM((width, width), jnp.float32)] * 2,
        compiler_params=FIRST if snapshots else PARAMS,
        cost_estimate=LONG if note == "read" else COST,
        name="rotation",
    )(flags, total, other, *norm, *snapshots)


def apply_both_kernel(first, joined, high, low, *refs):
    if not first:
        before, *refs = refs
    sent, sent_turned, kept, kept_turned, norm = refs
    width = sent.shape[1]
    result = dot3(split(joined[...]), (high[...], low[...]))
    sent[...] = result[:, :width]
    kept[...] = result[:, width:]
    squares = []
    for half, ref in ((result[:, width:], kept_turned), (result[:, :width], sent_turned)):
        turned = half.T
        ref[...] = turned
        squares.append(jnp.broadcast_to(jnp.sum(turned * turned, axis=1, keepdims=True), (width, SIDE)))
    squares = jnp.concatenate(squares, axis=1)
    step = pl.program_id(0)

    @pl.when(step == 0)
    def _():
        norm[...] = squares if first else before[...] + squares

    @pl.when(step > 0)
    def _():
        norm[...] += squares


def apply_both(snapshots, start, high, low, before, blocks):
    width = high.shape[0] // 2
    rows = blocks * BLOCK
    block = (BLOCK, width)
    by_row = pl.BlockSpec(block, lambda i: (i, 0))
    by_column = pl.BlockSpec((width, BLOCK), lambda i: (0, i))
    norm = whole((width, 2 * SIDE))
    piece = jax.ShapeDtypeStruct((rows, width), jnp.float32)
    turned = jax.ShapeDtypeStruct((width, rows), jnp.float32)
    first = before is None
    return pl.pallas_call(
        functools.partial(apply_both_kernel, first),
        grid=(blocks,),
        in_specs=[pl.BlockSpec((BLOCK, 2 * width), lambda i: (start + i, 0)), whole(high.shape), whole(low.shape)]
        + [norm] * (not first),
        out_specs=[by_row, by_column, by_row, by_column, norm],
        out_shape=[piece, turned, piece, turned, jax.ShapeDtypeStruct((width, 2 * SIDE), jnp.float32)],
        compiler_params=FIRST,
        cost_estimate=COST,
        name="apply_both",
    )(snapshots, high, low, *([] if first else [before]))


def rotate(one, two, high, low):
    joined = jnp.concatenate((one[...], two[...]), axis=1)
    return dot3(split(joined), (high[...], low[...]))


def apply_all_kernel(counts, *refs):
    stay, refs = refs[: counts[0]], refs[counts[0] :]
    move, refs = refs[: counts[1]], refs[counts[1] :]
    high, low, sent, sent_turned, kept_turned, norm, *kept = refs
    width = norm.shape[0]

    def body(views, sums):
        one, two, sent, sent_turned, kept, kept_turned = views
        result = rotate(one, two, high, low)
        new = []
        for start, ref, turned, total in ((width, kept, kept_turned, sums[0]), (0, sent, sent_turned, sums[1])):
            value = result[:, start : start + width]
            ref[...] = value
            turned[...] = value.T
            new.append(total + row_sums(value))
        return tuple(new)

    lists = (
        straight(stay),
        straight(move),
        straight([sent]),
        transposed([sent_turned]),
        straight(kept),
        transposed([kept_turned]),
    )
    sums = over_blocks(lists, body, (jnp.zeros((8, width), jnp.float32),) * 2)
    for half in range(2):
        norm[:, half * SIDE : (half + 1) * SIDE] = column(jnp.sum(sums[half], axis=0, keepdims=True))


def apply_all(stay, move, high, low, sizes):
    width = high.shape[0] // 2
    rows = sum(sizes)
    shapes = [(rows, width), (width, rows), (width, rows), (width, 2 * SIDE)] + [(size, width) for size in sizes]
    vmem = pl.BlockSpec(memory_space=pltpu.VMEM)
    sent, sent_turned, kept_turned, norm, *kept = pl.pallas_call(
        functools.partial(apply_all_kernel, (len(stay), len(move))),
        in_specs=[vmem] * (len(stay) + len(move) + 2),
        out_specs=[vmem] * len(shapes),
        out_shape=[jax.ShapeDtypeStruct(shape, jnp.float32) for shape in shapes],
        compiler_params=LARGE,
        cost_estimate=COST,
        name="apply_all",
    )(*stay, *move, high, low)
    return sent, sent_turned, kept, kept_turned, norm


def rebuild_kernel(counts, *refs):
    sent, refs = refs[: counts[0]], refs[counts[0] :]
    raw, refs = refs[: counts[1]], refs[counts[1] :]
    high, low, turned, came, total = refs
    total[...] = jnp.zeros_like(total)

    def body(views, carry):
        one, two, kept, out = views
        value = rotate(one, two, high, low)
        out[...] = value
        add_gram(total, kept[...], value)
        return carry

    over_blocks((straight(sent), straight(raw), transposed([turned]), straight([came])), body, 0)


def rebuild(sent, raw, high, low, turned):
    width, rows = turned.shape
    vmem = pl.BlockSpec(memory_space=pltpu.VMEM)
    args = (*sent, *raw, high, low, turned)
    return pl.pallas_call(
        functools.partial(rebuild_kernel, (len(sent), len(raw))),
        in_specs=[vmem] * len(args),
        out_specs=[vmem] * 2,
        out_shape=[
            jax.ShapeDtypeStruct((rows, width), jnp.float32),
            jax.ShapeDtypeStruct((width + 8, width), jnp.float32),
        ],
        compiler_params=LARGE,
        cost_estimate=COST,
        name="rebuild",
    )(*args)


def finish_kernel(counts, kept, aliased, flags, *refs):
    stay, refs = refs[: counts[0]], refs[counts[0] :]
    move, refs = refs[: counts[1]], refs[counts[1] :]
    high, low, *refs = refs
    out, token, held, done = refs[aliased:]
    width = held.shape[1]
    token[...] = jnp.zeros_like(token)
    half = pl.ds(width, width) if kept else pl.ds(0, width)
    columns = pl.ds(pl.multiple_of(output_half(flags, kept) * width, width), width)

    def write(index):
        rows = pl.ds(pl.multiple_of(index * BLOCK, BLOCK), BLOCK)
        return pltpu.make_async_copy(held.at[rows], out.at[rows, columns], done.at[index])

    def body(views, index):
        one, two, block = views
        block[...] = rotate(one, two, high.at[:, half], low.at[:, half])
        write(index).start()
        return index + 1

    over_blocks((straight(stay), straight(move), straight([held])), body, 0)
    for index in range(min(sum(ref.shape[0] for ref in pieces) for pieces in (stay, move)) // BLOCK):
        write(index).wait()


def put_kernel(start, flags, came, before, out, done):
    width = came.shape[1]
    columns = pl.ds(pl.multiple_of(output_half(flags, False) * width, width), width)
    copies = []
    for index in range(came.shape[0] // PUT):
        rows = pl.ds(index * PUT, PUT)
        copy = pltpu.make_async_copy(came.at[rows], out.at[pl.ds(start + index * PUT, PUT), columns], done.at[index])
        copy.start()
        copies.append(copy)
    for copy in copies:
        copy.wait()


def put(flags, came, before, start):
    vmem = pl.BlockSpec(memory_space=pltpu.VMEM)
    anywhere = pl.BlockSpec(memory_space=pl.ANY)
    return pl.pallas_call(
        functools.partial(put_kernel, start),
        in_specs=[vmem, vmem, anywhere],
        out_specs=anywhere,
        out_shape=jax.ShapeDtypeStruct(before.shape, jnp.float32),
        input_output_aliases={2: 0},
        scratch_shapes=[pltpu.SemaphoreType.DMA((came.shape[0] // PUT,))],
        compiler_params=PARAMS,
        cost_estimate=COST,
        name="put",
    )(flags, came, before)


def relay_kernel(message, *refs):
    refs[-1][...] = message[...]


def relay(message, after):
    vmem = pl.BlockSpec(memory_space=pltpu.VMEM)
    return pl.pallas_call(
        relay_kernel,
        in_specs=[vmem] + [pl.BlockSpec(memory_space=pl.ANY)] * len(after),
        out_specs=vmem,
        out_shape=jax.ShapeDtypeStruct(message.shape, jnp.float32),
        compiler_params=PARAMS,
        cost_estimate=COST,
        name="relay",
    )(message, *after)


def apply_one_kernel(skip, stay, move, high, low, sent):
    half = pl.ds(0, sent.shape[1])

    def body(views, carry):
        one, two, out = views
        out[...] = rotate(one, two, high.at[:, half], low.at[:, half])
        return carry

    over_blocks((straight([stay]), straight([move]), straight([sent])), body, 0, (0, skip * BLOCK, 0))


def apply_one(stay, move, high, low, skip):
    vmem = pl.BlockSpec(memory_space=pltpu.VMEM)
    return pl.pallas_call(
        functools.partial(apply_one_kernel, skip),
        in_specs=[vmem] * 4,
        out_specs=vmem,
        out_shape=jax.ShapeDtypeStruct(stay.shape, jnp.float32),
        compiler_params=PARAMS,
        cost_estimate=COST,
        name="apply_one",
    )(stay, move, high, low)


def finish(kept, flags, stay, move, high, low, before, shape, after=()):
    width = high.shape[0] // 2
    vmem = pl.BlockSpec(memory_space=pltpu.VMEM)
    anywhere = pl.BlockSpec(memory_space=pl.ANY)
    args = (flags, *stay, *move, high, low)
    blocks = shape[0] // BLOCK
    return pl.pallas_call(
        functools.partial(finish_kernel, (len(stay), len(move)), kept, len(before) + len(after)),
        in_specs=[vmem] * len(args) + [anywhere] * (len(before) + len(after)),
        out_specs=[anywhere, vmem],
        out_shape=[jax.ShapeDtypeStruct(shape, jnp.float32), jax.ShapeDtypeStruct((8, SIDE), jnp.float32)],
        input_output_aliases={len(args): 0} if before else {},
        scratch_shapes=[pltpu.VMEM((shape[0], width), jnp.float32), pltpu.SemaphoreType.DMA((blocks,))],
        compiler_params=LARGE,
        cost_estimate=COST,
        name="finish",
    )(*args, *before, *after)


def per_device(snapshots, plan):
    rows = snapshots.shape[0]
    rounds = plan.shape[0]
    size = rows // BLOCK // PIECES
    device = lax.axis_index("pair")
    count = lax.axis_size("pair")
    total = first_gram(snapshots)
    flags = make_flags(plan, jnp.stack((device, lax.axis_index("row"))), count, snapshots.shape[1] // 2)
    high, low, outgoing = rotation(0, 0, True, flags, total, (), None, (snapshots,), size * BLOCK)
    move = [shift(outgoing, "pair", -2)]
    norm = None
    held = [None] * PIECES
    for piece in [*range(1, PIECES), 0]:
        *held[piece], norm = apply_both(snapshots, piece * size, high, low, norm, size)
        if piece:
            move.append(shift(held[piece][0], "pair", -2))
    sent, sent_turned, stay, stay_turned = zip(*held)
    total = ()
    for one, two in zip(stay_turned, move):
        total = (gram((one,), (two,), total),)
    (total,) = total
    for step in range(1, rounds):
        last = step == rounds - 1
        direction = 2 if step % 2 else -2
        raw = [shift(value, "pair", direction) for value in (stay[:-1] if last else stay)]
        norm = norm + shift(norm, "row", 1)
        if last:
            break
        high, low = rotation(step, 0, True, flags, total, (norm,))
        sizes = [rows // 2, rows // 4, rows // 4] if step == rounds - 2 else [rows // 2] * 2
        new_sent, new_sent_turned, stay, stay_turned, own_norm = apply_all(stay, move, high, low, sizes)
        total = gram(sent_turned, raw, (), (own_norm,))
        high, low = rotation(rounds + step, SIDE, False, flags, total, (norm,))
        came, total = rebuild(sent, raw, high, low, stay_turned)
        move, norm = (came,), own_norm
        sent, sent_turned = (new_sent,), (new_sent_turned,)
    high, low, message = rotation(step, 0, True, flags, total, (norm,), note="write")
    message = shift(message, "pair", direction)
    outgoing = apply_one(stay[-1], came, high, low, (rows - stay[-1].shape[0]) // BLOCK)
    last_piece = shift(outgoing, "pair", direction)
    field, token = finish(1, flags, stay, move, high, low, (), snapshots.shape)
    message = relay(message, (outgoing, token, *raw))
    high, low = rotation(rounds + step, SIDE, False, flags, message, (norm,), note="read")
    field, _ = finish(0, flags, raw, sent, high, low, (field,), snapshots.shape)
    return put(flags, last_piece, field, rows - last_piece.shape[0])


def solution(mesh):
    in_specs = (P(("basin", "row"), "pair"), P())
    out_specs = P(("basin", "row"), "pair")
    return jax.shard_map(
        per_device, mesh=mesh, in_specs=in_specs, out_specs=out_specs, check_vma=False
    )
```

```python
import functools

import jax
import jax.numpy as jnp
from jax import lax
from jax.experimental import pallas as pl
from jax.experimental.pallas import tpu as pltpu
from jax.sharding import PartitionSpec as P

NS_ITERS = 6
EPSILON = 1e-06
BLOCK = 256
PIECES = 4
SIDE = 128
PUT = 512
GROUP = 4
FIRST_MIB = 48
PARAMS = pltpu.CompilerParams(vmem_limit_bytes=12 * 1024 * 1024)
LARGE = pltpu.CompilerParams(vmem_limit_bytes=24 * 1024 * 1024)
FIRST = pltpu.CompilerParams(vmem_limit_bytes=FIRST_MIB * 1024 * 1024)


def shift(value, axis, by):
    size = lax.axis_size(axis)
    return lax.ppermute(value, axis, [(i, (i + by) % size) for i in range(size)])


def split(value):
    high = value.astype(jnp.bfloat16)
    return high, (value - high.astype(jnp.float32)).astype(jnp.bfloat16)


def dot(left, right):
    return jnp.dot(left, right, preferred_element_type=jnp.float32)


def dot3(left, right):
    (left_high, left_low), (right_high, right_low) = left, right
    return dot(left_high, right_high) + dot(left_low, right_high) + dot(left_high, right_low)


def whole(shape):
    return pl.BlockSpec(shape, lambda *_: (0,) * len(shape))


SMEM = pl.BlockSpec(memory_space=pltpu.SMEM)


COST = pl.CostEstimate(flops=1024, bytes_accessed=1024, transcendentals=0)
LONG = pl.CostEstimate(flops=4_000_000_000, bytes_accessed=1024, transcendentals=0)


def eye(size):
    row = lax.broadcasted_iota(jnp.int32, (size, size), 0)
    column = lax.broadcasted_iota(jnp.int32, (size, size), 1)
    return jnp.where(row == column, 1.0, 0.0).astype(jnp.float32)


def route(count, plan, device):
    stay_first = jnp.int32(1)
    flags = []
    for step in range(plan.shape[0]):
        odd = step % 2
        position = lax.rem(device + odd, count)
        upper = lax.rem(position + 1, count)
        second = 2 * position + 1
        second_up = jnp.where((plan[step, 2 * upper] == second) | (plan[step, 2 * upper + 1] == second), 1, 0)
        send_second = second_up if odd else 1 - second_up
        flags.append((stay_first, jnp.where(send_second == stay_first, 0, 1)))
        target = device if odd else upper
        below = lax.rem(target + count - 1, count)
        from_below = jnp.where(plan[step, 2 * target] // 2 == below, 1, 0)
        stay_first = 1 - from_below if odd else from_below
    return flags, stay_first


def flags_kernel(count, plan, device, flags):
    rounds = plan.shape[0]
    own, stay_first = route(count, plan, device[0])
    above, _ = route(count, plan, lax.rem(device[0] + 2, count))
    below, _ = route(count, plan, lax.rem(device[0] + count - 2 % count, count))
    senders = [(below if step % 2 else above)[step] for step in range(rounds)]
    pairs = own + [(1 - first, 1 - send) for first, send in senders]
    pairs += [(1 - stay_first, stay_first), (device[1], device[1])]
    for index, pair in enumerate(pairs):
        for half in range(2):
            row = jnp.broadcast_to(pair[half], (1, flags.shape[1])).astype(jnp.float32)
            flags[2 * index + half : 2 * index + half + 1, :] = row


def make_flags(plan, device, count, width):
    return pl.pallas_call(
        functools.partial(flags_kernel, count),
        in_specs=[SMEM, SMEM],
        out_specs=pl.BlockSpec(memory_space=pltpu.VMEM),
        out_shape=jax.ShapeDtypeStruct((4 * plan.shape[0] + 4, width), jnp.float32),
        compiler_params=PARAMS,
        cost_estimate=COST,
        name="flags",
    )(plan, device)


def flag(flags, index):
    index = index % flags.shape[0]
    return flags[index : index + 1, :] == 1.0


def output_half(flags, kept):
    row = flags.shape[0] - (4 if kept else 3)
    return jnp.max(flags[row : row + 1, :]).astype(jnp.int32)


def column(row):
    return jnp.broadcast_to(row, (SIDE, row.shape[1])).T


def row_sums(value):
    return jnp.sum((value * value).reshape(-1, 8, value.shape[1]), axis=0)


def first_gram_kernel(snapshots, total, held, done):
    rows, columns = snapshots.shape
    width = columns // 2

    def read(index):
        rows = pl.ds(pl.multiple_of(index * BLOCK, BLOCK), BLOCK)
        return pltpu.make_async_copy(snapshots.at[rows], held.at[rows], done.at[index])

    for index in range(rows // BLOCK):
        read(index).start()
    total[...] = jnp.zeros_like(total)

    def step(index, squares):
        for part in range(GROUP):
            read(index * GROUP + part).wait()
        here = pl.ds(pl.multiple_of(index * GROUP * BLOCK, BLOCK), GROUP * BLOCK)
        kept = held[here, :width]
        add_gram(total, kept.T, held[here, width:])
        return squares + row_sums(kept)

    total[width + 8 :, :] = lax.fori_loop(0, rows // (GROUP * BLOCK), step, jnp.zeros((8, width), jnp.float32))


def first_gram(snapshots):
    rows, columns = snapshots.shape
    width = columns // 2
    vmem = pl.BlockSpec(memory_space=pltpu.VMEM)
    blocks = rows // BLOCK
    return pl.pallas_call(
        first_gram_kernel,
        in_specs=[pl.BlockSpec(memory_space=pl.ANY)],
        out_specs=vmem,
        out_shape=jax.ShapeDtypeStruct((width + 16, width), jnp.float32),
        scratch_shapes=[pltpu.VMEM((rows, columns), jnp.float32), pltpu.SemaphoreType.DMA((blocks,))],
        compiler_params=pltpu.CompilerParams(vmem_limit_bytes=52 * 1024 * 1024),
        cost_estimate=COST,
        name="first_gram",
    )(snapshots)


def add_gram(total, turned, value):
    width = value.shape[1]
    total[:width, :] += dot3(split(turned), split(value))
    total[width : width + 8, :] += row_sums(value)


def over_blocks(lists, body, carry=None, skip=None):
    skip = skip or [0] * len(lists)
    cuts, ends = [], []
    for pieces, first in zip(lists, skip):
        start, cut = -first, []
        for ref, turned in pieces:
            size = ref.shape[1] if turned else ref.shape[0]
            cut.append((start, start + size, ref, turned))
            start += size
        cuts.append(cut)
        ends.append(start)
    marks = sorted({max(0, edge) for cut in cuts for piece in cut for edge in piece[:2] if edge <= min(ends)})
    for low, high in zip(marks, marks[1:]):
        found = [next(piece for piece in cut if piece[0] <= low < piece[1]) for cut in cuts]

        def step(index, carry):
            views = []
            for start, _, ref, turned in found:
                rows = pl.ds(pl.multiple_of(low - start + index * BLOCK, BLOCK), BLOCK)
                views.append(ref.at[:, rows] if turned else ref.at[rows])
            return body(views, carry)

        carry = lax.fori_loop(0, (high - low) // BLOCK, step, carry)
    return carry


def straight(refs):
    return [(ref, False) for ref in refs]


def transposed(refs):
    return [(ref, True) for ref in refs]


def gram_kernel(counts, offset, *refs):
    turned, refs = refs[: counts[0]], refs[counts[0] :]
    came, refs = refs[: counts[1]], refs[counts[1] :]
    total = refs[-1]
    total[...] = refs[0][...] if counts[2] else jnp.zeros_like(total)

    def body(views, carry):
        add_gram(total, views[0][...], views[1][...])
        return carry

    over_blocks((transposed(turned), straight(came)), body, 0, (offset * BLOCK, 0))


def gram(turned, came, before=(), after=(), offset=0):
    width = came[0].shape[1]
    vmem = pl.BlockSpec(memory_space=pltpu.VMEM)
    args = (*turned, *came, *before)
    return pl.pallas_call(
        functools.partial(gram_kernel, (len(turned), len(came), len(before)), offset),
        in_specs=[vmem] * len(args) + [pl.BlockSpec(memory_space=pl.ANY)] * len(after),
        out_specs=vmem,
        out_shape=jax.ShapeDtypeStruct((width + 8, width), jnp.float32),
        compiler_params=PARAMS,
        cost_estimate=COST,
        name="gram",
    )(*args, *after)


def rotation_kernel(step, side, both, note, piece, flags, mine, other, *refs):
    width = mine.shape[1]
    *refs, base, product = refs
    if step:
        norm, *refs = refs
    if piece:
        snapshots, *refs, held, done = refs
        copy = pltpu.make_async_copy(snapshots.at[pl.ds(0, held.shape[0])], held, done)
        copy.start()
    second_core = flag(flags, -1)
    if note == "read":
        one, two = mine[: width // 2, :], other[: width // 2, :]
        total = jnp.concatenate((jnp.where(second_core, two, one), jnp.where(second_core, one, two)), axis=0)
        norm_move = mine[width // 2 : width // 2 + 1, :]
        norm_stay = column(mine[width // 2 + 1 : width // 2 + 2, :])[:, :1]
    else:
        total = mine[...] + other[...]
        norm_move = jnp.sum(total[width : width + 8, :], axis=0, keepdims=True)
        if step:
            norm_stay = norm[:, side : side + 1]
        else:
            norm_stay = column(jnp.sum(total[width + 8 :, :], axis=0, keepdims=True))[:, :1]
        total = total[:width, :]
    if note == "write":
        *refs, message = refs
        message[: width // 2, :] = jnp.where(second_core, total[width // 2 :, :], total[: width // 2, :])
        stay_row = norm[:, side : side + SIDE].T[:1, :]
        index = lax.broadcasted_iota(jnp.int32, (8, width), 0)
        message[width // 2 :, :] = jnp.where(index == 0, norm_move, stay_row)
    coupled = total / (norm_stay + norm_move + EPSILON)
    turned = coupled.T
    stay_first = flag(flags, 2 * step)
    send_is_stay = flag(flags, 2 * step + 1)
    if note == "read":
        stay_first, send_is_stay = ~stay_first, ~send_is_stay
    coupling = jnp.where(stay_first, coupled, turned)
    coupling_turned = jnp.where(stay_first, turned, coupled)
    identity = eye(width)
    scale = 1.0 / (1.0 + jnp.sum(coupled * coupled))
    left, right = split(coupling_turned), split(coupling)
    base[...] = scale * (identity + dot3(right, left))
    product[...] = scale * coupling_turned

    def sweep(_, carry):
        pair = split(base[...])
        product[...] = 2.0 * product[...] - dot3(split(product[...]), pair)
        base[...] = 2.0 * base[...] - dot3(pair, pair)
        return carry

    lax.fori_loop(0, NS_ITERS, sweep, 0)
    product_turned = product[...]
    pair = split(product_turned)
    second_second = identity - 2.0 * dot3(pair, right)
    first_first = 2.0 * (base[...] - dot3(right, pair)) - identity
    first_second = 2.0 * product_turned.T
    second_first = -2.0 * product_turned
    stay_stay = jnp.where(stay_first, first_first, second_second)
    move_move = jnp.where(stay_first, second_second, first_first)
    stay_move = jnp.where(stay_first, first_second, second_first)
    move_stay = jnp.where(stay_first, second_first, first_second)
    top = split(jnp.where(send_is_stay, stay_stay, stay_move))
    end = split(jnp.where(send_is_stay, move_stay, move_move))
    if len(refs) > 2:
        *refs, sent = refs
        copy.wait()
        sent[...] = dot3(split(held[:, :width]), top) + dot3(split(held[:, width:]), end)
    high, low = refs
    for ref, upper, lower in zip((high, low), top, end):
        ref[:width, :width] = upper
        ref[width:, :width] = lower
    if both:
        top = split(jnp.where(send_is_stay, stay_move, stay_stay))
        end = split(jnp.where(send_is_stay, move_move, move_stay))
        for ref, upper, lower in zip((high, low), top, end):
            ref[:width, width:] = upper
            ref[width:, width:] = lower


def rotation(step, side, both, flags, total, norm, note=None, snapshots=(), size=0):
    other = shift(total, "row", 1)
    width = total.shape[1]
    matrix = (2 * width, 2 * width if both else width)
    shapes = [(size, width)] if snapshots else [(width // 2 + 8, width)] if note == "write" else []
    return pl.pallas_call(
        functools.partial(rotation_kernel, step, side, both, note, bool(snapshots)),
        grid=(1,),
        in_specs=[whole(value.shape) for value in (flags, total, other, *norm)]
        + [pl.BlockSpec(memory_space=pl.ANY)] * len(snapshots),
        out_specs=[whole(matrix)] * 2 + [whole(shape) for shape in shapes],
        out_shape=[jax.ShapeDtypeStruct(matrix, jnp.bfloat16)] * 2
        + [jax.ShapeDtypeStruct(shape, jnp.float32) for shape in shapes],
        scratch_shapes=([pltpu.VMEM((size, 2 * width), jnp.float32), pltpu.SemaphoreType.DMA] if snapshots else [])
        + [pltpu.VMEM((width, width), jnp.float32)] * 2,
        compiler_params=FIRST if snapshots else PARAMS,
        cost_estimate=LONG if note == "read" else COST,
        name="rotation",
    )(flags, total, other, *norm, *snapshots)


def apply_both_kernel(first, joined, high, low, *refs):
    if not first:
        before, *refs = refs
    sent, sent_turned, kept, kept_turned, norm = refs
    width = sent.shape[1]
    result = dot3(split(joined[...]), (high[...], low[...]))
    sent[...] = result[:, :width]
    kept[...] = result[:, width:]
    squares = []
    for half, ref in ((result[:, width:], kept_turned), (result[:, :width], sent_turned)):
        turned = half.T
        ref[...] = turned
        squares.append(jnp.broadcast_to(jnp.sum(turned * turned, axis=1, keepdims=True), (width, SIDE)))
    squares = jnp.concatenate(squares, axis=1)
    step = pl.program_id(0)

    @pl.when(step == 0)
    def _():
        norm[...] = squares if first else before[...] + squares

    @pl.when(step > 0)
    def _():
        norm[...] += squares


def apply_both(snapshots, start, high, low, before, blocks):
    width = high.shape[0] // 2
    rows = blocks * BLOCK
    block = (BLOCK, width)
    by_row = pl.BlockSpec(block, lambda i: (i, 0))
    by_column = pl.BlockSpec((width, BLOCK), lambda i: (0, i))
    norm = whole((width, 2 * SIDE))
    piece = jax.ShapeDtypeStruct((rows, width), jnp.float32)
    turned = jax.ShapeDtypeStruct((width, rows), jnp.float32)
    first = before is None
    return pl.pallas_call(
        functools.partial(apply_both_kernel, first),
        grid=(blocks,),
        in_specs=[pl.BlockSpec((BLOCK, 2 * width), lambda i: (start + i, 0)), whole(high.shape), whole(low.shape)]
        + [norm] * (not first),
        out_specs=[by_row, by_column, by_row, by_column, norm],
        out_shape=[piece, turned, piece, turned, jax.ShapeDtypeStruct((width, 2 * SIDE), jnp.float32)],
        compiler_params=FIRST,
        cost_estimate=COST,
        name="apply_both",
    )(snapshots, high, low, *([] if first else [before]))


def rotate(one, two, high, low):
    joined = jnp.concatenate((one[...], two[...]), axis=1)
    return dot3(split(joined), (high[...], low[...]))


def apply_all_kernel(counts, *refs):
    stay, refs = refs[: counts[0]], refs[counts[0] :]
    move, refs = refs[: counts[1]], refs[counts[1] :]
    high, low, sent, sent_turned, kept_turned, norm, *kept = refs
    width = norm.shape[0]

    def body(views, sums):
        one, two, sent, sent_turned, kept, kept_turned = views
        result = rotate(one, two, high, low)
        new = []
        for start, ref, turned, total in ((width, kept, kept_turned, sums[0]), (0, sent, sent_turned, sums[1])):
            value = result[:, start : start + width]
            ref[...] = value
            turned[...] = value.T
            new.append(total + row_sums(value))
        return tuple(new)

    lists = (
        straight(stay),
        straight(move),
        straight([sent]),
        transposed([sent_turned]),
        straight(kept),
        transposed([kept_turned]),
    )
    sums = over_blocks(lists, body, (jnp.zeros((8, width), jnp.float32),) * 2)
    for half in range(2):
        norm[:, half * SIDE : (half + 1) * SIDE] = column(jnp.sum(sums[half], axis=0, keepdims=True))


def apply_all(stay, move, high, low, sizes):
    width = high.shape[0] // 2
    rows = sum(sizes)
    shapes = [(rows, width), (width, rows), (width, rows), (width, 2 * SIDE)] + [(size, width) for size in sizes]
    vmem = pl.BlockSpec(memory_space=pltpu.VMEM)
    sent, sent_turned, kept_turned, norm, *kept = pl.pallas_call(
        functools.partial(apply_all_kernel, (len(stay), len(move))),
        in_specs=[vmem] * (len(stay) + len(move) + 2),
        out_specs=[vmem] * len(shapes),
        out_shape=[jax.ShapeDtypeStruct(shape, jnp.float32) for shape in shapes],
        compiler_params=LARGE,
        cost_estimate=COST,
        name="apply_all",
    )(*stay, *move, high, low)
    return sent, sent_turned, kept, kept_turned, norm


def rebuild_kernel(counts, *refs):
    sent, refs = refs[: counts[0]], refs[counts[0] :]
    raw, refs = refs[: counts[1]], refs[counts[1] :]
    high, low, turned, came, total = refs
    total[...] = jnp.zeros_like(total)

    def body(views, carry):
        one, two, kept, out = views
        value = rotate(one, two, high, low)
        out[...] = value
        add_gram(total, kept[...], value)
        return carry

    over_blocks((straight(sent), straight(raw), transposed([turned]), straight([came])), body, 0)


def rebuild(sent, raw, high, low, turned):
    width, rows = turned.shape
    vmem = pl.BlockSpec(memory_space=pltpu.VMEM)
    args = (*sent, *raw, high, low, turned)
    return pl.pallas_call(
        functools.partial(rebuild_kernel, (len(sent), len(raw))),
        in_specs=[vmem] * len(args),
        out_specs=[vmem] * 2,
        out_shape=[
            jax.ShapeDtypeStruct((rows, width), jnp.float32),
            jax.ShapeDtypeStruct((width + 8, width), jnp.float32),
        ],
        compiler_params=LARGE,
        cost_estimate=COST,
        name="rebuild",
    )(*args)


def finish_kernel(counts, kept, aliased, flags, *refs):
    stay, refs = refs[: counts[0]], refs[counts[0] :]
    move, refs = refs[: counts[1]], refs[counts[1] :]
    high, low, *refs = refs
    out, token, held, done = refs[aliased:]
    width = held.shape[1]
    token[...] = jnp.zeros_like(token)
    half = pl.ds(width, width) if kept else pl.ds(0, width)
    columns = pl.ds(pl.multiple_of(output_half(flags, kept) * width, width), width)

    def write(index):
        rows = pl.ds(pl.multiple_of(index * BLOCK, BLOCK), BLOCK)
        return pltpu.make_async_copy(held.at[rows], out.at[rows, columns], done.at[index])

    def body(views, index):
        one, two, block = views
        block[...] = rotate(one, two, high.at[:, half], low.at[:, half])
        write(index).start()
        return index + 1

    over_blocks((straight(stay), straight(move), straight([held])), body, 0)
    for index in range(min(sum(ref.shape[0] for ref in pieces) for pieces in (stay, move)) // BLOCK):
        write(index).wait()


def put_kernel(start, flags, came, before, out, done):
    width = came.shape[1]
    columns = pl.ds(pl.multiple_of(output_half(flags, False) * width, width), width)
    copies = []
    for index in range(came.shape[0] // PUT):
        rows = pl.ds(index * PUT, PUT)
        copy = pltpu.make_async_copy(came.at[rows], out.at[pl.ds(start + index * PUT, PUT), columns], done.at[index])
        copy.start()
        copies.append(copy)
    for copy in copies:
        copy.wait()


def put(flags, came, before, start):
    vmem = pl.BlockSpec(memory_space=pltpu.VMEM)
    anywhere = pl.BlockSpec(memory_space=pl.ANY)
    return pl.pallas_call(
        functools.partial(put_kernel, start),
        in_specs=[vmem, vmem, anywhere],
        out_specs=anywhere,
        out_shape=jax.ShapeDtypeStruct(before.shape, jnp.float32),
        input_output_aliases={2: 0},
        scratch_shapes=[pltpu.SemaphoreType.DMA((came.shape[0] // PUT,))],
        compiler_params=PARAMS,
        cost_estimate=COST,
        name="put",
    )(flags, came, before)


def relay_kernel(message, *refs):
    refs[-1][...] = message[...]


def relay(message, after):
    vmem = pl.BlockSpec(memory_space=pltpu.VMEM)
    return pl.pallas_call(
        relay_kernel,
        in_specs=[vmem] + [pl.BlockSpec(memory_space=pl.ANY)] * len(after),
        out_specs=vmem,
        out_shape=jax.ShapeDtypeStruct(message.shape, jnp.float32),
        compiler_params=PARAMS,
        cost_estimate=COST,
        name="relay",
    )(message, *after)


def apply_one_kernel(skip, stay, move, high, low, sent):
    half = pl.ds(0, sent.shape[1])

    def body(views, carry):
        one, two, out = views
        out[...] = rotate(one, two, high.at[:, half], low.at[:, half])
        return carry

    over_blocks((straight([stay]), straight([move]), straight([sent])), body, 0, (0, skip * BLOCK, 0))


def apply_one(stay, move, high, low, skip):
    vmem = pl.BlockSpec(memory_space=pltpu.VMEM)
    return pl.pallas_call(
        functools.partial(apply_one_kernel, skip),
        in_specs=[vmem] * 4,
        out_specs=vmem,
        out_shape=jax.ShapeDtypeStruct(stay.shape, jnp.float32),
        compiler_params=PARAMS,
        cost_estimate=COST,
        name="apply_one",
    )(stay, move, high, low)


def finish(kept, flags, stay, move, high, low, before, shape, after=()):
    width = high.shape[0] // 2
    vmem = pl.BlockSpec(memory_space=pltpu.VMEM)
    anywhere = pl.BlockSpec(memory_space=pl.ANY)
    args = (flags, *stay, *move, high, low)
    blocks = shape[0] // BLOCK
    return pl.pallas_call(
        functools.partial(finish_kernel, (len(stay), len(move)), kept, len(before) + len(after)),
        in_specs=[vmem] * len(args) + [anywhere] * (len(before) + len(after)),
        out_specs=[anywhere, vmem],
        out_shape=[jax.ShapeDtypeStruct(shape, jnp.float32), jax.ShapeDtypeStruct((8, SIDE), jnp.float32)],
        input_output_aliases={len(args): 0} if before else {},
        scratch_shapes=[pltpu.VMEM((shape[0], width), jnp.float32), pltpu.SemaphoreType.DMA((blocks,))],
        compiler_params=LARGE,
        cost_estimate=COST,
        name="finish",
    )(*args, *before, *after)


def per_device(snapshots, plan):
    rows = snapshots.shape[0]
    rounds = plan.shape[0]
    size = rows // BLOCK // PIECES
    device = lax.axis_index("pair")
    count = lax.axis_size("pair")
    total = first_gram(snapshots)
    flags = make_flags(plan, jnp.stack((device, lax.axis_index("row"))), count, snapshots.shape[1] // 2)
    high, low, outgoing = rotation(0, 0, True, flags, total, (), None, (snapshots,), size * BLOCK)
    move = [shift(outgoing, "pair", -2)]
    norm = None
    held = [None] * PIECES
    for piece in [*range(1, PIECES), 0]:
        *held[piece], norm = apply_both(snapshots, piece * size, high, low, norm, size)
        if piece:
            move.append(shift(held[piece][0], "pair", -2))
    sent, sent_turned, stay, stay_turned = zip(*held)
    total = ()
    for one, two in zip(stay_turned, move):
        total = (gram((one,), (two,), total),)
    (total,) = total
    for step in range(1, rounds):
        last = step == rounds - 1
        direction = 2 if step % 2 else -2
        raw = [shift(value, "pair", direction) for value in (stay[:-1] if last else stay)]
        norm = norm + shift(norm, "row", 1)
        if last:
            break
        high, low = rotation(step, 0, True, flags, total, (norm,))
        sizes = [rows // 2, rows // 4, rows // 4] if step == rounds - 2 else [rows // 2] * 2
        new_sent, new_sent_turned, stay, stay_turned, own_norm = apply_all(stay, move, high, low, sizes)
        total = gram(sent_turned, raw, (), (own_norm,))
        high, low = rotation(rounds + step, SIDE, False, flags, total, (norm,))
        came, total = rebuild(sent, raw, high, low, stay_turned)
        move, norm = (came,), own_norm
        sent, sent_turned = (new_sent,), (new_sent_turned,)
    high, low, message = rotation(step, 0, True, flags, total, (norm,), note="write")
    message = shift(message, "pair", direction)
    outgoing = apply_one(stay[-1], came, high, low, (rows - stay[-1].shape[0]) // BLOCK)
    last_piece = shift(outgoing, "pair", direction)
    field, token = finish(1, flags, stay, move, high, low, (), snapshots.shape)
    message = relay(message, (outgoing, token, *raw))
    high, low = rotation(rounds + step, SIDE, False, flags, message, (norm,), note="read")
    field, _ = finish(0, flags, raw, sent, high, low, (field,), snapshots.shape)
    return put(flags, last_piece, field, rows - last_piece.shape[0])


def solution(mesh):
    in_specs = (P(("basin", "row"), "pair"), P())
    out_specs = P(("basin", "row"), "pair")
    return jax.shard_map(
        per_device, mesh=mesh, in_specs=in_specs, out_specs=out_specs, check_vma=False
    )
```
